32 devices in a mesh: rows: 4 (over x, core), dp: 8 (over z, y).
Axes of the slice: x: 2, y: 2, z: 4, core: 2. Of those that a mesh axis runs over, the one named last changes fastest.
Arguments:
- images: bfloat16 [8, 8, 512, 128], P('dp', 'rows'), may hold values from -54 to 54
- conv_weight: bfloat16 [3, 3, 128, 128], replicated, may hold values from -0.1875 to 0.1875
- conv_bias: float32 [128], replicated, may hold values from -3 to 3
- norm_gain: float32 [128], replicated, may hold values from 0.5 to 1.5
- norm_shift: float32 [128], replicated, may hold values from -3 to 3
- down_weight: bfloat16 [3, 3, 128, 256], replicated, may hold values from -0.1875 to 0.1875
- down_bias: float32 [256], replicated, may hold values from -3 to 3
- cotangent: bfloat16 [8, 4, 256, 256], P('dp', 'rows'), may hold values from -6 to 6
Outputs:
- block_out: bfloat16 [8, 4, 256, 256], P('dp', 'rows')
- grad_images: bfloat16 [8, 8, 512, 128], P('dp', 'rows')
- grad_conv_weight: float32 [3, 3, 128, 128], P(None, None, None, 'dp')
- grad_conv_bias: float32 [128], P('dp')
- grad_gain: float32 [128], P('dp')
- grad_shift: float32 [128], P('dp')
- grad_down_weight: float32 [3, 3, 128, 256], P(None, None, None, 'dp')
- grad_down_bias: float32 [256], P('dp')
The draws below stay inside these ranges and needn't reach their ends.
All inputs are finite; a program needn't handle non-finite values.
Results may differ from the reference program's by a relative error of at most 0.0048.
Values may be sent and summed in bfloat16 or wider, within the bound.
No kernel may reach another device: no remote copies, remote signals or barrier semaphores. Data moves between devices by JAX's collectives and lax.ppermute only.
A program may use at most 64 MiB of HBM per device.

```python
import math
import jax
import jax.numpy as jnp
from jax import lax

CH0 = 128
CH1 = 256
GROUPS = 32
COLS = 512
HEIGHT = 8
SAMPLES = 8


def draw_images(key, part):
    first, second, third = jax.random.split(jax.random.fold_in(key, 11), 3)
    position = jnp.arange(HEIGHT, dtype=jnp.float32) / max(HEIGHT - 1, 1)
    row_scale = jnp.power(3.0, position) * jnp.exp(jax.random.uniform(second, (HEIGHT,), jnp.float32, 0.0, math.log(2.0)))
    col_scale = jnp.exp(jax.random.uniform(third, (COLS,), jnp.float32, 0.0, math.log(5.0)))
    base = jnp.clip(jax.random.normal(first, (SAMPLES, HEIGHT, COLS, CH0), jnp.float32), -4.0, 4.0)
    values = 0.3 * base * row_scale[None, :, None, None] * col_scale[None, None, :, None]
    return values.astype(jnp.bfloat16)


def spiked(drawn, stream_key, source, target, shards_of, factor):
    owner, partner = [(jnp.arange(drawn.shape[dim]) // (drawn.shape[dim] // shards_of)).reshape([-1 if axis == dim else 1 for axis in range(drawn.ndim)]) for dim in (source, target)]
    chosen = jax.random.permutation(stream_key, shards_of)[partner]
    strong = (owner == chosen) | (owner == (partner + shards_of // 2) % shards_of)
    return jnp.where(strong, factor * drawn, drawn)


def steps_of(own_key, dims, shards, least, top_value):
    level, own = 1.0, jax.random.fold_in(own_key, 6)
    for dim, parts in shards:
        heights = jnp.exp(jax.random.uniform(jax.random.fold_in(own, dim), (parts,), jnp.float32, least / len(shards), top_value / len(shards)))
        level = level * jnp.repeat(heights, dims[dim] // parts).reshape([-1 if axis == dim else 1 for axis in range(len(dims))])
    return level


def bell_draw(stream_key, extent, scale, reach, shards=(), held_as=jnp.bfloat16):
    factor_of = steps_of(stream_key, extent, shards, -0.22, 0.18) if shards else 1.0
    result = jax.random.normal(stream_key, extent, jnp.float32) * scale * factor_of
    return jnp.minimum(jnp.maximum(result, -reach), reach).astype(held_as)


def noise_with(key, extent, scale, limit, cuts, heavy, held_as=jnp.bfloat16):
    array = scale * jax.random.normal(key, extent, jnp.float32)
    if cuts:
        array = array * steps_of(key, extent, cuts, -0.22, 0.18)
    return jnp.clip(spiked(array, jax.random.fold_in(key, 3), *heavy), -limit, limit).astype(held_as)


def setup_inputs(seed: int = 0) -> dict:
    keys = jax.random.split(jax.random.key(seed), 9)
    return {
        "images": draw_images(jax.random.fold_in(keys[8], 71), 0),
        "conv_weight": bell_draw(keys[1], (3, 3, CH0, CH0), (9 * CH0) ** -0.5, 0.1875),
        "conv_bias": bell_draw(keys[2], (CH0,), 0.5, 3.0, (), jnp.float32),
        "norm_gain": jnp.clip(1.0 + 0.1 * jax.random.normal(keys[3], (CH0,), jnp.float32), 0.5, 1.5),
        "norm_shift": bell_draw(keys[4], (CH0,), 0.5, 3.0, (), jnp.float32),
        "down_weight": bell_draw(keys[5], (3, 3, CH0, CH1), (9 * CH0) ** -0.5, 0.1875),
        "down_bias": bell_draw(keys[6], (CH1,), 0.5, 3.0, (), jnp.float32),
        "cotangent": noise_with(keys[7], (SAMPLES, HEIGHT // 2, COLS // 2, CH1), 1.0, 6.0, ((0, 8), (1, 4)), (0, 3, 8, 2.0)),
    }


def taps_conv(padded, weight, rows, cols):
    total = jnp.zeros((rows * cols, weight.shape[3]), jnp.float32)
    for kh in range(3):
        for kw in range(3):
            piece = padded[kh:kh + rows, kw:kw + cols].reshape(rows * cols, -1)
            total = total + jnp.dot(piece, weight[kh, kw], preferred_element_type=jnp.float32)
    return total.reshape(rows, cols, weight.shape[3])

def one_sample(image, cot, conv_weight, conv_bias, norm_gain, norm_shift, down_weight, down_bias):
    half_rows = HEIGHT // 2
    half_cols = COLS // 2
    width = CH0 // GROUPS
    count = float(HEIGHT * COLS * width)
    padded = jnp.pad(image, ((1, 1), (1, 1), (0, 0)))
    hidden = taps_conv(padded, conv_weight, HEIGHT, COLS) + conv_bias
    grouped = hidden.reshape(HEIGHT, COLS, GROUPS, width)
    mean = lax.optimization_barrier(jnp.sum(grouped, axis=(0, 1, 3))) / count
    centred = grouped - mean[:, None]
    var = lax.optimization_barrier(jnp.sum(centred * centred, axis=(0, 1, 3))) / count
    rstd = lax.rsqrt(var + 1e-05)
    normed = (centred * rstd[:, None]).reshape(HEIGHT, COLS, CH0)
    pre = normed * norm_gain + norm_shift
    sig = jax.nn.sigmoid(pre)
    mixed = (image.astype(jnp.float32) + pre * sig).astype(jnp.bfloat16)
    shifted = jnp.pad(mixed, ((1, 0), (1, 0), (0, 0)))
    cot_flat = cot.reshape(half_rows * half_cols, CH1)
    out = jnp.zeros((half_rows * half_cols, CH1), jnp.float32)
    grad_down = []
    grad_mixed_pad = jnp.zeros((HEIGHT + 1, COLS + 1, CH0), jnp.float32)
    for kh in range(3):
        line = []
        for kw in range(3):
            piece = shifted[kh:kh + 2 * half_rows:2, kw:kw + 2 * half_cols:2].reshape(half_rows * half_cols, CH0)
            out = out + jnp.dot(piece, down_weight[kh, kw], preferred_element_type=jnp.float32)
            line.append(jnp.dot(piece.T, cot_flat, preferred_element_type=jnp.float32))
            back = jnp.dot(cot_flat, down_weight[kh, kw].T, preferred_element_type=jnp.float32)
            grad_mixed_pad = grad_mixed_pad.at[kh:kh + 2 * half_rows:2, kw:kw + 2 * half_cols:2].add(back.reshape(half_rows, half_cols, CH0))
        grad_down.append(jnp.stack(line))
    block = (out + down_bias).astype(jnp.bfloat16).reshape(half_rows, half_cols, CH1)
    grad_down = jnp.stack(grad_down)
    grad_down_bias = lax.optimization_barrier(jnp.sum(cot.astype(jnp.float32), axis=(0, 1)))
    grad_mixed = grad_mixed_pad[1:, 1:]
    grad_pre = grad_mixed * sig * (1.0 + pre * (1.0 - sig))
    grad_gain = lax.optimization_barrier(jnp.sum(grad_pre * normed, axis=(0, 1)))
    grad_shift = lax.optimization_barrier(jnp.sum(grad_pre, axis=(0, 1)))
    scaled = (grad_pre * norm_gain).reshape(HEIGHT, COLS, GROUPS, width)
    normed_g = normed.reshape(HEIGHT, COLS, GROUPS, width)
    first = lax.optimization_barrier(jnp.sum(scaled, axis=(0, 1, 3))) / count
    second = lax.optimization_barrier(jnp.sum(scaled * normed_g, axis=(0, 1, 3))) / count
    grad_hidden = (rstd[:, None] * (scaled - first[:, None] - normed_g * second[:, None])).reshape(HEIGHT, COLS, CH0)
    grad_bias = lax.optimization_barrier(jnp.sum(grad_hidden, axis=(0, 1)))
    rounded = grad_hidden.astype(jnp.bfloat16)
    flat = rounded.reshape(HEIGHT * COLS, CH0)
    grad_conv = []
    for kh in range(3):
        line = []
        for kw in range(3):
            piece = padded[kh:kh + HEIGHT, kw:kw + COLS].reshape(HEIGHT * COLS, CH0)
            line.append(jnp.dot(piece.T, flat, preferred_element_type=jnp.float32))
        grad_conv.append(jnp.stack(line))
    grad_conv = jnp.stack(grad_conv)
    grad_pad = jnp.pad(rounded, ((1, 1), (1, 1), (0, 0)))
    back = jnp.zeros((HEIGHT * COLS, CH0), jnp.float32)
    for kh in range(3):
        for kw in range(3):
            piece = grad_pad[2 - kh:2 - kh + HEIGHT, 2 - kw:2 - kw + COLS].reshape(HEIGHT * COLS, CH0)
            back = back + jnp.dot(piece, conv_weight[kh, kw].T, preferred_element_type=jnp.float32)
    grad_image = (grad_mixed + back.reshape(HEIGHT, COLS, CH0)).astype(jnp.bfloat16)
    return (block, grad_image, (grad_conv, grad_bias, grad_gain, grad_shift, grad_down, grad_down_bias))

def reference(images, conv_weight, conv_bias, norm_gain, norm_shift, down_weight, down_bias, cotangent):
    start = (jnp.zeros((3, 3, CH0, CH0), jnp.float32), jnp.zeros((CH0,), jnp.float32), jnp.zeros((CH0,), jnp.float32), jnp.zeros((CH0,), jnp.float32), jnp.zeros((3, 3, CH0, CH1), jnp.float32), jnp.zeros((CH1,), jnp.float32))

    def step(carry, pair):
        block, grad_image, grads = one_sample(pair[0], pair[1], conv_weight, conv_bias, norm_gain, norm_shift, down_weight, down_bias)
        carry = tuple((c + g for c, g in zip(carry, grads)))
        return (carry, (block, grad_image))
    sums, (blocks, grad_images) = lax.scan(step, start, (images, cotangent))
    return (blocks, grad_images, sums[0], sums[1], sums[2], sums[3], sums[4], sums[5])
```

```python
import functools

import jax
import jax.numpy as jnp
from jax import lax
from jax.experimental import pallas as pl
from jax.experimental.pallas import tpu as pltpu
from jax.sharding import PartitionSpec as P

GROUPS = 32
EPS = 1e-05
F32 = jnp.float32
BF16 = jnp.bfloat16
MIB = 1 << 20


def dot(a, b):
    return jnp.dot(a, b, preferred_element_type=F32)


def dot_nt(a, b):
    return lax.dot_general(a, b, (((1,), (1,)), ((), ())), preferred_element_type=F32)


def dot_tn(a, b):
    return lax.dot_general(a, b, (((0,), (0,)), ((), ())), preferred_element_type=F32)


def lanes(*parts):
    return jnp.concatenate(parts, axis=1)


def stack(*parts):
    return jnp.concatenate(parts, axis=0)


def later(x):
    row = lax.broadcasted_iota(jnp.int32, x.shape, 0)
    return jnp.where(row == 0, 0.0, pltpu.roll(x, 1, 0))


def sooner(x):
    row = lax.broadcasted_iota(jnp.int32, x.shape, 0)
    return jnp.where(row == x.shape[0] - 1, 0.0, pltpu.roll(x, x.shape[0] - 1, 0))


def grouped(row, width):
    n = row.shape[1]
    a = lax.broadcasted_iota(jnp.int32, (n, n), 0) // width
    b = lax.broadcasted_iota(jnp.int32, (n, n), 1) // width
    same = jnp.where(a == b, 1.0, 0.0).astype(F32)
    wide = jnp.broadcast_to(row, (8, n))
    return jnp.dot(wide, same, precision=lax.Precision.HIGHEST, preferred_element_type=F32)[0:1]


def split(scr, row):
    half = row.shape[0] // 2
    scr[...] = row.astype(F32)
    return scr[pl.ds(0, half, stride=2), :], scr[pl.ds(1, half, stride=2), :]


def conv_weights(w):
    tap = [stack(w[0, k], w[1, k], w[2, k]) for k in range(3)]
    return stack(lanes(tap[1], tap[0]), lanes(tap[2], tap[1])), tap[0], tap[2]


def conv_rows(even, odd, weights, bias):
    both, first, last = weights
    base = dot(lanes(even, odd), both)
    chans = first.shape[1]
    from_odd = dot(odd, first)
    from_even = dot(even, last)
    return base[:, :chans] + bias, base[:, chans:] + bias, from_odd, from_even


def hidden_kernel(width, up, img, dn, w, bias, x_out, hid_out, stat_out, scr):
    half = x_out.shape[2]
    rows = (up[1], img[0], img[1], dn[0])
    for p in range(4):
        even, odd = split(scr, rows[p])
        x_out[p, 0] = even.astype(BF16)
        x_out[p, 1] = odd.astype(BF16)
    weights = conv_weights(w)
    even = stack(*[lanes(x_out[p, 0], x_out[p + 1, 0], x_out[p + 2, 0]) for p in range(2)])
    odd = stack(*[lanes(x_out[p, 1], x_out[p + 1, 1], x_out[p + 2, 1]) for p in range(2)])
    base_e, base_o, from_odd, from_even = conv_rows(even, odd, weights, bias[...])
    total = 0.0
    for p in range(2):
        sl = slice(p * half, (p + 1) * half)
        he = base_e[sl] + later(from_odd[sl])
        ho = base_o[sl] + sooner(from_even[sl])
        hid_out[p, 0] = he
        hid_out[p, 1] = ho
        total = total + jnp.sum(he + ho, axis=0, keepdims=True)
    mean = grouped(total, width) / float(4 * half * width)
    spread = 0.0
    for p in range(2):
        for c in range(2):
            d = hid_out[p, c] - mean
            spread = spread + jnp.sum(d * d, axis=0, keepdims=True)
    stat_out[...] = jnp.zeros(stat_out.shape, F32)
    stat_out[0:1] = mean
    stat_out[1:2] = grouped(spread, width)


def edge_kernel(up, x, dn, w, bias, cot_up, cot, cot_dn, dw, hid_out, gm_out, cb_out, scr):
    half = x.shape[2]
    top = [v.astype(BF16) for v in split(scr, up[0])]
    low = [v.astype(BF16) for v in split(scr, dn[1])]
    weights = conv_weights(w)
    even = stack(lanes(top[0], x[0, 0], x[1, 0]), lanes(x[2, 0], x[3, 0], low[0]))
    odd = stack(lanes(top[1], x[0, 1], x[1, 1]), lanes(x[2, 1], x[3, 1], low[1]))
    base_e, base_o, from_odd, from_even = conv_rows(even, odd, weights, bias[...])
    for p in range(2):
        sl = slice(p * half, (p + 1) * half)
        hid_out[p, 0] = base_e[sl] + later(from_odd[sl])
        hid_out[p, 1] = base_o[sl] + sooner(from_even[sl])
    chans = x.shape[3]

    def taps(c, kh):
        flat = dw[kh].reshape(3 * chans, dw.shape[3])
        got = dot_nt(c, flat)
        return got[:, chans : 2 * chans], got[:, 2 * chans :], got[:, :chans]

    def put(p, even_part, odd_part, odd_shift):
        gm_out[p, 0] = even_part
        gm_out[p, 1] = odd_part + sooner(odd_shift)

    mine = [taps(cot[...], kh) for kh in range(3)]
    above = taps(cot_up[...], 2)
    below0 = taps(cot_dn[...], 0)
    below1 = taps(cot_dn[...], 1)
    put(0, *[a + b for a, b in zip(above, mine[0])])
    put(1, *mine[1])
    put(2, *[a + b for a, b in zip(mine[2], below0)])
    put(3, *below1)
    cb_out[...] = jnp.broadcast_to(jnp.sum(cot[...].astype(F32), axis=0, keepdims=True), cb_out.shape)


def norm_kernel(width, count, ranks, *refs):
    stats = refs[:ranks]
    x, hid, gm, gain, shift, par_out, mix_out, gp_out, sum_out = refs[ranks:]
    half = x.shape[2]
    local = float(4 * half * width)
    mean = sum(s[0:1] for s in stats) / float(len(stats))
    spread = 0.0
    for s in stats:
        d = s[0:1] - mean
        spread = spread + (s[1:2] + local * (d * d))
    rstd = lax.rsqrt(spread / count + EPS)
    par_out[...] = jnp.zeros(par_out.shape, F32)
    par_out[0:1] = mean
    par_out[1:2] = rstd
    first = 0.0
    second = 0.0
    for p in range(2):
        mixed = []
        for c in range(2):
            normed = (hid[p, c] - mean) * rstd
            pre = normed * gain[...] + shift[...]
            sig = jax.nn.sigmoid(pre)
            mixed.append(x[p + 1, c].astype(F32) + pre * sig)
            gp = gm[p + 1, c] * (sig * (1.0 + pre * (1.0 - sig)))
            gp_out[p, c] = gp
            first = first + jnp.sum(gp * normed, axis=0, keepdims=True)
            second = second + jnp.sum(gp, axis=0, keepdims=True)
        mix_out[p] = lanes(later(mixed[1]).astype(BF16), mixed[0].astype(BF16), mixed[1].astype(BF16))
    sum_out[...] = jnp.zeros(sum_out.shape, F32)
    sum_out[0:1] = first
    sum_out[1:2] = second


def down_kernel(packed, me_ref, par, x, hid, gain, shift, mix, cot, top_out, *rest):
    mean, rstd = par[0:1], par[1:2]
    chans = x.shape[3]
    inside = jnp.where(me_ref[0] > 0, 1.0, 0.0)
    mixed = []
    for c in range(2):
        pre = (hid[0, c] - mean) * rstd * gain[...] + shift[...]
        mixed.append((x[0, c].astype(F32) + pre * jax.nn.sigmoid(pre)) * inside)
    top = lanes(later(mixed[1]).astype(BF16), mixed[0].astype(BF16), mixed[1].astype(BF16))
    top_out[...] = top
    grad = dot_tn(cot[...], lanes(top, mix[0], mix[1]))
    if not packed:
        rest[0][...] = grad
        return
    last_out, e0, e1, e2, e3, dscr = rest
    outs_chunk = e0.shape[2]
    for q in range(4):
        for t in range(2):
            tap = 2 * q + t
            dscr[q, t] = grad[:, tap * chans : (tap + 1) * chans].reshape(-1, outs_chunk, chans)
    last_out[...] = grad[:, 8 * chans :]
    me = me_ref[0]
    e0[...] = dscr[me]
    for k, ref in ((1, e1), (2, e2), (3, e3)):
        ref[...] = dscr[me ^ k].astype(BF16)


def hi_lo(full):
    hi = full.astype(BF16).astype(F32)
    return jnp.concatenate([hi, full - hi], axis=-2)


def back_kernel(width, count, ranks, packed, me_ref, *refs):
    sum_refs = refs[:ranks]
    par, x, hid, gp, gain, *refs = refs[ranks:]
    if packed:
        dlast, cbias, par_out, g_out, l0, l1, l2, l3, lscr = refs
    else:
        par_out, g_out, grad_out, small_out = refs
    half = x.shape[2]
    chans = x.shape[3]
    me = me_ref[0]
    mean, rstd = par[0:1], par[1:2]
    sums = sum(s[...] for s in sum_refs)
    m2 = grouped(sums[0:1] * gain[...], width) / count
    m1 = grouped(sums[1:2] * gain[...], width) / count
    coef = (rstd * gain[...], -(rstd * rstd) * m2, -rstd * m1)
    par_out[...] = jnp.zeros(par_out.shape, F32)
    par_out[0:1] = mean
    for i in range(3):
        par_out[1 + i : 2 + i] = coef[i]
    bias = 0.0
    left, right = [], []
    for p in range(2):
        ge = coef[0] * gp[p, 0] + coef[1] * (hid[p, 0] - mean) + coef[2]
        go = coef[0] * gp[p, 1] + coef[1] * (hid[p, 1] - mean) + coef[2]
        bias = bias + jnp.sum(ge + go, axis=0, keepdims=True)
        ge_b, go_b = ge.astype(BF16), go.astype(BF16)
        g_out[p, 0] = ge_b
        g_out[p, 1] = go_b
        left += [lanes(go_b, ge_b, later(go).astype(BF16)), lanes(sooner(ge).astype(BF16), go_b, ge_b)]
        right += [lanes(x[p, c], x[p + 1, c], x[p + 2, c]) for c in range(2)]
    grad = dot_tn(stack(*left), stack(*right))
    full = stack(bias, sum_refs[0][0:2], jnp.zeros((5, chans), F32))
    if not packed:
        grad_out[...] = grad
        small_out[...] = full
        return
    owners, _, _ = l0.shape
    chunk = chans // owners
    for kh in range(3):
        for kw in range(3):
            piece = grad[kw * chans : (kw + 1) * chans, kh * chans : (kh + 1) * chans]
            lscr[kh, :, kw * chunk : (kw + 1) * chunk, :] = piece.reshape(-1, chunk, chans)
    lscr[3, :, 0 : 2 * chunk, :] = dlast[...].reshape(owners, 2 * chunk, chans)
    wide = [cbias[0:1, i * chans : (i + 1) * chans] for i in range(cbias.shape[1] // chans)]
    row_id = lax.broadcasted_iota(jnp.int32, full.shape, 0)
    for d in range(owners):
        at = d * chunk
        mine = full if at == 0 else pltpu.roll(full, chans - at, 1)
        at = d * 2 * chunk
        row = jnp.broadcast_to(wide[at // chans], full.shape)
        if at % chans:
            row = pltpu.roll(row, chans - at % chans, 1)
        lscr[3, d, 2 * chunk :, :] = hi_lo(jnp.where(row_id == 3, row, mine))
    l0[...] = lscr[me]
    for k, ref in ((1, l1), (2, l2), (3, l3)):
        ref[...] = lscr[me ^ k].astype(BF16)


def image_kernel(last, me_ref, par, hid, gm, gain, shift, par2, g, mix_top, mix, w, dw, dbias, block_out, gi_out, scr):
    half = g.shape[2]
    chans = g.shape[3]
    flat = [dw[:, k].reshape(3 * chans, dw.shape[3]) for k in range(3)]
    odd_before = lanes(mix_top[:, :chans], mix[0, :, :chans], mix[1, :, :chans])
    even = lanes(mix_top[:, chans : 2 * chans], mix[0, :, chans : 2 * chans], mix[1, :, chans : 2 * chans])
    odd = lanes(mix_top[:, 2 * chans :], mix[0, :, 2 * chans :], mix[1, :, 2 * chans :])
    block = dot(lanes(odd_before, even, odd), stack(*flat)) + dbias[...]
    block_out[...] = block.astype(BF16)

    mean, rstd = par[0:1], par[1:2]
    me = me_ref[0]
    edge = []
    for i, p, there in ((0, 0, me > 0), (1, 3, me < last)):
        keep = jnp.where(there, 1.0, 0.0)
        pair = []
        for c in range(2):
            centred = hid[i, c] - mean
            pre = centred * rstd * gain[...] + shift[...]
            sig = jax.nn.sigmoid(pre)
            gp = gm[p, c] * (sig * (1.0 + pre * (1.0 - sig)))
            pair.append(((par2[1:2] * gp + par2[2:3] * centred + par2[3:4]) * keep).astype(BF16))
        edge.append(pair)
    rows = [edge[0], [g[0, 0], g[0, 1]], [g[1, 0], g[1, 1]], edge[1]]
    tap = [lanes(w[0, k], w[1, k], w[2, k]) for k in range(3)]
    both = stack(lanes(tap[1], tap[0]), lanes(tap[2], tap[1]))
    ge = stack(*[lanes(rows[p + 2][0], rows[p + 1][0], rows[p][0]) for p in range(2)])
    go = stack(*[lanes(rows[p + 2][1], rows[p + 1][1], rows[p][1]) for p in range(2)])
    base = dot_nt(lanes(ge, go), both)
    from_odd = dot_nt(go, tap[2])
    from_even = dot_nt(ge, tap[0])
    for p in range(2):
        sl = slice(p * half, (p + 1) * half)
        scr[pl.ds(0, half, stride=2), :] = base[sl, :chans] + later(from_odd[sl]) + gm[p + 1, 0]
        scr[pl.ds(1, half, stride=2), :] = base[sl, chans:] + sooner(from_even[sl]) + gm[p + 1, 1]
        gi_out[p] = scr[...].astype(BF16)


def resplit(total, on):
    whole = total[..., 0:8, :] + total[..., 8:16, :]
    return jnp.where(on, hi_lo(whole), total)


def rows_kernel(me_ref, e0, e1, e2, e3, l0, l1, l2, l3, out):
    me = me_ref[0]
    early = e0[...] + e1[...].astype(F32) + e2[...].astype(F32) + e3[...].astype(F32)
    late = l0[...] + l1[...].astype(F32) + l2[...].astype(F32) + l3[...].astype(F32)
    n = early.shape[2]
    m = late.shape[1]
    for t in range(2):
        out[:, t * n : (t + 1) * n, :] = early[t].astype(BF16)
    out[:, 2 * n : 2 * n + m - 16, :] = late[:, : m - 16].astype(BF16)
    out[:, 2 * n + m - 16 :, :] = resplit(late[:, m - 16 :], me == 3).astype(BF16)


def dp_kernel(me_ref, got, out):
    total = jnp.sum(got[...].astype(F32), axis=0)
    n = total.shape[0]
    out[: n - 16] = total[: n - 16].astype(BF16)
    out[n - 16 :] = resplit(total[n - 16 :], me_ref[0] == 3).astype(BF16)


def last_kernel(chunk, me_ref, q0, q1, q2, q3, down, conv, cb, ga, sh, db, scr):
    me = me_ref[0]
    for k, ref in enumerate((q0, q1, q2, q3)):
        scr[me ^ k] = ref[...].astype(F32)
    wide = 2 * chunk
    for q in range(4):
        for t in range(2):
            down[2 * q + t] = scr[q, t * wide : (t + 1) * wide, :]
    for kh in range(3):
        for kw in range(3):
            at = 2 * wide + kw * chunk
            conv[3 * kh + kw] = scr[kh, at : at + chunk, :]
    down[8] = scr[3, 2 * wide : 3 * wide, :]
    rows = scr[3, 3 * wide : 3 * wide + 8, :] + scr[3, 3 * wide + 8 :, :]
    cb[...] = rows[0:1, :chunk]
    ga[...] = rows[1:2, :chunk]
    sh[...] = rows[2:3, :chunk]
    db[...] = rows[3:4, :wide]


def beside(x, up):
    n = lax.axis_size("rows")
    pairs = [(i, i + 1) for i in range(n - 1)]
    return lax.ppermute(x, "rows", pairs if up else [(b, a) for a, b in pairs])


def swap(x, axis, k):
    return lax.ppermute(x, axis, [(i, i ^ k) for i in range(lax.axis_size(axis))])


def shards(images, conv_weight, conv_bias, norm_gain, norm_shift, down_weight, down_bias, cotangent):
    img, cot = images[0], cotangent[0, 0]
    rows, cols, chans = img.shape
    half, outs = cot.shape
    ranks, owners = lax.axis_size("rows"), lax.axis_size("dp")
    width = chans // GROUPS
    count = float(rows * cols * width * ranks)
    chunk, wide = chans // owners, outs // owners
    packed = ranks == 4 and chunk == 16 and wide == 32
    me = lax.axis_index("rows").astype(jnp.int32).reshape(1)
    smem = pl.BlockSpec(memory_space=pltpu.SMEM)
    vmem = pl.BlockSpec(memory_space=pltpu.VMEM)

    def run(kernel, args, outs, scratch=()):
        return pl.pallas_call(
            kernel,
            in_specs=[smem if a is me else vmem for a in args],
            out_shape=[jax.ShapeDtypeStruct(s, d) for s, d in outs],
            out_specs=[vmem] * len(outs),
            scratch_shapes=list(scratch),
            compiler_params=pltpu.CompilerParams(vmem_limit_bytes=24 * MIB),
            cost_estimate=pl.CostEstimate(flops=1 << 27, bytes_accessed=2 << 20, transcendentals=0),
        )(*args)

    def with_swaps(mine, others):
        return [mine] + [swap(other, "rows", k + 1) for k, other in enumerate(others)]

    bias = conv_bias.reshape(1, chans)
    gain = norm_gain.reshape(1, chans)
    shift = norm_shift.reshape(1, chans)
    dbias = down_bias.reshape(1, outs)
    up, dn = beside(img, True), beside(img, False)
    cot_up, cot_dn = beside(cot, True), beside(cot, False)
    row_scr = pltpu.VMEM((cols, chans), F32)
    block_of = (2, 2, half, chans)
    tile = ((8, chans), F32)
    x, hid, stat = run(
        functools.partial(hidden_kernel, width),
        (up, img, dn, conv_weight, bias),
        [((4, 2, half, chans), BF16), (block_of, F32), tile],
        [row_scr],
    )
    stats = with_swaps(stat, [stat] * (ranks - 1))
    hid_edge, gm, cbias = run(
        edge_kernel,
        (up, x, dn, conv_weight, bias, cot_up, cot, cot_dn, down_weight),
        [(block_of, F32), ((4, 2, half, chans), F32), ((8, outs), F32)],
        [row_scr],
    )
    par, mix, gp, sums = run(
        functools.partial(norm_kernel, width, count, ranks),
        (*stats, x, hid, gm, gain, shift),
        [tile, ((2, half, 3 * chans), BF16), (block_of, F32), tile],
    )
    all_sums = with_swaps(sums, [sums] * (ranks - 1))
    early_shape = (2, owners, wide, chans)
    late_shape = (owners, 3 * chunk, chans)
    deep = 2 * wide + 3 * chunk

    def by_rank(shape):
        return [(shape, F32)] + [(shape, BF16)] * (ranks - 1)

    mix_top, *down_grad = run(
        functools.partial(down_kernel, packed),
        (me, par, x, hid_edge, gain, shift, mix, cot),
        [((half, 3 * chans), BF16)]
        + ([((outs, chans), F32)] + by_rank(early_shape) if packed else [((outs, 9 * chans), F32)]),
        [pltpu.VMEM((4,) + early_shape, F32)] if packed else [],
    )
    if packed:
        dlast, *early = down_grad
        early = with_swaps(early[0], early[1:])
    par2, g, *conv_grad = run(
        functools.partial(back_kernel, width, count, ranks, packed),
        (me, *all_sums, par, x, hid, gp, gain) + ((dlast, cbias) if packed else ()),
        [tile, (block_of, BF16)] + (by_rank(late_shape) if packed else [((3 * chans, 3 * chans), F32), tile]),
        [pltpu.VMEM((4,) + late_shape, F32)] if packed else [],
    )
    if packed:
        late = with_swaps(conv_grad[0], conv_grad[1:])
    block, gi = run(
        functools.partial(image_kernel, ranks - 1),
        (me, par, hid_edge, gm, gain, shift, par2, g, mix_top, mix, conv_weight, down_weight, dbias),
        [((half, outs), BF16), ((rows, cols, chans), BF16)],
        [row_scr],
    )
    if packed:
        (mine,) = run(rows_kernel, (me, *early, *late), [((owners, deep, chans), BF16)])
        got = lax.all_to_all(mine, "dp", 0, 0)
        (part,) = run(dp_kernel, (me, got), [((deep, chans), BF16)])
        down, conv, cb, ga, sh, db = run(
            functools.partial(last_kernel, chunk),
            (me, *with_swaps(part, [part] * (ranks - 1))),
            [((9, wide, chans), F32), ((9, chunk, chans), F32)] + [((1, chunk), F32)] * 3 + [((1, wide), F32)],
            [pltpu.VMEM((4, deep, chans), F32)],
        )
    else:
        totals = lax.psum((down_grad[0], conv_grad[0], conv_grad[1], cbias[:1]), ("rows", "dp"))
        owner = lax.axis_index("dp")
        down = totals[0].reshape(outs, 9, chans).transpose(1, 0, 2)
        down = lax.dynamic_slice_in_dim(down, owner * wide, wide, 1)
        conv = totals[1].reshape(3, chans, 3, chans).transpose(2, 0, 1, 3).reshape(9, chans, chans)
        conv = lax.dynamic_slice_in_dim(conv, owner * chunk, chunk, 1)
        cb, ga, sh = lax.dynamic_slice_in_dim(totals[2], owner * chunk, chunk, 1)[:3]
        db = lax.dynamic_slice_in_dim(totals[3], owner * wide, wide, 1)
    return (
        block[None, None],
        gi[None],
        conv.reshape(3, 3, chunk, chans).transpose(0, 1, 3, 2),
        cb.reshape(-1),
        ga.reshape(-1),
        sh.reshape(-1),
        down.reshape(3, 3, wide, chans).transpose(0, 1, 3, 2),
        db.reshape(-1),
    )


def solution(mesh):
    spec = P("dp", "rows", None, None)
    in_specs = (spec, P(), P(), P(), P(), P(), P(), spec)
    last = P(None, None, None, "dp")
    out_specs = (spec, spec, last, P("dp"), P("dp"), P("dp"), last, P("dp"))
    return jax.shard_map(shards, mesh=mesh, in_specs=in_specs, out_specs=out_specs, check_vma=False)
```

```python
import functools

import jax
import jax.numpy as jnp
from jax import lax
from jax.experimental import pallas as pl
from jax.experimental.pallas import tpu as pltpu
from jax.sharding import PartitionSpec as P

GROUPS = 32
EPS = 1e-05
F32 = jnp.float32
BF16 = jnp.bfloat16
MIB = 1 << 20


def dot(a, b):
    return jnp.dot(a, b, preferred_element_type=F32)


def dot_nt(a, b):
    return lax.dot_general(a, b, (((1,), (1,)), ((), ())), preferred_element_type=F32)


def dot_tn(a, b):
    return lax.dot_general(a, b, (((0,), (0,)), ((), ())), preferred_element_type=F32)


def lanes(*parts):
    return jnp.concatenate(parts, axis=1)


def stack(*parts):
    return jnp.concatenate(parts, axis=0)


def later(x):
    row = lax.broadcasted_iota(jnp.int32, x.shape, 0)
    return jnp.where(row == 0, 0.0, pltpu.roll(x, 1, 0))


def sooner(x):
    row = lax.broadcasted_iota(jnp.int32, x.shape, 0)
    return jnp.where(row == x.shape[0] - 1, 0.0, pltpu.roll(x, x.shape[0] - 1, 0))


def grouped(row, width):
    n = row.shape[1]
    a = lax.broadcasted_iota(jnp.int32, (n, n), 0) // width
    b = lax.broadcasted_iota(jnp.int32, (n, n), 1) // width
    same = jnp.where(a == b, 1.0, 0.0).astype(F32)
    wide = jnp.broadcast_to(row, (8, n))
    return jnp.dot(wide, same, precision=lax.Precision.HIGHEST, preferred_element_type=F32)[0:1]


def split(scr, row):
    half = row.shape[0] // 2
    scr[...] = row.astype(F32)
    return scr[pl.ds(0, half, stride=2), :], scr[pl.ds(1, half, stride=2), :]


def conv_weights(w):
    tap = [stack(w[0, k], w[1, k], w[2, k]) for k in range(3)]
    return stack(lanes(tap[1], tap[0]), lanes(tap[2], tap[1])), tap[0], tap[2]


def conv_rows(even, odd, weights, bias):
    both, first, last = weights
    base = dot(lanes(even, odd), both)
    chans = first.shape[1]
    from_odd = dot(odd, first)
    from_even = dot(even, last)
    return base[:, :chans] + bias, base[:, chans:] + bias, from_odd, from_even


def first_kernel(me_ref, out):
    out[...] = jnp.zeros(out.shape, F32)


def prep_kernel(ahead, img, w, dw, cot, bias, gain, shift, dbias, *refs):
    outs, (x_out, gm_out, cb_out, img_v, scr, sems) = refs[:7], refs[7:]
    pairs = list(zip((img, w, dw, cot, bias, gain, shift, dbias), (img_v,) + outs))
    copies = [pltpu.make_async_copy(src, dst, sems.at[i]) for i, (src, dst) in enumerate(pairs)]
    for copy in copies:
        copy.start()
    copies[0].wait()
    for p in range(2):
        even, odd = split(scr, img_v[p])
        x_out[p, 0] = even.astype(BF16)
        x_out[p, 1] = odd.astype(BF16)
    for copy in copies[1:]:
        copy.wait()
    dw_v, cot_v = outs[1], outs[2]
    for p, kh in enumerate(range(3)):
        even, odd, late = back_taps(cot_v[...], dw_v, kh)
        gm_out[p, 0] = even
        gm_out[p, 1] = odd + sooner(late)
    cb_out[...] = jnp.broadcast_to(jnp.sum(cot_v[...].astype(F32), axis=0, keepdims=True), cb_out.shape)


def back_taps(c, dw, kh):
    chans, outs = dw.shape[2:]
    got = dot_nt(c, dw[kh].reshape(3 * chans, outs))
    return got[:, chans : 2 * chans], got[:, 2 * chans :], got[:, :chans]


def either(flag, a, b):
    return jnp.where(flag, a.astype(F32), b.astype(F32))


def hidden_kernel(width, me_ref, core, chip, own, w, bias, x_out, hid_out, stat_out, scr):
    half = x_out.shape[2]
    odd_rank = (me_ref[0] & 1) == 1
    for p, row in ((0, either(odd_rank, core[1], chip[1])), (3, either(odd_rank, chip[0], core[0]))):
        even, odd = split(scr, row)
        x_out[p, 0] = even.astype(BF16)
        x_out[p, 1] = odd.astype(BF16)
    for p in range(2):
        x_out[p + 1] = own[p]
    weights = conv_weights(w)
    even = stack(*[lanes(x_out[p, 0], x_out[p + 1, 0], x_out[p + 2, 0]) for p in range(2)])
    odd = stack(*[lanes(x_out[p, 1], x_out[p + 1, 1], x_out[p + 2, 1]) for p in range(2)])
    base_e, base_o, from_odd, from_even = conv_rows(even, odd, weights, bias[...])
    total = 0.0
    for p in range(2):
        sl = slice(p * half, (p + 1) * half)
        he = base_e[sl] + later(from_odd[sl])
        ho = base_o[sl] + sooner(from_even[sl])
        hid_out[p, 0] = he
        hid_out[p, 1] = ho
        total = total + jnp.sum(he + ho, axis=0, keepdims=True)
    mean = grouped(total, width) / float(4 * half * width)
    spread = 0.0
    for p in range(2):
        for c in range(2):
            d = hid_out[p, c] - mean
            spread = spread + jnp.sum(d * d, axis=0, keepdims=True)
    stat_out[...] = jnp.zeros(stat_out.shape, F32)
    stat_out[0:1] = mean
    stat_out[1:2] = grouped(spread, width)


def edge_kernel(me_ref, core, chip, x, w, bias, cot_core, cot_chip, dw, own_gm, hid_out, gm_out, scr):
    half = x.shape[2]
    odd_rank = (me_ref[0] & 1) == 1
    top = [v.astype(BF16) for v in split(scr, either(odd_rank, core[0], chip[0]))]
    low = [v.astype(BF16) for v in split(scr, either(odd_rank, chip[1], core[1]))]
    weights = conv_weights(w)
    even = stack(lanes(top[0], x[0, 0], x[1, 0]), lanes(x[2, 0], x[3, 0], low[0]))
    odd = stack(lanes(top[1], x[0, 1], x[1, 1]), lanes(x[2, 1], x[3, 1], low[1]))
    base_e, base_o, from_odd, from_even = conv_rows(even, odd, weights, bias[...])
    for p in range(2):
        sl = slice(p * half, (p + 1) * half)
        hid_out[p, 0] = base_e[sl] + later(from_odd[sl])
        hid_out[p, 1] = base_o[sl] + sooner(from_even[sl])
    above = either(odd_rank, cot_core[...], cot_chip[...]).astype(BF16)
    below = either(odd_rank, cot_chip[...], cot_core[...]).astype(BF16)
    zero = jnp.zeros((half, x.shape[3]), F32)
    for p, c, kh in ((0, above, 2), (1, None, 0), (2, below, 0), (3, below, 1)):
        even, odd, late = back_taps(c, dw, kh) if c is not None else (zero, zero, zero)
        own = own_gm[p] if p < 3 else (zero, zero)
        gm_out[p, 0] = own[0] + even
        gm_out[p, 1] = own[1] + (odd + sooner(late) if c is not None else odd)


def norm_kernel(width, count, ranks, *refs):
    stats = refs[:ranks]
    x, hid, gm, gain, shift, par_out, mix_out, gp_out, sum_out = refs[ranks:]
    half = x.shape[2]
    local = float(4 * half * width)
    mean = sum(s[0:1] for s in stats) / float(len(stats))
    spread = 0.0
    for s in stats:
        d = s[0:1] - mean
        spread = spread + (s[1:2] + local * (d * d))
    rstd = lax.rsqrt(spread / count + EPS)
    par_out[...] = jnp.zeros(par_out.shape, F32)
    par_out[0:1] = mean
    par_out[1:2] = rstd
    first = 0.0
    second = 0.0
    for p in range(2):
        mixed = []
        for c in range(2):
            normed = (hid[p, c] - mean) * rstd
            pre = normed * gain[...] + shift[...]
            sig = jax.nn.sigmoid(pre)
            mixed.append(x[p + 1, c].astype(F32) + pre * sig)
            gp = gm[p + 1, c] * (sig * (1.0 + pre * (1.0 - sig)))
            gp_out[p, c] = gp
            first = first + jnp.sum(gp * normed, axis=0, keepdims=True)
            second = second + jnp.sum(gp, axis=0, keepdims=True)
        mix_out[p] = lanes(later(mixed[1]).astype(BF16), mixed[0].astype(BF16), mixed[1].astype(BF16))
    sum_out[...] = jnp.zeros(sum_out.shape, F32)
    sum_out[0:1] = first
    sum_out[1:2] = second


def down_kernel(packed, me_ref, par, x, hid, gain, shift, mix, cot, top_out, *rest):
    mean, rstd = par[0:1], par[1:2]
    chans = x.shape[3]
    inside = jnp.where(me_ref[0] > 0, 1.0, 0.0)
    mixed = []
    for c in range(2):
        pre = (hid[0, c] - mean) * rstd * gain[...] + shift[...]
        mixed.append((x[0, c].astype(F32) + pre * jax.nn.sigmoid(pre)) * inside)
    top = lanes(later(mixed[1]).astype(BF16), mixed[0].astype(BF16), mixed[1].astype(BF16))
    top_out[...] = top
    grad = dot_tn(cot[...], lanes(top, mix[0], mix[1]))
    if not packed:
        rest[0][...] = grad
        return
    last_out, keep_out, send_out, dscr = rest
    outs_chunk = keep_out.shape[3]
    for q in range(4):
        for t in range(2):
            tap = 2 * q + t
            dscr[q, t] = grad[:, tap * chans : (tap + 1) * chans].reshape(-1, outs_chunk, chans)
    last_out[...] = grad[:, 8 * chans :]
    halve(me_ref[0] & 1, dscr, keep_out, send_out)


def halve(core, quarters, keep_out, send_out):
    for i in range(2):
        keep_out[i] = quarters[2 * i + core]
        send_out[i] = quarters[2 * i + 1 - core].astype(BF16)


def hi_lo(full):
    hi = full.astype(BF16).astype(F32)
    return jnp.concatenate([hi, full - hi], axis=-2)


def back_kernel(width, count, ranks, packed, me_ref, *refs):
    sum_refs = refs[:ranks]
    par, x, hid, gp, gain, *refs = refs[ranks:]
    if packed:
        dlast, cbias, keep, got, par_out, g_out, early_own, early_send, keep_out, send_out, lscr = refs
    else:
        par_out, g_out, grad_out, small_out = refs
    half = x.shape[2]
    chans = x.shape[3]
    me = me_ref[0]
    mean, rstd = par[0:1], par[1:2]
    sums = sum(s[...] for s in sum_refs)
    m2 = grouped(sums[0:1] * gain[...], width) / count
    m1 = grouped(sums[1:2] * gain[...], width) / count
    coef = (rstd * gain[...], -(rstd * rstd) * m2, -rstd * m1)
    par_out[...] = jnp.zeros(par_out.shape, F32)
    par_out[0:1] = mean
    for i in range(3):
        par_out[1 + i : 2 + i] = coef[i]
    bias = 0.0
    left, right = [], []
    for p in range(2):
        ge = coef[0] * gp[p, 0] + coef[1] * (hid[p, 0] - mean) + coef[2]
        go = coef[0] * gp[p, 1] + coef[1] * (hid[p, 1] - mean) + coef[2]
        bias = bias + jnp.sum(ge + go, axis=0, keepdims=True)
        ge_b, go_b = ge.astype(BF16), go.astype(BF16)
        g_out[p, 0] = ge_b
        g_out[p, 1] = go_b
        left += [lanes(go_b, ge_b, later(go).astype(BF16)), lanes(sooner(ge).astype(BF16), go_b, ge_b)]
        right += [lanes(x[p, c], x[p + 1, c], x[p + 2, c]) for c in range(2)]
    grad = dot_tn(stack(*left), stack(*right))
    full = stack(bias, sum_refs[0][0:2], jnp.zeros((5, chans), F32))
    if not packed:
        grad_out[...] = grad
        small_out[...] = full
        return
    owners = lscr.shape[1]
    chunk = chans // owners
    for kh in range(3):
        for kw in range(3):
            piece = grad[kw * chans : (kw + 1) * chans, kh * chans : (kh + 1) * chans]
            lscr[kh, :, kw * chunk : (kw + 1) * chunk, :] = piece.reshape(-1, chunk, chans)
    lscr[3, :, 0 : 2 * chunk, :] = dlast[...].reshape(owners, 2 * chunk, chans)
    wide = [cbias[0:1, i * chans : (i + 1) * chans] for i in range(cbias.shape[1] // chans)]
    row_id = lax.broadcasted_iota(jnp.int32, full.shape, 0)
    for d in range(owners):
        at = d * chunk
        mine = full if at == 0 else pltpu.roll(full, chans - at, 1)
        at = d * 2 * chunk
        row = jnp.broadcast_to(wide[at // chans], full.shape)
        if at % chans:
            row = pltpu.roll(row, chans - at % chans, 1)
        lscr[3, d, 2 * chunk :, :] = hi_lo(jnp.where(row_id == 3, row, mine))
    halve(me & 1, lscr, keep_out, send_out)
    chip = me >> 1
    early_own[...] = keep[chip] + got[chip].astype(F32)
    early_send[...] = (keep[1 - chip] + got[1 - chip].astype(F32)).astype(BF16)


def image_kernel(last, me_ref, par, hid, gm, gain, shift, par2, g, mix_top, mix, w, dw, dbias, block_out, gi_out, done_out, scr):
    half = g.shape[2]
    chans = g.shape[3]
    flat = [dw[:, k].reshape(3 * chans, dw.shape[3]) for k in range(3)]
    odd_before = lanes(mix_top[:, :chans], mix[0, :, :chans], mix[1, :, :chans])
    even = lanes(mix_top[:, chans : 2 * chans], mix[0, :, chans : 2 * chans], mix[1, :, chans : 2 * chans])
    odd = lanes(mix_top[:, 2 * chans :], mix[0, :, 2 * chans :], mix[1, :, 2 * chans :])
    block = dot(lanes(odd_before, even, odd), stack(*flat)) + dbias[...]
    block_out[...] = block.astype(BF16)

    mean, rstd = par[0:1], par[1:2]
    me = me_ref[0]
    edge = []
    for i, p, there in ((0, 0, me > 0), (1, 3, me < last)):
        keep = jnp.where(there, 1.0, 0.0)
        pair = []
        for c in range(2):
            centred = hid[i, c] - mean
            pre = centred * rstd * gain[...] + shift[...]
            sig = jax.nn.sigmoid(pre)
            gp = gm[p, c] * (sig * (1.0 + pre * (1.0 - sig)))
            pair.append(((par2[1:2] * gp + par2[2:3] * centred + par2[3:4]) * keep).astype(BF16))
        edge.append(pair)
    rows = [edge[0], [g[0, 0], g[0, 1]], [g[1, 0], g[1, 1]], edge[1]]
    tap = [lanes(w[0, k], w[1, k], w[2, k]) for k in range(3)]
    both = stack(lanes(tap[1], tap[0]), lanes(tap[2], tap[1]))
    ge = stack(*[lanes(rows[p + 2][0], rows[p + 1][0], rows[p][0]) for p in range(2)])
    go = stack(*[lanes(rows[p + 2][1], rows[p + 1][1], rows[p][1]) for p in range(2)])
    base = dot_nt(lanes(ge, go), both)
    from_odd = dot_nt(go, tap[2])
    from_even = dot_nt(ge, tap[0])
    for p in range(2):
        sl = slice(p * half, (p + 1) * half)
        scr[pl.ds(0, half, stride=2), :] = base[sl, :chans] + later(from_odd[sl]) + gm[p + 1, 0]
        scr[pl.ds(1, half, stride=2), :] = base[sl, chans:] + sooner(from_even[sl]) + gm[p + 1, 1]
        gi_out[p] = scr[...].astype(BF16)
    done_out[...] = jnp.zeros(done_out.shape, F32)


def resplit(total, on):
    whole = total[..., 0:8, :] + total[..., 8:16, :]
    return jnp.where(on, hi_lo(whole), total)


def core_kernel(me_ref, keep, got, own, send):
    me = me_ref[0]
    core, chip = me & 1, me >> 1
    own[...] = keep[chip] + got[chip].astype(F32)
    other = keep[1 - chip] + got[1 - chip].astype(F32)
    m = other.shape[1] - 16
    send[:, :m] = other[:, :m].astype(BF16)
    send[:, m:] = resplit(other[:, m:], 2 * (1 - chip) + core == 3).astype(BF16)


def rows_kernel(me_ref, early_own, early_got, late_own, late_got, after, out):
    early = early_own[...] + early_got[...].astype(F32)
    late = late_own[...] + late_got[...].astype(F32)
    n = early.shape[2]
    m = late.shape[1]
    for t in range(2):
        out[:, t * n : (t + 1) * n, :] = early[t].astype(BF16)
    out[:, 2 * n : 2 * n + m - 16, :] = late[:, : m - 16].astype(BF16)
    out[:, 2 * n + m - 16 :, :] = resplit(late[:, m - 16 :], me_ref[0] == 3).astype(BF16)


def dp_kernel(me_ref, got, out):
    total = jnp.sum(got[...].astype(F32), axis=0)
    n = total.shape[0]
    out[: n - 16] = total[: n - 16].astype(BF16)
    out[n - 16 :] = resplit(total[n - 16 :], me_ref[0] == 3).astype(BF16)


def last_kernel(chunk, me_ref, q0, q1, q2, q3, down, conv, cb, ga, sh, db, scr):
    me = me_ref[0]
    for k, ref in enumerate((q0, q1, q2, q3)):
        scr[me ^ k] = ref[...].astype(F32)
    wide = 2 * chunk
    for q in range(4):
        for t in range(2):
            down[2 * q + t] = scr[q, t * wide : (t + 1) * wide, :]
    for kh in range(3):
        for kw in range(3):
            at = 2 * wide + kw * chunk
            conv[3 * kh + kw] = scr[kh, at : at + chunk, :]
    down[8] = scr[3, 2 * wide : 3 * wide, :]
    rows = scr[3, 3 * wide : 3 * wide + 8, :] + scr[3, 3 * wide + 8 :, :]
    cb[...] = rows[0:1, :chunk]
    ga[...] = rows[1:2, :chunk]
    sh[...] = rows[2:3, :chunk]
    db[...] = rows[3:4, :wide]


def across(x):
    n = lax.axis_size("rows")
    return lax.ppermute(x, "rows", [p for i in range(1, n - 1, 2) for p in ((i, i + 1), (i + 1, i))])


def swap(x, axis, k):
    return lax.ppermute(x, axis, [(i, i ^ k) for i in range(lax.axis_size(axis))])


def shards(images, conv_weight, conv_bias, norm_gain, norm_shift, down_weight, down_bias, cotangent):
    img, cot = images[0], cotangent[0, 0]
    rows, cols, chans = img.shape
    half, outs = cot.shape
    ranks, owners = lax.axis_size("rows"), lax.axis_size("dp")
    width = chans // GROUPS
    count = float(rows * cols * width * ranks)
    chunk, wide = chans // owners, outs // owners
    packed = ranks == 4 and chunk == 16 and wide == 32
    me = lax.axis_index("rows").astype(jnp.int32).reshape(1)
    smem = pl.BlockSpec(memory_space=pltpu.SMEM)
    vmem = pl.BlockSpec(memory_space=pltpu.VMEM)
    hbm = pl.BlockSpec(memory_space=pltpu.HBM)

    def run(kernel, args, outs, scratch=(), specs=None, cost=1 << 27):
        return pl.pallas_call(
            kernel,
            in_specs=specs or [smem if a is me else vmem for a in args],
            out_shape=[jax.ShapeDtypeStruct(s, d) for s, d in outs],
            out_specs=[vmem] * len(outs),
            scratch_shapes=list(scratch),
            compiler_params=pltpu.CompilerParams(vmem_limit_bytes=24 * MIB),
            cost_estimate=pl.CostEstimate(flops=cost, bytes_accessed=1 << 10, transcendentals=0),
        )(*args)

    def with_swaps(mine, others):
        return [mine] + [swap(other, "rows", k + 1) for k, other in enumerate(others)]

    chip_img, core_img = across(img), swap(img, "rows", 1)
    row_scr = pltpu.VMEM((cols, chans), F32)
    block_of = (2, 2, half, chans)
    tile = ((8, chans), F32)
    (ahead,) = run(first_kernel, (me,), [tile], cost=1 << 34)
    raw = (
        img,
        conv_weight,
        down_weight,
        cot,
        conv_bias.reshape(1, chans),
        norm_gain.reshape(1, chans),
        norm_shift.reshape(1, chans),
        down_bias.reshape(1, outs),
    )
    w, dw, cot, bias, gain, shift, dbias, own_x, own_gm, cbias = run(
        prep_kernel,
        (ahead, *raw),
        [(v.shape, v.dtype) for v in raw[1:]] + [(block_of, BF16), ((3, 2, half, chans), F32), ((8, outs), F32)],
        [pltpu.VMEM(img.shape, BF16), row_scr, pltpu.SemaphoreType.DMA((len(raw),))],
        [vmem] + [hbm] * len(raw),
    )
    chip_cot, core_cot = across(cot), swap(cot, "rows", 1)
    x, hid, stat = run(
        functools.partial(hidden_kernel, width),
        (me, core_img, chip_img, own_x, w, bias),
        [((4, 2, half, chans), BF16), (block_of, F32), tile],
        [row_scr],
    )
    stats = with_swaps(stat, [stat] * (ranks - 1))
    hid_edge, gm = run(
        edge_kernel,
        (me, core_img, chip_img, x, w, bias, core_cot, chip_cot, dw, own_gm),
        [(block_of, F32), ((4, 2, half, chans), F32)],
        [row_scr],
    )
    par, mix, gp, sums = run(
        functools.partial(norm_kernel, width, count, ranks),
        (*stats, x, hid, gm, gain, shift),
        [tile, ((2, half, 3 * chans), BF16), (block_of, F32), tile],
    )
    all_sums = with_swaps(sums, [sums] * (ranks - 1))
    early_shape = (2, owners, wide, chans)
    late_shape = (owners, 3 * chunk, chans)
    deep = 2 * wide + 3 * chunk

    mix_top, *down_grad = run(
        functools.partial(down_kernel, packed),
        (me, par, x, hid_edge, gain, shift, mix, cot),
        [((half, 3 * chans), BF16)]
        + (
            [((outs, chans), F32), ((2,) + early_shape, F32), ((2,) + early_shape, BF16)]
            if packed
            else [((outs, 9 * chans), F32)]
        ),
        [pltpu.VMEM((4,) + early_shape, F32)] if packed else [],
    )
    if packed:
        dlast, keep, send = down_grad
        got = swap(send, "rows", 1)
    par2, g, *conv_grad = run(
        functools.partial(back_kernel, width, count, ranks, packed),
        (me, *all_sums, par, x, hid, gp, gain) + ((dlast, cbias, keep, got) if packed else ()),
        [tile, (block_of, BF16)]
        + (
            [(early_shape, F32), (early_shape, BF16), ((2,) + late_shape, F32), ((2,) + late_shape, BF16)]
            if packed
            else [((3 * chans, 3 * chans), F32), tile]
        ),
        [pltpu.VMEM((4,) + late_shape, F32)] if packed else [],
    )
    block, gi, done = run(
        functools.partial(image_kernel, ranks - 1),
        (me, par, hid_edge, gm, gain, shift, par2, g, mix_top, mix, w, dw, dbias),
        [((half, outs), BF16), ((rows, cols, chans), BF16), tile],
        [row_scr],
    )
    if packed:
        early_own, early_send, keep, send = conv_grad
        late_own, late_send = run(
            core_kernel, (me, keep, swap(send, "rows", 1)), [(late_shape, F32), (late_shape, BF16)]
        )
        (mine,) = run(
            rows_kernel,
            (me, early_own, swap(early_send, "rows", 2), late_own, swap(late_send, "rows", 2), done),
            [((owners, deep, chans), BF16)],
        )
        got = lax.all_to_all(mine, "dp", 0, 0)
        (part,) = run(dp_kernel, (me, got), [((deep, chans), BF16)])
        down, conv, cb, ga, sh, db = run(
            functools.partial(last_kernel, chunk),
            (me, *with_swaps(part, [part] * (ranks - 1))),
            [((9, wide, chans), F32), ((9, chunk, chans), F32)] + [((1, chunk), F32)] * 3 + [((1, wide), F32)],
            [pltpu.VMEM((4, deep, chans), F32)],
        )
    else:
        totals = lax.psum((down_grad[0], conv_grad[0], conv_grad[1], cbias[:1]), ("rows", "dp"))
        owner = lax.axis_index("dp")
        down = totals[0].reshape(outs, 9, chans).transpose(1, 0, 2)
        down = lax.dynamic_slice_in_dim(down, owner * wide, wide, 1)
        conv = totals[1].reshape(3, chans, 3, chans).transpose(2, 0, 1, 3).reshape(9, chans, chans)
        conv = lax.dynamic_slice_in_dim(conv, owner * chunk, chunk, 1)
        cb, ga, sh = lax.dynamic_slice_in_dim(totals[2], owner * chunk, chunk, 1)[:3]
        db = lax.dynamic_slice_in_dim(totals[3], owner * wide, wide, 1)
    return (
        block[None, None],
        gi[None],
        conv.reshape(3, 3, chunk, chans).transpose(0, 1, 3, 2),
        cb.reshape(-1),
        ga.reshape(-1),
        sh.reshape(-1),
        down.reshape(3, 3, wide, chans).transpose(0, 1, 3, 2),
        db.reshape(-1),
    )


def solution(mesh):
    spec = P("dp", "rows", None, None)
    in_specs = (spec, P(), P(), P(), P(), P(), P(), spec)
    last = P(None, None, None, "dp")
    out_specs = (spec, spec, last, P("dp"), P("dp"), P("dp"), last, P("dp"))
    return jax.shard_map(shards, mesh=mesh, in_specs=in_specs, out_specs=out_specs, check_vma=False)
```

```python
import functools

import jax
import jax.numpy as jnp
from jax import lax
from jax.experimental import pallas as pl
from jax.experimental.pallas import tpu as pltpu
from jax.sharding import PartitionSpec as P

GROUPS = 32
EPS = 1e-05
F32 = jnp.float32
BF16 = jnp.bfloat16
MIB = 1 << 20
BACK = 1 << 32


def dot(a, b):
    return jnp.dot(a, b, preferred_element_type=F32)


def dot_nt(a, b):
    return lax.dot_general(a, b, (((1,), (1,)), ((), ())), preferred_element_type=F32)


def dot_tn(a, b):
    return lax.dot_general(a, b, (((0,), (0,)), ((), ())), preferred_element_type=F32)


def lanes(*parts):
    return jnp.concatenate(parts, axis=1)


def stack(*parts):
    return jnp.concatenate(parts, axis=0)


def later(x):
    row = lax.broadcasted_iota(jnp.int32, x.shape, 0)
    return jnp.where(row == 0, 0.0, pltpu.roll(x, 1, 0))


def sooner(x):
    row = lax.broadcasted_iota(jnp.int32, x.shape, 0)
    return jnp.where(row == x.shape[0] - 1, 0.0, pltpu.roll(x, x.shape[0] - 1, 0))


def grouped(row, width):
    n = row.shape[1]
    a = lax.broadcasted_iota(jnp.int32, (n, n), 0) // width
    b = lax.broadcasted_iota(jnp.int32, (n, n), 1) // width
    same = jnp.where(a == b, 1.0, 0.0).astype(F32)
    wide = jnp.broadcast_to(row, (8, n))
    return jnp.dot(wide, same, precision=lax.Precision.HIGHEST, preferred_element_type=F32)[0:1]


def split(scr, row):
    half = row.shape[0] // 2
    scr[...] = row.astype(F32)
    return scr[pl.ds(0, half, stride=2), :], scr[pl.ds(1, half, stride=2), :]


def conv_weights(w):
    tap = [stack(w[0, k], w[1, k], w[2, k]) for k in range(3)]
    return stack(lanes(tap[1], tap[0]), lanes(tap[2], tap[1])), tap[0], tap[2]


def conv_rows(even, odd, weights, bias):
    both, first, last = weights
    base = dot(lanes(even, odd), both)
    chans = first.shape[1]
    from_odd = dot(odd, first)
    from_even = dot(even, last)
    return base[:, :chans] + bias, base[:, chans:] + bias, from_odd, from_even


def first_kernel(me_ref, out):
    out[...] = jnp.zeros(out.shape, F32)


def prep_kernel(ahead, img, w, dw, cot, bias, gain, shift, dbias, *refs):
    outs, (x_out, gm_out, cb_out, img_v, scr, sems) = refs[:7], refs[7:]
    pairs = list(zip((img, w, dw, cot, bias, gain, shift, dbias), (img_v,) + outs))
    copies = [pltpu.make_async_copy(src, dst, sems.at[i]) for i, (src, dst) in enumerate(pairs)]
    for copy in copies:
        copy.start()
    copies[0].wait()
    for p in range(2):
        even, odd = split(scr, img_v[p])
        x_out[p, 0] = even.astype(BF16)
        x_out[p, 1] = odd.astype(BF16)
    for copy in copies[1:]:
        copy.wait()
    dw_v, cot_v = outs[1], outs[2]
    for p, kh in enumerate(range(3)):
        even, odd, late = back_taps(cot_v[...], dw_v, kh)
        gm_out[p, 0] = even
        gm_out[p, 1] = odd + sooner(late)
    cb_out[...] = jnp.broadcast_to(jnp.sum(cot_v[...].astype(F32), axis=0, keepdims=True), cb_out.shape)


def back_taps(c, dw, kh):
    chans, outs = dw.shape[2:]
    got = dot_nt(c, dw[kh].reshape(3 * chans, outs))
    return got[:, chans : 2 * chans], got[:, 2 * chans :], got[:, :chans]


def either(flag, a, b):
    return jnp.where(flag, a.astype(F32), b.astype(F32))


def hidden_kernel(width, me_ref, core, chip, own, w, bias, x_out, hid_out, stat_out, scr):
    half = x_out.shape[2]
    odd_rank = (me_ref[0] & 1) == 1
    for p, row in ((0, either(odd_rank, core[1], chip[1])), (3, either(odd_rank, chip[0], core[0]))):
        even, odd = split(scr, row)
        x_out[p, 0] = even.astype(BF16)
        x_out[p, 1] = odd.astype(BF16)
    for p in range(2):
        x_out[p + 1] = own[p]
    weights = conv_weights(w)
    even = stack(*[lanes(x_out[p, 0], x_out[p + 1, 0], x_out[p + 2, 0]) for p in range(2)])
    odd = stack(*[lanes(x_out[p, 1], x_out[p + 1, 1], x_out[p + 2, 1]) for p in range(2)])
    base_e, base_o, from_odd, from_even = conv_rows(even, odd, weights, bias[...])
    total = 0.0
    for p in range(2):
        sl = slice(p * half, (p + 1) * half)
        he = base_e[sl] + later(from_odd[sl])
        ho = base_o[sl] + sooner(from_even[sl])
        hid_out[p, 0] = he
        hid_out[p, 1] = ho
        total = total + jnp.sum(he + ho, axis=0, keepdims=True)
    mean = grouped(total, width) / float(4 * half * width)
    spread = 0.0
    for p in range(2):
        for c in range(2):
            d = hid_out[p, c] - mean
            spread = spread + jnp.sum(d * d, axis=0, keepdims=True)
    stat_out[...] = jnp.zeros(stat_out.shape, F32)
    stat_out[0:1] = mean
    stat_out[1:2] = grouped(spread, width)


def edge_kernel(me_ref, core, chip, x, w, bias, cot_core, cot_chip, dw, own_gm, hid_out, gm_out, scr):
    half = x.shape[2]
    odd_rank = (me_ref[0] & 1) == 1
    top = [v.astype(BF16) for v in split(scr, either(odd_rank, core[0], chip[0]))]
    low = [v.astype(BF16) for v in split(scr, either(odd_rank, chip[1], core[1]))]
    weights = conv_weights(w)
    even = stack(lanes(top[0], x[0, 0], x[1, 0]), lanes(x[2, 0], x[3, 0], low[0]))
    odd = stack(lanes(top[1], x[0, 1], x[1, 1]), lanes(x[2, 1], x[3, 1], low[1]))
    base_e, base_o, from_odd, from_even = conv_rows(even, odd, weights, bias[...])
    for p in range(2):
        sl = slice(p * half, (p + 1) * half)
        hid_out[p, 0] = base_e[sl] + later(from_odd[sl])
        hid_out[p, 1] = base_o[sl] + sooner(from_even[sl])
    above = either(odd_rank, cot_core[...], cot_chip[...]).astype(BF16)
    below = either(odd_rank, cot_chip[...], cot_core[...]).astype(BF16)
    zero = jnp.zeros((half, x.shape[3]), F32)
    for p, c, kh in ((0, above, 2), (1, None, 0), (2, below, 0), (3, below, 1)):
        even, odd, late = back_taps(c, dw, kh) if c is not None else (zero, zero, zero)
        own = own_gm[p] if p < 3 else (zero, zero)
        gm_out[p, 0] = own[0] + even
        gm_out[p, 1] = own[1] + (odd + sooner(late) if c is not None else odd)


def norm_kernel(width, count, ranks, *refs):
    stats = refs[:ranks]
    x, hid, gm, gain, shift, par_out, mix_out, gp_out, sum_out = refs[ranks:]
    half = x.shape[2]
    local = float(4 * half * width)
    mean = sum(s[0:1] for s in stats) / float(len(stats))
    spread = 0.0
    for s in stats:
        d = s[0:1] - mean
        spread = spread + (s[1:2] + local * (d * d))
    rstd = lax.rsqrt(spread / count + EPS)
    par_out[...] = jnp.zeros(par_out.shape, F32)
    par_out[0:1] = mean
    par_out[1:2] = rstd
    first = 0.0
    second = 0.0
    for p in range(2):
        mixed = []
        for c in range(2):
            normed = (hid[p, c] - mean) * rstd
            pre = normed * gain[...] + shift[...]
            sig = jax.nn.sigmoid(pre)
            mixed.append(x[p + 1, c].astype(F32) + pre * sig)
            gp = gm[p + 1, c] * (sig * (1.0 + pre * (1.0 - sig)))
            gp_out[p, c] = gp
            first = first + jnp.sum(gp * normed, axis=0, keepdims=True)
            second = second + jnp.sum(gp, axis=0, keepdims=True)
        mix_out[p] = lanes(later(mixed[1]).astype(BF16), mixed[0].astype(BF16), mixed[1].astype(BF16))
    sum_out[...] = jnp.zeros(sum_out.shape, F32)
    sum_out[0:1] = first
    sum_out[1:2] = second


def down_kernel(packed, me_ref, par, x, hid, gain, shift, mix, cot, top_out, *rest):
    mean, rstd = par[0:1], par[1:2]
    chans = x.shape[3]
    inside = jnp.where(me_ref[0] > 0, 1.0, 0.0)
    mixed = []
    for c in range(2):
        pre = (hid[0, c] - mean) * rstd * gain[...] + shift[...]
        mixed.append((x[0, c].astype(F32) + pre * jax.nn.sigmoid(pre)) * inside)
    top = lanes(later(mixed[1]).astype(BF16), mixed[0].astype(BF16), mixed[1].astype(BF16))
    top_out[...] = top
    grad = dot_tn(cot[...], lanes(top, mix[0], mix[1]))
    if not packed:
        rest[0][...] = grad
        return
    last_out, keep_out, send_out, dscr = rest
    outs_chunk = keep_out.shape[3]
    for q in range(4):
        for t in range(2):
            tap = 2 * q + t
            dscr[q, t] = grad[:, tap * chans : (tap + 1) * chans].reshape(-1, outs_chunk, chans)
    last_out[...] = grad[:, 8 * chans :]
    halve(me_ref[0] & 1, dscr, keep_out, send_out)


def halve(core, quarters, keep_out, *send_outs):
    n = len(send_outs)
    for i in range(2):
        keep_out[i] = quarters[2 * i + core]
        other = quarters[2 * i + 1 - core].astype(BF16)
        size = other.shape[-2] // n
        for j, ref in enumerate(send_outs):
            ref[i] = other[..., j * size : (j + 1) * size, :]


def hi_lo(full):
    hi = full.astype(BF16).astype(F32)
    return jnp.concatenate([hi, full - hi], axis=-2)


def back_kernel(width, count, ranks, packed, me_ref, *refs):
    sum_refs = refs[:ranks]
    par, x, hid, gp, gain, _, *refs = refs[ranks:]
    if packed:
        dlast, cbias, par_out, g_out, keep_out, *send_outs, lscr = refs
    else:
        par_out, g_out, grad_out, small_out = refs
    half = x.shape[2]
    chans = x.shape[3]
    me = me_ref[0]
    mean, rstd = par[0:1], par[1:2]
    sums = sum(s[...] for s in sum_refs)
    m2 = grouped(sums[0:1] * gain[...], width) / count
    m1 = grouped(sums[1:2] * gain[...], width) / count
    coef = (rstd * gain[...], -(rstd * rstd) * m2, -rstd * m1)
    par_out[...] = jnp.zeros(par_out.shape, F32)
    par_out[0:1] = mean
    for i in range(3):
        par_out[1 + i : 2 + i] = coef[i]
    bias = 0.0
    left, right = [], []
    for p in range(2):
        ge = coef[0] * gp[p, 0] + coef[1] * (hid[p, 0] - mean) + coef[2]
        go = coef[0] * gp[p, 1] + coef[1] * (hid[p, 1] - mean) + coef[2]
        bias = bias + jnp.sum(ge + go, axis=0, keepdims=True)
        ge_b, go_b = ge.astype(BF16), go.astype(BF16)
        g_out[p, 0] = ge_b
        g_out[p, 1] = go_b
        left += [lanes(go_b, ge_b, later(go).astype(BF16)), lanes(sooner(ge).astype(BF16), go_b, ge_b)]
        right += [lanes(x[p, c], x[p + 1, c], x[p + 2, c]) for c in range(2)]
    grad = dot_tn(stack(*left), stack(*right))
    full = stack(bias, sum_refs[0][0:2], jnp.zeros((5, chans), F32))
    if not packed:
        grad_out[...] = grad
        small_out[...] = full
        return
    owners = lscr.shape[1]
    chunk = chans // owners
    for kh in range(3):
        for kw in range(3):
            piece = grad[kw * chans : (kw + 1) * chans, kh * chans : (kh + 1) * chans]
            lscr[kh, :, kw * chunk : (kw + 1) * chunk, :] = piece.reshape(-1, chunk, chans)
    lscr[3, :, 0 : 2 * chunk, :] = dlast[...].reshape(owners, 2 * chunk, chans)
    wide = [cbias[0:1, i * chans : (i + 1) * chans] for i in range(cbias.shape[1] // chans)]
    row_id = lax.broadcasted_iota(jnp.int32, full.shape, 0)
    for d in range(owners):
        at = d * chunk
        mine = full if at == 0 else pltpu.roll(full, chans - at, 1)
        at = d * 2 * chunk
        row = jnp.broadcast_to(wide[at // chans], full.shape)
        if at % chans:
            row = pltpu.roll(row, chans - at % chans, 1)
        lscr[3, d, 2 * chunk :, :] = hi_lo(jnp.where(row_id == 3, row, mine))
    halve(me & 1, lscr, keep_out, *send_outs)


def block_kernel(ahead, mix_top, mix, dw, dbias, block_out, done_out):
    chans, outs = dw.shape[2:]
    flat = [dw[:, k].reshape(3 * chans, outs) for k in range(3)]
    odd_before = lanes(mix_top[:, :chans], mix[0, :, :chans], mix[1, :, :chans])
    even = lanes(mix_top[:, chans : 2 * chans], mix[0, :, chans : 2 * chans], mix[1, :, chans : 2 * chans])
    odd = lanes(mix_top[:, 2 * chans :], mix[0, :, 2 * chans :], mix[1, :, 2 * chans :])
    block = dot(lanes(odd_before, even, odd), stack(*flat)) + dbias[...]
    block_out[...] = block.astype(BF16)
    done_out[...] = jnp.zeros(done_out.shape, F32)


def image_kernel(last, me_ref, par, hid, gm, gain, shift, par2, g, w, gi_out, done_out, scr):
    half = g.shape[2]
    chans = g.shape[3]
    mean, rstd = par[0:1], par[1:2]
    me = me_ref[0]
    edge = []
    for i, p, there in ((0, 0, me > 0), (1, 3, me < last)):
        keep = jnp.where(there, 1.0, 0.0)
        pair = []
        for c in range(2):
            centred = hid[i, c] - mean
            pre = centred * rstd * gain[...] + shift[...]
            sig = jax.nn.sigmoid(pre)
            gp = gm[p, c] * (sig * (1.0 + pre * (1.0 - sig)))
            pair.append(((par2[1:2] * gp + par2[2:3] * centred + par2[3:4]) * keep).astype(BF16))
        edge.append(pair)
    rows = [edge[0], [g[0, 0], g[0, 1]], [g[1, 0], g[1, 1]], edge[1]]
    tap = [lanes(w[0, k], w[1, k], w[2, k]) for k in range(3)]
    both = stack(lanes(tap[1], tap[0]), lanes(tap[2], tap[1]))
    ge = stack(*[lanes(rows[p + 2][0], rows[p + 1][0], rows[p][0]) for p in range(2)])
    go = stack(*[lanes(rows[p + 2][1], rows[p + 1][1], rows[p][1]) for p in range(2)])
    base = dot_nt(lanes(ge, go), both)
    from_odd = dot_nt(go, tap[2])
    from_even = dot_nt(ge, tap[0])
    for p in range(2):
        sl = slice(p * half, (p + 1) * half)
        scr[pl.ds(0, half, stride=2), :] = base[sl, :chans] + later(from_odd[sl]) + gm[p + 1, 0]
        scr[pl.ds(1, half, stride=2), :] = base[sl, chans:] + sooner(from_even[sl]) + gm[p + 1, 1]
        gi_out[p] = scr[...].astype(BF16)
    done_out[...] = jnp.zeros(done_out.shape, F32)


def rounded(total, on):
    n = total.shape[0] - 16
    last = total[n:]
    whole = last[0:8] + last[8:16]
    last = jnp.where(on, hi_lo(whole), last)
    return stack(total[:n], last).astype(BF16)


def early_kernel(me_ref, keep, got, own, send, done_out):
    done_out[...] = jnp.zeros(done_out.shape, F32)
    chip = me_ref[0] >> 1
    own[...] = keep[chip] + got[chip].astype(F32)
    send[...] = (keep[1 - chip] + got[1 - chip].astype(F32)).astype(BF16)


def late_kernel(me_ref, owner_ref, keep, got0, got1, got2, e_own, e_got, own, sx, sy, sxy, ey_own, ey_send):
    me, side = me_ref[0], owner_ref[0] & 1
    core, chip = me & 1, me >> 1
    mine, other = me == 3, 2 * (1 - chip) + core == 3

    def total(x, d):
        parts = [got[x, d].astype(F32) for got in (got0, got1, got2)]
        return keep[x, d] + jnp.concatenate(parts, axis=0)

    for z in range(own.shape[0]):
        here, there = 2 * z + side, 2 * z + 1 - side
        own[z] = total(chip, here)
        sx[z] = rounded(total(1 - chip, here), other)
        sy[z] = rounded(total(chip, there), mine)
        sxy[z] = rounded(total(1 - chip, there), other)
        for t in range(2):
            ey_own[t, z] = e_own[t, here] + e_got[t, here].astype(F32)
            ey_send[t, z] = (e_own[t, there] + e_got[t, there].astype(F32)).astype(BF16)


def pack_kernel(me_ref, owner_ref, own, gx, gy, gxy, ey_own, ey_got, after, out, s1, s2, s3, scr):
    z = owner_ref[0] >> 1
    early = ey_own[...] + ey_got[...].astype(F32)
    n = early.shape[2]
    for t in range(2):
        scr[:, t * n : (t + 1) * n, :] = early[t]
    scr[:, 2 * n :, :] = own[...] + gx[...].astype(F32) + gy[...].astype(F32) + gxy[...].astype(F32)
    out[...] = scr[z]
    for k, ref in ((1, s1), (2, s2), (3, s3)):
        ref[...] = rounded(scr[z ^ k], me_ref[0] == 3)


def sum_kernel(me_ref, own, g1, g2, g3, out, send):
    total = own[...] + g1[...].astype(F32) + g2[...].astype(F32) + g3[...].astype(F32)
    out[...] = total
    send[...] = rounded(total, me_ref[0] == 3)


def last_kernel(chunk, me_ref, q0, q1, q2, q3, down, conv, cb, ga, sh, db, scr):
    me = me_ref[0]
    for k, ref in enumerate((q0, q1, q2, q3)):
        scr[me ^ k] = ref[...].astype(F32)
    wide = 2 * chunk
    for q in range(4):
        for t in range(2):
            down[2 * q + t] = scr[q, t * wide : (t + 1) * wide, :]
    for kh in range(3):
        for kw in range(3):
            at = 2 * wide + kw * chunk
            conv[3 * kh + kw] = scr[kh, at : at + chunk, :]
    down[8] = scr[3, 2 * wide : 3 * wide, :]
    rows = scr[3, 3 * wide : 3 * wide + 8, :] + scr[3, 3 * wide + 8 :, :]
    cb[...] = rows[0:1, :chunk]
    ga[...] = rows[1:2, :chunk]
    sh[...] = rows[2:3, :chunk]
    db[...] = rows[3:4, :wide]


def across(x):
    n = lax.axis_size("rows")
    return lax.ppermute(x, "rows", [p for i in range(1, n - 1, 2) for p in ((i, i + 1), (i + 1, i))])


def swap(x, axis, k):
    return lax.ppermute(x, axis, [(i, i ^ k) for i in range(lax.axis_size(axis))])


def swap_both(x, k_rows, k_dp):
    both = ("rows", "dp")
    k = k_rows * lax.axis_size("dp") + k_dp
    return lax.ppermute(x, both, [(i, i ^ k) for i in range(lax.axis_size(both))])


def shards(images, conv_weight, conv_bias, norm_gain, norm_shift, down_weight, down_bias, cotangent):
    img, cot = images[0], cotangent[0, 0]
    rows, cols, chans = img.shape
    half, outs = cot.shape
    ranks, owners = lax.axis_size("rows"), lax.axis_size("dp")
    width = chans // GROUPS
    count = float(rows * cols * width * ranks)
    chunk, wide = chans // owners, outs // owners
    packed = ranks == 4 and owners == 8 and chunk == 16 and wide == 32
    me = lax.axis_index("rows").astype(jnp.int32).reshape(1)
    owner = lax.axis_index("dp").astype(jnp.int32).reshape(1)
    smem = pl.BlockSpec(memory_space=pltpu.SMEM)
    vmem = pl.BlockSpec(memory_space=pltpu.VMEM)
    hbm = pl.BlockSpec(memory_space=pltpu.HBM)

    def run(kernel, args, outs, scratch=(), specs=None, cost=1 << 27):
        return pl.pallas_call(
            kernel,
            in_specs=specs or [smem if a is me or a is owner else vmem for a in args],
            out_shape=[jax.ShapeDtypeStruct(s, d) for s, d in outs],
            out_specs=[vmem] * len(outs),
            scratch_shapes=list(scratch),
            compiler_params=pltpu.CompilerParams(vmem_limit_bytes=24 * MIB),
            cost_estimate=pl.CostEstimate(flops=cost, bytes_accessed=1 << 10, transcendentals=0),
        )(*args)

    def with_swaps(mine, other):
        return [mine] + [swap(other, "rows", k) for k in range(1, ranks)]

    chip_img, core_img = across(img), swap(img, "rows", 1)
    row_scr = pltpu.VMEM((cols, chans), F32)
    block_of = (2, 2, half, chans)
    tile = ((8, chans), F32)
    (ahead,) = run(first_kernel, (me,), [tile], cost=1 << 34)
    raw = (
        img,
        conv_weight,
        down_weight,
        cot,
        conv_bias.reshape(1, chans),
        norm_gain.reshape(1, chans),
        norm_shift.reshape(1, chans),
        down_bias.reshape(1, outs),
    )
    w, dw, cot, bias, gain, shift, dbias, own_x, own_gm, cbias = run(
        prep_kernel,
        (ahead, *raw),
        [(v.shape, v.dtype) for v in raw[1:]] + [(block_of, BF16), ((3, 2, half, chans), F32), ((8, outs), F32)],
        [pltpu.VMEM(img.shape, BF16), row_scr, pltpu.SemaphoreType.DMA((len(raw),))],
        [vmem] + [hbm] * len(raw),
    )
    chip_cot, core_cot = across(cot), swap(cot, "rows", 1)
    x, hid, stat = run(
        functools.partial(hidden_kernel, width),
        (me, core_img, chip_img, own_x, w, bias),
        [((4, 2, half, chans), BF16), (block_of, F32), tile],
        [row_scr],
    )
    stats = with_swaps(stat, stat)
    hid_edge, gm = run(
        edge_kernel,
        (me, core_img, chip_img, x, w, bias, core_cot, chip_cot, dw, own_gm),
        [(block_of, F32), ((4, 2, half, chans), F32)],
        [row_scr],
    )
    par, mix, gp, sums = run(
        functools.partial(norm_kernel, width, count, ranks),
        (*stats, x, hid, gm, gain, shift),
        [tile, ((2, half, 3 * chans), BF16), (block_of, F32), tile],
    )
    all_sums = with_swaps(sums, sums)
    early_shape = (2, owners, wide, chans)
    late_shape = (owners, 3 * chunk, chans)
    deep = 2 * wide + 3 * chunk

    mix_top, *down_grad = run(
        functools.partial(down_kernel, packed),
        (me, par, x, hid_edge, gain, shift, mix, cot),
        [((half, 3 * chans), BF16)]
        + (
            [((outs, chans), F32), ((2,) + early_shape, F32), ((2,) + early_shape, BF16)]
            if packed
            else [((outs, 9 * chans), F32)]
        ),
        [pltpu.VMEM((4,) + early_shape, F32)] if packed else [],
    )
    if packed:
        dlast, keep, send = down_grad
        early_own, early_send, ahead = run(
            early_kernel, (me, keep, swap(send, "rows", 1)), [(early_shape, F32), (early_shape, BF16), tile]
        )
        early_got = swap(early_send, "rows", 2)
    block, block_done = run(block_kernel, (ahead, mix_top, mix, dw, dbias), [((half, outs), BF16), tile])
    par2, g, *conv_grad = run(
        functools.partial(back_kernel, width, count, ranks, packed),
        (me, *all_sums, par, x, hid, gp, gain, block_done) + ((dlast, cbias) if packed else ()),
        [tile, (block_of, BF16)]
        + (
            [((2,) + late_shape, F32)] + [((2, owners, chunk, chans), BF16)] * 3
            if packed
            else [((3 * chans, 3 * chans), F32), tile]
        ),
        [pltpu.VMEM((4,) + late_shape, F32)] if packed else [],
        cost=BACK,
    )
    gi, done = run(
        functools.partial(image_kernel, ranks - 1),
        (me, par, hid_edge, gm, gain, shift, par2, g, w),
        [((rows, cols, chans), BF16), tile],
        [row_scr],
    )
    if packed:
        keep, *sends = conv_grad
        zs = owners // 2
        late_cut, early_cut = (zs, 3 * chunk, chans), (2, zs, wide, chans)
        late_own, sx, sy, sxy, early_own, early_send = run(
            late_kernel,
            (me, owner, keep, *[swap(send, "rows", 1) for send in sends], early_own, early_got),
            [(late_cut, F32)] + [(late_cut, BF16)] * 3 + [(early_cut, F32), (early_cut, BF16)],
        )
        gxy = swap_both(sxy, 2, 1)
        late_got = swap(sx, "rows", 2), swap(sy, "dp", 1), gxy
        part, *sends = run(
            pack_kernel,
            (me, owner, late_own, *late_got, early_own, swap(early_send, "dp", 1), done),
            [((deep, chans), F32)] + [((deep, chans), BF16)] * 3,
            [pltpu.VMEM((zs, deep, chans), F32)],
        )
        part, send = run(
            sum_kernel,
            (me, part, *[swap(sends[k], "dp", 2 * k + 2) for k in (1, 2, 0)]),
            [((deep, chans), F32), ((deep, chans), BF16)],
        )
        down, conv, cb, ga, sh, db = run(
            functools.partial(last_kernel, chunk),
            (me, *with_swaps(part, send)),
            [((9, wide, chans), F32), ((9, chunk, chans), F32)] + [((1, chunk), F32)] * 3 + [((1, wide), F32)],
            [pltpu.VMEM((4, deep, chans), F32)],
        )
    else:
        totals = lax.psum((down_grad[0], conv_grad[0], conv_grad[1], cbias[:1]), ("rows", "dp"))
        owner = owner[0]
        down = totals[0].reshape(outs, 9, chans).transpose(1, 0, 2)
        down = lax.dynamic_slice_in_dim(down, owner * wide, wide, 1)
        conv = totals[1].reshape(3, chans, 3, chans).transpose(2, 0, 1, 3).reshape(9, chans, chans)
        conv = lax.dynamic_slice_in_dim(conv, owner * chunk, chunk, 1)
        cb, ga, sh = lax.dynamic_slice_in_dim(totals[2], owner * chunk, chunk, 1)[:3]
        db = lax.dynamic_slice_in_dim(totals[3], owner * wide, wide, 1)
    return (
        block[None, None],
        gi[None],
        conv.reshape(3, 3, chunk, chans).transpose(0, 1, 3, 2),
        cb.reshape(-1),
        ga.reshape(-1),
        sh.reshape(-1),
        down.reshape(3, 3, wide, chans).transpose(0, 1, 3, 2),
        db.reshape(-1),
    )


def solution(mesh):
    spec = P("dp", "rows", None, None)
    in_specs = (spec, P(), P(), P(), P(), P(), P(), spec)
    last = P(None, None, None, "dp")
    out_specs = (spec, spec, last, P("dp"), P("dp"), P("dp"), last, P("dp"))
    return jax.shard_map(shards, mesh=mesh, in_specs=in_specs, out_specs=out_specs, check_vma=False)
```

```python
import functools

import jax
import jax.numpy as jnp
from jax import lax
from jax.experimental import pallas as pl
from jax.experimental.pallas import tpu as pltpu
from jax.sharding import PartitionSpec as P

GROUPS = 32
EPS = 1e-05
F32 = jnp.float32
BF16 = jnp.bfloat16
MIB = 1 << 20
BACK = 1 << 32


def dot(a, b):
    return jnp.dot(a, b, preferred_element_type=F32)


def dot_nt(a, b):
    return lax.dot_general(a, b, (((1,), (1,)), ((), ())), preferred_element_type=F32)


def dot_tn(a, b):
    return lax.dot_general(a, b, (((0,), (0,)), ((), ())), preferred_element_type=F32)


def lanes(*parts):
    return jnp.concatenate(parts, axis=1)


def stack(*parts):
    return jnp.concatenate(parts, axis=0)


def later(x):
    row = lax.broadcasted_iota(jnp.int32, x.shape, 0)
    return jnp.where(row == 0, 0.0, pltpu.roll(x, 1, 0))


def sooner(x):
    row = lax.broadcasted_iota(jnp.int32, x.shape, 0)
    return jnp.where(row == x.shape[0] - 1, 0.0, pltpu.roll(x, x.shape[0] - 1, 0))


def grouped(row, width):
    n = row.shape[1]
    a = lax.broadcasted_iota(jnp.int32, (n, n), 0) // width
    b = lax.broadcasted_iota(jnp.int32, (n, n), 1) // width
    same = jnp.where(a == b, 1.0, 0.0).astype(F32)
    wide = jnp.broadcast_to(row, (8, n))
    return jnp.dot(wide, same, precision=lax.Precision.HIGHEST, preferred_element_type=F32)[0:1]


def split(scr, row):
    half = row.shape[0] // 2
    scr[...] = row.astype(F32)
    return scr[pl.ds(0, half, stride=2), :], scr[pl.ds(1, half, stride=2), :]


def conv_weights(w):
    tap = [stack(w[0, k], w[1, k], w[2, k]) for k in range(3)]
    return stack(lanes(tap[1], tap[0]), lanes(tap[2], tap[1])), tap[0], tap[2]


def conv_rows(even, odd, weights, bias):
    both, first, last = weights
    base = dot(lanes(even, odd), both)
    chans = first.shape[1]
    from_odd = dot(odd, first)
    from_even = dot(even, last)
    return base[:, :chans] + bias, base[:, chans:] + bias, from_odd, from_even


def first_kernel(me_ref, out):
    out[...] = jnp.zeros(out.shape, F32)


def prep_kernel(ahead, img, w, dw, cot, bias, gain, shift, dbias, *refs):
    outs, (x_out, gm_out, cb_out, img_v, scr, sems) = refs[:7], refs[7:]
    pairs = list(zip((img, w, dw, cot, bias, gain, shift, dbias), (img_v,) + outs))
    copies = [pltpu.make_async_copy(src, dst, sems.at[i]) for i, (src, dst) in enumerate(pairs)]
    for copy in copies:
        copy.start()
    copies[0].wait()
    for p in range(2):
        even, odd = split(scr, img_v[p])
        x_out[p, 0] = even.astype(BF16)
        x_out[p, 1] = odd.astype(BF16)
    for copy in copies[1:]:
        copy.wait()
    dw_v, cot_v = outs[1], outs[2]
    for p, kh in enumerate(range(3)):
        even, odd, late = back_taps(cot_v[...], dw_v, kh)
        gm_out[p, 0] = even
        gm_out[p, 1] = odd + sooner(late)
    cb_out[...] = jnp.broadcast_to(jnp.sum(cot_v[...].astype(F32), axis=0, keepdims=True), cb_out.shape)


def back_taps(c, dw, kh):
    chans, outs = dw.shape[2:]
    got = dot_nt(c, dw[kh].reshape(3 * chans, outs))
    return got[:, chans : 2 * chans], got[:, 2 * chans :], got[:, :chans]


def either(flag, a, b):
    return jnp.where(flag, a.astype(F32), b.astype(F32))


def hidden_kernel(width, me_ref, core, chip, own, w, bias, x_out, hid_out, stat_out, scr):
    half = x_out.shape[2]
    odd_rank = (me_ref[0] & 1) == 1
    for p, row in ((0, either(odd_rank, core[1], chip[1])), (3, either(odd_rank, chip[0], core[0]))):
        even, odd = split(scr, row)
        x_out[p, 0] = even.astype(BF16)
        x_out[p, 1] = odd.astype(BF16)
    for p in range(2):
        x_out[p + 1] = own[p]
    weights = conv_weights(w)
    even = stack(*[lanes(x_out[p, 0], x_out[p + 1, 0], x_out[p + 2, 0]) for p in range(2)])
    odd = stack(*[lanes(x_out[p, 1], x_out[p + 1, 1], x_out[p + 2, 1]) for p in range(2)])
    base_e, base_o, from_odd, from_even = conv_rows(even, odd, weights, bias[...])
    total = 0.0
    for p in range(2):
        sl = slice(p * half, (p + 1) * half)
        he = base_e[sl] + later(from_odd[sl])
        ho = base_o[sl] + sooner(from_even[sl])
        hid_out[p, 0] = he
        hid_out[p, 1] = ho
        total = total + jnp.sum(he + ho, axis=0, keepdims=True)
    mean = grouped(total, width) / float(4 * half * width)
    spread = 0.0
    for p in range(2):
        for c in range(2):
            d = hid_out[p, c] - mean
            spread = spread + jnp.sum(d * d, axis=0, keepdims=True)
    stat_out[...] = jnp.zeros(stat_out.shape, F32)
    stat_out[0:1] = mean
    stat_out[1:2] = grouped(spread, width)


def edge_kernel(me_ref, core, chip, x, w, bias, cot_core, cot_chip, dw, own_gm, hid_out, gm_out, scr):
    half = x.shape[2]
    odd_rank = (me_ref[0] & 1) == 1
    top = [v.astype(BF16) for v in split(scr, either(odd_rank, core[0], chip[0]))]
    low = [v.astype(BF16) for v in split(scr, either(odd_rank, chip[1], core[1]))]
    weights = conv_weights(w)
    even = stack(lanes(top[0], x[0, 0], x[1, 0]), lanes(x[2, 0], x[3, 0], low[0]))
    odd = stack(lanes(top[1], x[0, 1], x[1, 1]), lanes(x[2, 1], x[3, 1], low[1]))
    base_e, base_o, from_odd, from_even = conv_rows(even, odd, weights, bias[...])
    for p in range(2):
        sl = slice(p * half, (p + 1) * half)
        hid_out[p, 0] = base_e[sl] + later(from_odd[sl])
        hid_out[p, 1] = base_o[sl] + sooner(from_even[sl])
    above = either(odd_rank, cot_core[...], cot_chip[...]).astype(BF16)
    below = either(odd_rank, cot_chip[...], cot_core[...]).astype(BF16)
    zero = jnp.zeros((half, x.shape[3]), F32)
    for p, c, kh in ((0, above, 2), (1, None, 0), (2, below, 0), (3, below, 1)):
        even, odd, late = back_taps(c, dw, kh) if c is not None else (zero, zero, zero)
        own = own_gm[p] if p < 3 else (zero, zero)
        gm_out[p, 0] = own[0] + even
        gm_out[p, 1] = own[1] + (odd + sooner(late) if c is not None else odd)


def norm_kernel(width, count, ranks, *refs):
    stats = refs[:ranks]
    x, hid, gm, gain, shift, par_out, mix_out, gp_out, sum_out = refs[ranks:]
    half = x.shape[2]
    local = float(4 * half * width)
    mean = sum(s[0:1] for s in stats) / float(len(stats))
    spread = 0.0
    for s in stats:
        d = s[0:1] - mean
        spread = spread + (s[1:2] + local * (d * d))
    rstd = lax.rsqrt(spread / count + EPS)
    par_out[...] = jnp.zeros(par_out.shape, F32)
    par_out[0:1] = mean
    par_out[1:2] = rstd
    first = 0.0
    second = 0.0
    for p in range(2):
        mixed = []
        for c in range(2):
            normed = (hid[p, c] - mean) * rstd
            pre = normed * gain[...] + shift[...]
            sig = jax.nn.sigmoid(pre)
            mixed.append(x[p + 1, c].astype(F32) + pre * sig)
            gp = gm[p + 1, c] * (sig * (1.0 + pre * (1.0 - sig)))
            gp_out[p, c] = gp
            first = first + jnp.sum(gp * normed, axis=0, keepdims=True)
            second = second + jnp.sum(gp, axis=0, keepdims=True)
        mix_out[p] = lanes(later(mixed[1]).astype(BF16), mixed[0].astype(BF16), mixed[1].astype(BF16))
    sum_out[...] = jnp.zeros(sum_out.shape, F32)
    sum_out[0:1] = first
    sum_out[1:2] = second


def down_kernel(packed, me_ref, par, x, hid, gain, shift, mix, cot, top_out, *rest):
    mean, rstd = par[0:1], par[1:2]
    chans = x.shape[3]
    inside = jnp.where(me_ref[0] > 0, 1.0, 0.0)
    mixed = []
    for c in range(2):
        pre = (hid[0, c] - mean) * rstd * gain[...] + shift[...]
        mixed.append((x[0, c].astype(F32) + pre * jax.nn.sigmoid(pre)) * inside)
    top = lanes(later(mixed[1]).astype(BF16), mixed[0].astype(BF16), mixed[1].astype(BF16))
    top_out[...] = top
    grad = dot_tn(cot[...], lanes(top, mix[0], mix[1]))
    if not packed:
        rest[0][...] = grad
        return
    last_out, keep_out, send_out = rest
    outs_chunk = keep_out.shape[3]
    taps = [grad[:, t * chans : (t + 1) * chans] for t in range(9)]
    last_out[...] = taps[8]
    for t in range(2):
        quarters = [taps[2 * q + t].reshape(-1, outs_chunk, chans) for q in range(4)]
        halve(me_ref[0] & 1, quarters, keep_out, [send_out], (t,))


def halve(core, quarters, keep_out, send_outs, at=()):
    first = core == 0
    for i in range(2):
        one, two = quarters[2 * i], quarters[2 * i + 1]
        keep_out[(i, *at)] = jnp.where(first, one, two)
        other = jnp.where(first, two, one).astype(BF16)
        size = other.shape[0] // len(send_outs)
        for j, ref in enumerate(send_outs):
            ref[(i, *at)] = other[j * size : (j + 1) * size]


def hi_lo(full):
    hi = full.astype(BF16).astype(F32)
    return jnp.concatenate([hi, full - hi], axis=-2)


def back_kernel(width, count, ranks, packed, me_ref, *refs):
    sum_refs = refs[:ranks]
    par, x, hid, gp, gain, _, *refs = refs[ranks:]
    if packed:
        dlast, cbias, par_out, g_out, keep_out, *send_outs = refs
    else:
        par_out, g_out, grad_out, small_out = refs
    half = x.shape[2]
    chans = x.shape[3]
    me = me_ref[0]
    mean, rstd = par[0:1], par[1:2]
    sums = sum(s[...] for s in sum_refs)
    m2 = grouped(sums[0:1] * gain[...], width) / count
    m1 = grouped(sums[1:2] * gain[...], width) / count
    coef = (rstd * gain[...], -(rstd * rstd) * m2, -rstd * m1)
    par_out[...] = jnp.zeros(par_out.shape, F32)
    par_out[0:1] = mean
    for i in range(3):
        par_out[1 + i : 2 + i] = coef[i]
    bias = 0.0
    left, right = [], []
    for p in range(2):
        ge = coef[0] * gp[p, 0] + coef[1] * (hid[p, 0] - mean) + coef[2]
        go = coef[0] * gp[p, 1] + coef[1] * (hid[p, 1] - mean) + coef[2]
        bias = bias + jnp.sum(ge + go, axis=0, keepdims=True)
        ge_b, go_b = ge.astype(BF16), go.astype(BF16)
        g_out[p, 0] = ge_b
        g_out[p, 1] = go_b
        left += [lanes(go_b, ge_b, later(go).astype(BF16)), lanes(sooner(ge).astype(BF16), go_b, ge_b)]
        right += [lanes(x[p, c], x[p + 1, c], x[p + 2, c]) for c in range(2)]
    grad = dot_tn(stack(*left), stack(*right))
    full = stack(bias, sum_refs[0][0:2], jnp.zeros((5, chans), F32))
    if not packed:
        grad_out[...] = grad
        small_out[...] = full
        return
    owners = keep_out.shape[1]
    chunk = chans // owners
    wide = [cbias[0:1, i * chans : (i + 1) * chans] for i in range(cbias.shape[1] // chans)]
    row_id = lax.broadcasted_iota(jnp.int32, full.shape, 0)
    small = []
    for d in range(owners):
        at = d * chunk
        mine = full if at == 0 else pltpu.roll(full, chans - at, 1)
        at = d * 2 * chunk
        row = jnp.broadcast_to(wide[at // chans], full.shape)
        if at % chans:
            row = pltpu.roll(row, chans - at % chans, 1)
        small.append(hi_lo(jnp.where(row_id == 3, row, mine))[None])
    quarters = [
        jnp.concatenate(
            [
                grad[kw * chans : (kw + 1) * chans, kh * chans : (kh + 1) * chans].reshape(owners, chunk, chans)
                for kw in range(3)
            ],
            axis=1,
        )
        for kh in range(3)
    ]
    quarters.append(jnp.concatenate([dlast[...].reshape(owners, 2 * chunk, chans), stack(*small)], axis=1))
    halve(me & 1, quarters, keep_out, send_outs)


def block_kernel(ahead, mix_top, mix, dw, dbias, block_out, done_out):
    chans, outs = dw.shape[2:]
    flat = [dw[:, k].reshape(3 * chans, outs) for k in range(3)]
    odd_before = lanes(mix_top[:, :chans], mix[0, :, :chans], mix[1, :, :chans])
    even = lanes(mix_top[:, chans : 2 * chans], mix[0, :, chans : 2 * chans], mix[1, :, chans : 2 * chans])
    odd = lanes(mix_top[:, 2 * chans :], mix[0, :, 2 * chans :], mix[1, :, 2 * chans :])
    block = dot(lanes(odd_before, even, odd), stack(*flat)) + dbias[...]
    block_out[...] = block.astype(BF16)
    done_out[...] = jnp.zeros(done_out.shape, F32)


def image_kernel(last, me_ref, par, hid, gm, gain, shift, par2, g, w, gi_out, done_out, scr):
    half = g.shape[2]
    chans = g.shape[3]
    mean, rstd = par[0:1], par[1:2]
    me = me_ref[0]
    edge = []
    for i, p, there in ((0, 0, me > 0), (1, 3, me < last)):
        keep = jnp.where(there, 1.0, 0.0)
        pair = []
        for c in range(2):
            centred = hid[i, c] - mean
            pre = centred * rstd * gain[...] + shift[...]
            sig = jax.nn.sigmoid(pre)
            gp = gm[p, c] * (sig * (1.0 + pre * (1.0 - sig)))
            pair.append(((par2[1:2] * gp + par2[2:3] * centred + par2[3:4]) * keep).astype(BF16))
        edge.append(pair)
    rows = [edge[0], [g[0, 0], g[0, 1]], [g[1, 0], g[1, 1]], edge[1]]
    tap = [lanes(w[0, k], w[1, k], w[2, k]) for k in range(3)]
    both = stack(lanes(tap[1], tap[0]), lanes(tap[2], tap[1]))
    ge = stack(*[lanes(rows[p + 2][0], rows[p + 1][0], rows[p][0]) for p in range(2)])
    go = stack(*[lanes(rows[p + 2][1], rows[p + 1][1], rows[p][1]) for p in range(2)])
    base = dot_nt(lanes(ge, go), both)
    from_odd = dot_nt(go, tap[2])
    from_even = dot_nt(ge, tap[0])
    for p in range(2):
        sl = slice(p * half, (p + 1) * half)
        scr[pl.ds(0, half, stride=2), :] = base[sl, :chans] + later(from_odd[sl]) + gm[p + 1, 0]
        scr[pl.ds(1, half, stride=2), :] = base[sl, chans:] + sooner(from_even[sl]) + gm[p + 1, 1]
        gi_out[p] = scr[...].astype(BF16)
    done_out[...] = jnp.zeros(done_out.shape, F32)


def rounded(total, on):
    n = total.shape[0] - 16
    last = total[n:]
    whole = last[0:8] + last[8:16]
    last = jnp.where(on, hi_lo(whole), last)
    return stack(total[:n], last).astype(BF16)


def early_kernel(me_ref, keep, got, own, send, done_out):
    done_out[...] = jnp.zeros(done_out.shape, F32)
    chip = me_ref[0] >> 1
    own[...] = keep[chip] + got[chip].astype(F32)
    send[...] = (keep[1 - chip] + got[1 - chip].astype(F32)).astype(BF16)


def late_kernel(me_ref, owner_ref, keep, got0, got1, e_own, e_got, own, sx, sy, sxy):
    me, side = me_ref[0], owner_ref[0] & 1
    core, chip = me & 1, me >> 1
    mine, other = me == 3, 2 * (1 - chip) + core == 3
    n = e_own.shape[2]

    def total(x, z, y):
        got = (got0, got1)[z // 2]
        return keep[x, 2 * z + y] + got[x, 2 * (z % 2) + y].astype(F32)

    for z in range(own.shape[0]):
        here, there = 2 * z + side, 2 * z + 1 - side
        for t in range(2):
            own[z, t * n : (t + 1) * n] = e_own[t, here] + e_got[t, here].astype(F32)
            sy[z, t * n : (t + 1) * n] = (e_own[t, there] + e_got[t, there].astype(F32)).astype(BF16)
        own[z, 2 * n :] = total(chip, z, side)
        sy[z, 2 * n :] = rounded(total(chip, z, 1 - side), mine)
        sx[z] = rounded(total(1 - chip, z, side), other)
        sxy[z] = rounded(total(1 - chip, z, 1 - side), other)


def pack_kernel(me_ref, owner_ref, own, gx, gy, gxy, after, out, s1, s2, s3, scr):
    z = owner_ref[0] >> 1
    n = own.shape[1] - gx.shape[1]
    scr[:, :n, :] = own[:, :n, :] + gy[:, :n, :].astype(F32)
    late = gx[...].astype(F32) + gy[:, n:, :].astype(F32) + gxy[...].astype(F32)
    scr[:, n:, :] = own[:, n:, :] + late
    out[...] = scr[z]
    for k, ref in ((1, s1), (2, s2), (3, s3)):
        ref[...] = rounded(scr[z ^ k], me_ref[0] == 3)


def sum_kernel(me_ref, own, g1, g2, g3, out, send):
    total = own[...] + g1[...].astype(F32) + g2[...].astype(F32) + g3[...].astype(F32)
    out[...] = total
    send[...] = rounded(total, me_ref[0] == 3)


def last_kernel(chunk, me_ref, q0, q1, q2, q3, down, conv, cb, ga, sh, db, scr):
    me = me_ref[0]
    for k, ref in enumerate((q0, q1, q2, q3)):
        scr[me ^ k] = ref[...].astype(F32)
    wide = 2 * chunk
    for q in range(4):
        for t in range(2):
            down[2 * q + t] = scr[q, t * wide : (t + 1) * wide, :]
    for kh in range(3):
        for kw in range(3):
            at = 2 * wide + kw * chunk
            conv[3 * kh + kw] = scr[kh, at : at + chunk, :]
    down[8] = scr[3, 2 * wide : 3 * wide, :]
    rows = scr[3, 3 * wide : 3 * wide + 8, :] + scr[3, 3 * wide + 8 :, :]
    cb[...] = rows[0:1, :chunk]
    ga[...] = rows[1:2, :chunk]
    sh[...] = rows[2:3, :chunk]
    db[...] = rows[3:4, :wide]


def across(x):
    n = lax.axis_size("rows")
    return lax.ppermute(x, "rows", [p for i in range(1, n - 1, 2) for p in ((i, i + 1), (i + 1, i))])


def swap(x, axis, k):
    return lax.ppermute(x, axis, [(i, i ^ k) for i in range(lax.axis_size(axis))])


def swap_both(x, k_rows, k_dp):
    both = ("rows", "dp")
    k = k_rows * lax.axis_size("dp") + k_dp
    return lax.ppermute(x, both, [(i, i ^ k) for i in range(lax.axis_size(both))])


def shards(images, conv_weight, conv_bias, norm_gain, norm_shift, down_weight, down_bias, cotangent):
    img, cot = images[0], cotangent[0, 0]
    rows, cols, chans = img.shape
    half, outs = cot.shape
    ranks, owners = lax.axis_size("rows"), lax.axis_size("dp")
    width = chans // GROUPS
    count = float(rows * cols * width * ranks)
    chunk, wide = chans // owners, outs // owners
    packed = ranks == 4 and owners == 8 and chunk == 16 and wide == 32
    me = lax.axis_index("rows").astype(jnp.int32).reshape(1)
    owner = lax.axis_index("dp").astype(jnp.int32).reshape(1)
    smem = pl.BlockSpec(memory_space=pltpu.SMEM)
    vmem = pl.BlockSpec(memory_space=pltpu.VMEM)
    hbm = pl.BlockSpec(memory_space=pltpu.HBM)

    def run(kernel, args, outs, scratch=(), specs=None, cost=1 << 27):
        return pl.pallas_call(
            kernel,
            in_specs=specs or [smem if a is me or a is owner else vmem for a in args],
            out_shape=[jax.ShapeDtypeStruct(s, d) for s, d in outs],
            out_specs=[vmem] * len(outs),
            scratch_shapes=list(scratch),
            compiler_params=pltpu.CompilerParams(vmem_limit_bytes=24 * MIB),
            cost_estimate=pl.CostEstimate(flops=cost, bytes_accessed=1 << 10, transcendentals=0),
        )(*args)

    def with_swaps(mine, other):
        return [mine] + [swap(other, "rows", k) for k in range(1, ranks)]

    chip_img, core_img = across(img), swap(img, "rows", 1)
    row_scr = pltpu.VMEM((cols, chans), F32)
    block_of = (2, 2, half, chans)
    tile = ((8, chans), F32)
    (ahead,) = run(first_kernel, (me,), [tile], cost=1 << 34)
    raw = (
        img,
        conv_weight,
        down_weight,
        cot,
        conv_bias.reshape(1, chans),
        norm_gain.reshape(1, chans),
        norm_shift.reshape(1, chans),
        down_bias.reshape(1, outs),
    )
    w, dw, cot, bias, gain, shift, dbias, own_x, own_gm, cbias = run(
        prep_kernel,
        (ahead, *raw),
        [(v.shape, v.dtype) for v in raw[1:]] + [(block_of, BF16), ((3, 2, half, chans), F32), ((8, outs), F32)],
        [pltpu.VMEM(img.shape, BF16), row_scr, pltpu.SemaphoreType.DMA((len(raw),))],
        [vmem] + [hbm] * len(raw),
    )
    chip_cot, core_cot = across(cot), swap(cot, "rows", 1)
    x, hid, stat = run(
        functools.partial(hidden_kernel, width),
        (me, core_img, chip_img, own_x, w, bias),
        [((4, 2, half, chans), BF16), (block_of, F32), tile],
        [row_scr],
    )
    stats = with_swaps(stat, stat)
    hid_edge, gm = run(
        edge_kernel,
        (me, core_img, chip_img, x, w, bias, core_cot, chip_cot, dw, own_gm),
        [(block_of, F32), ((4, 2, half, chans), F32)],
        [row_scr],
    )
    par, mix, gp, sums = run(
        functools.partial(norm_kernel, width, count, ranks),
        (*stats, x, hid, gm, gain, shift),
        [tile, ((2, half, 3 * chans), BF16), (block_of, F32), tile],
    )
    all_sums = with_swaps(sums, sums)
    early_shape = (2, owners, wide, chans)
    late_shape = (owners, 3 * chunk, chans)
    deep = 2 * wide + 3 * chunk

    mix_top, *down_grad = run(
        functools.partial(down_kernel, packed),
        (me, par, x, hid_edge, gain, shift, mix, cot),
        [((half, 3 * chans), BF16)]
        + (
            [((outs, chans), F32), ((2,) + early_shape, F32), ((2,) + early_shape, BF16)]
            if packed
            else [((outs, 9 * chans), F32)]
        ),
    )
    if packed:
        dlast, keep, send = down_grad
        early_own, early_send, ahead = run(
            early_kernel, (me, keep, swap(send, "rows", 1)), [(early_shape, F32), (early_shape, BF16), tile]
        )
        early_got = swap(early_send, "rows", 2)
    block, block_done = run(block_kernel, (ahead, mix_top, mix, dw, dbias), [((half, outs), BF16), tile])
    par2, g, *conv_grad = run(
        functools.partial(back_kernel, width, count, ranks, packed),
        (me, *all_sums, par, x, hid, gp, gain, block_done) + ((dlast, cbias) if packed else ()),
        [tile, (block_of, BF16)]
        + (
            [((2,) + late_shape, F32)] + [((2, owners // 2, 3 * chunk, chans), BF16)] * 2
            if packed
            else [((3 * chans, 3 * chans), F32), tile]
        ),
        cost=BACK,
    )
    gi, done = run(
        functools.partial(image_kernel, ranks - 1),
        (me, par, hid_edge, gm, gain, shift, par2, g, w),
        [((rows, cols, chans), BF16), tile],
        [row_scr],
    )
    if packed:
        keep, *sends = conv_grad
        zs = owners // 2
        late_cut, both_cut = (zs, 3 * chunk, chans), (zs, deep, chans)
        own, sx, sy, sxy = run(
            late_kernel,
            (me, owner, keep, *[swap(send, "rows", 1) for send in sends], early_own, early_got),
            [(both_cut, F32), (late_cut, BF16), (both_cut, BF16), (late_cut, BF16)],
        )
        gxy = swap_both(sxy, 2, 1)
        gx, gy = swap(sx, "rows", 2), swap(sy, "dp", 1)
        part, *sends = run(
            pack_kernel,
            (me, owner, own, gx, gy, gxy, done),
            [((deep, chans), F32)] + [((deep, chans), BF16)] * 3,
            [pltpu.VMEM(both_cut, F32)],
        )
        part, send = run(
            sum_kernel,
            (me, part, *[swap(sends[k], "dp", 2 * k + 2) for k in (1, 2, 0)]),
            [((deep, chans), F32), ((deep, chans), BF16)],
        )
        down, conv, cb, ga, sh, db = run(
            functools.partial(last_kernel, chunk),
            (me, *with_swaps(part, send)),
            [((9, wide, chans), F32), ((9, chunk, chans), F32)] + [((1, chunk), F32)] * 3 + [((1, wide), F32)],
            [pltpu.VMEM((4, deep, chans), F32)],
        )
    else:
        totals = lax.psum((down_grad[0], conv_grad[0], conv_grad[1], cbias[:1]), ("rows", "dp"))
        owner = owner[0]
        down = totals[0].reshape(outs, 9, chans).transpose(1, 0, 2)
        down = lax.dynamic_slice_in_dim(down, owner * wide, wide, 1)
        conv = totals[1].reshape(3, chans, 3, chans).transpose(2, 0, 1, 3).reshape(9, chans, chans)
        conv = lax.dynamic_slice_in_dim(conv, owner * chunk, chunk, 1)
        cb, ga, sh = lax.dynamic_slice_in_dim(totals[2], owner * chunk, chunk, 1)[:3]
        db = lax.dynamic_slice_in_dim(totals[3], owner * wide, wide, 1)
    return (
        block[None, None],
        gi[None],
        conv.reshape(3, 3, chunk, chans).transpose(0, 1, 3, 2),
        cb.reshape(-1),
        ga.reshape(-1),
        sh.reshape(-1),
        down.reshape(3, 3, wide, chans).transpose(0, 1, 3, 2),
        db.reshape(-1),
    )


def solution(mesh):
    spec = P("dp", "rows", None, None)
    in_specs = (spec, P(), P(), P(), P(), P(), P(), spec)
    last = P(None, None, None, "dp")
    out_specs = (spec, spec, last, P("dp"), P("dp"), P("dp"), last, P("dp"))
    return jax.shard_map(shards, mesh=mesh, in_specs=in_specs, out_specs=out_specs, check_vma=False)
```

```python
import functools

import jax
import jax.numpy as jnp
from jax import lax
from jax.experimental import pallas as pl
from jax.experimental.pallas import tpu as pltpu
from jax.sharding import PartitionSpec as P

GROUPS = 32
EPS = 1e-05
F32 = jnp.float32
BF16 = jnp.bfloat16
MIB = 1 << 20
BACK = 1 << 32


def dot(a, b):
    return jnp.dot(a, b, preferred_element_type=F32)


def dot_nt(a, b):
    return lax.dot_general(a, b, (((1,), (1,)), ((), ())), preferred_element_type=F32)


def dot_tn(a, b):
    return lax.dot_general(a, b, (((0,), (0,)), ((), ())), preferred_element_type=F32)


def lanes(*parts):
    return jnp.concatenate(parts, axis=1)


def stack(*parts):
    return jnp.concatenate(parts, axis=0)


def later(x):
    row = lax.broadcasted_iota(jnp.int32, x.shape, 0)
    return jnp.where(row == 0, 0.0, pltpu.roll(x, 1, 0))


def sooner(x):
    row = lax.broadcasted_iota(jnp.int32, x.shape, 0)
    return jnp.where(row == x.shape[0] - 1, 0.0, pltpu.roll(x, x.shape[0] - 1, 0))


def grouped(row, width):
    n = row.shape[1]
    a = lax.broadcasted_iota(jnp.int32, (n, n), 0) // width
    b = lax.broadcasted_iota(jnp.int32, (n, n), 1) // width
    same = jnp.where(a == b, 1.0, 0.0).astype(F32)
    wide = jnp.broadcast_to(row, (8, n))
    return jnp.dot(wide, same, precision=lax.Precision.HIGHEST, preferred_element_type=F32)[0:1]


def split(scr, row):
    half = row.shape[0] // 2
    scr[...] = row.astype(F32)
    return scr[pl.ds(0, half, stride=2), :], scr[pl.ds(1, half, stride=2), :]


def conv_weights(w):
    tap = [stack(w[0, k], w[1, k], w[2, k]) for k in range(3)]
    return stack(lanes(tap[1], tap[0]), lanes(tap[2], tap[1])), tap[0], tap[2]


def conv_rows(even, odd, weights, bias):
    both, first, last = weights
    base = dot(lanes(even, odd), both)
    chans = first.shape[1]
    from_odd = dot(odd, first)
    from_even = dot(even, last)
    return base[:, :chans] + bias, base[:, chans:] + bias, from_odd, from_even


def first_kernel(out):
    out[...] = jnp.zeros(out.shape, F32)


def prep_kernel(ahead, img, w, dw, cot, bias, gain, shift, dbias, *refs):
    outs, (x_out, gm_out, cb_out, img_v, scr, sems) = refs[:7], refs[7:]
    pairs = list(zip((img, w, dw, cot, bias, gain, shift, dbias), (img_v,) + outs))
    copies = [pltpu.make_async_copy(src, dst, sems.at[i]) for i, (src, dst) in enumerate(pairs)]
    for copy in copies:
        copy.start()
    copies[0].wait()
    for p in range(2):
        even, odd = split(scr, img_v[p])
        x_out[p, 0] = even.astype(BF16)
        x_out[p, 1] = odd.astype(BF16)
    for copy in copies[1:]:
        copy.wait()
    dw_v, cot_v = outs[1], outs[2]
    for p, kh in enumerate(range(3)):
        even, odd, late = back_taps(cot_v[...], dw_v, kh)
        gm_out[p, 0] = even
        gm_out[p, 1] = odd + sooner(late)
    cb_out[...] = jnp.broadcast_to(jnp.sum(cot_v[...].astype(F32), axis=0, keepdims=True), cb_out.shape)


def back_taps(c, dw, kh):
    chans, outs = dw.shape[2:]
    got = dot_nt(c, dw[kh].reshape(3 * chans, outs))
    return got[:, chans : 2 * chans], got[:, 2 * chans :], got[:, :chans]


def either(flag, a, b):
    return jnp.where(flag, a.astype(F32), b.astype(F32))


def hidden_kernel(width, core, chip, own, w, bias, x_out, hid_out, stat_out, scr):
    half = x_out.shape[2]
    odd_rank = (lax.axis_index("rows") & 1) == 1
    for p, row in ((0, either(odd_rank, core[1], chip[1])), (3, either(odd_rank, chip[0], core[0]))):
        even, odd = split(scr, row)
        x_out[p, 0] = even.astype(BF16)
        x_out[p, 1] = odd.astype(BF16)
    for p in range(2):
        x_out[p + 1] = own[p]
    weights = conv_weights(w)
    even = stack(*[lanes(x_out[p, 0], x_out[p + 1, 0], x_out[p + 2, 0]) for p in range(2)])
    odd = stack(*[lanes(x_out[p, 1], x_out[p + 1, 1], x_out[p + 2, 1]) for p in range(2)])
    base_e, base_o, from_odd, from_even = conv_rows(even, odd, weights, bias[...])
    total = 0.0
    for p in range(2):
        sl = slice(p * half, (p + 1) * half)
        he = base_e[sl] + later(from_odd[sl])
        ho = base_o[sl] + sooner(from_even[sl])
        hid_out[p, 0] = he
        hid_out[p, 1] = ho
        total = total + jnp.sum(he + ho, axis=0, keepdims=True)
    mean = grouped(total, width) / float(4 * half * width)
    spread = 0.0
    for p in range(2):
        for c in range(2):
            d = hid_out[p, c] - mean
            spread = spread + jnp.sum(d * d, axis=0, keepdims=True)
    stat_out[...] = jnp.zeros(stat_out.shape, F32)
    stat_out[0:1] = mean
    stat_out[1:2] = grouped(spread, width)


def edge_kernel(core, chip, x, w, bias, cot_core, cot_chip, dw, own_gm, hid_out, gm_out, scr):
    half = x.shape[2]
    odd_rank = (lax.axis_index("rows") & 1) == 1
    top = [v.astype(BF16) for v in split(scr, either(odd_rank, core[0], chip[0]))]
    low = [v.astype(BF16) for v in split(scr, either(odd_rank, chip[1], core[1]))]
    weights = conv_weights(w)
    even = stack(lanes(top[0], x[0, 0], x[1, 0]), lanes(x[2, 0], x[3, 0], low[0]))
    odd = stack(lanes(top[1], x[0, 1], x[1, 1]), lanes(x[2, 1], x[3, 1], low[1]))
    base_e, base_o, from_odd, from_even = conv_rows(even, odd, weights, bias[...])
    for p in range(2):
        sl = slice(p * half, (p + 1) * half)
        hid_out[p, 0] = base_e[sl] + later(from_odd[sl])
        hid_out[p, 1] = base_o[sl] + sooner(from_even[sl])
    above = either(odd_rank, cot_core[...], cot_chip[...]).astype(BF16)
    below = either(odd_rank, cot_chip[...], cot_core[...]).astype(BF16)
    zero = jnp.zeros((half, x.shape[3]), F32)
    for p, c, kh in ((0, above, 2), (1, None, 0), (2, below, 0), (3, below, 1)):
        even, odd, late = back_taps(c, dw, kh) if c is not None else (zero, zero, zero)
        own = own_gm[p] if p < 3 else (zero, zero)
        gm_out[p, 0] = own[0] + even
        gm_out[p, 1] = own[1] + (odd + sooner(late) if c is not None else odd)


def norm_kernel(width, count, ranks, *refs):
    stats = refs[:ranks]
    x, hid, gm, gain, shift, par_out, mix_out, gp_out, sum_out = refs[ranks:]
    half = x.shape[2]
    local = float(4 * half * width)
    mean = sum(s[0:1] for s in stats) / float(len(stats))
    spread = 0.0
    for s in stats:
        d = s[0:1] - mean
        spread = spread + (s[1:2] + local * (d * d))
    rstd = lax.rsqrt(spread / count + EPS)
    par_out[...] = jnp.zeros(par_out.shape, F32)
    par_out[0:1] = mean
    par_out[1:2] = rstd
    first = 0.0
    second = 0.0
    for p in range(2):
        mixed = []
        for c in range(2):
            normed = (hid[p, c] - mean) * rstd
            pre = normed * gain[...] + shift[...]
            sig = jax.nn.sigmoid(pre)
            mixed.append(x[p + 1, c].astype(F32) + pre * sig)
            gp = gm[p + 1, c] * (sig * (1.0 + pre * (1.0 - sig)))
            gp_out[p, c] = gp
            first = first + jnp.sum(gp * normed, axis=0, keepdims=True)
            second = second + jnp.sum(gp, axis=0, keepdims=True)
        mix_out[p] = lanes(later(mixed[1]).astype(BF16), mixed[0].astype(BF16), mixed[1].astype(BF16))
    sum_out[...] = jnp.zeros(sum_out.shape, F32)
    sum_out[0:1] = first
    sum_out[1:2] = second


def down_kernel(packed, par, x, hid, gain, shift, mix, cot, top_out, *rest):
    mean, rstd = par[0:1], par[1:2]
    chans = x.shape[3]
    inside = jnp.where(lax.axis_index("rows") > 0, 1.0, 0.0)
    mixed = []
    for c in range(2):
        pre = (hid[0, c] - mean) * rstd * gain[...] + shift[...]
        mixed.append((x[0, c].astype(F32) + pre * jax.nn.sigmoid(pre)) * inside)
    top = lanes(later(mixed[1]).astype(BF16), mixed[0].astype(BF16), mixed[1].astype(BF16))
    top_out[...] = top
    grad = dot_tn(cot[...], lanes(top, mix[0], mix[1]))
    if not packed:
        rest[0][...] = grad
        return
    last_out, keep_out, send_out = rest
    outs_chunk = keep_out.shape[3]
    taps = [grad[:, t * chans : (t + 1) * chans] for t in range(9)]
    last_out[...] = taps[8]
    for t in range(2):
        quarters = [taps[2 * q + t].reshape(-1, outs_chunk, chans) for q in range(4)]
        halve(lax.axis_index("rows") & 1, quarters, keep_out, [send_out], (t,))


def halve(core, quarters, keep_out, send_outs, at=()):
    first = core == 0
    for i in range(2):
        one, two = quarters[2 * i], quarters[2 * i + 1]
        keep_out[(i, *at)] = jnp.where(first, one, two)
        other = jnp.where(first, two, one).astype(BF16)
        size = other.shape[0] // len(send_outs)
        for j, ref in enumerate(send_outs):
            ref[(i, *at)] = other[j * size : (j + 1) * size]


def hi_lo(full):
    hi = full.astype(BF16).astype(F32)
    return jnp.concatenate([hi, full - hi], axis=-2)


def back_kernel(width, count, ranks, packed, *refs):
    sum_refs = refs[:ranks]
    par, x, hid, gp, gain, _, *refs = refs[ranks:]
    if packed:
        dlast, cbias, par_out, g_out, keep_out, *send_outs = refs
    else:
        par_out, g_out, grad_out, small_out = refs
    half = x.shape[2]
    chans = x.shape[3]
    me = lax.axis_index("rows")
    mean, rstd = par[0:1], par[1:2]
    sums = sum(s[...] for s in sum_refs)
    m2 = grouped(sums[0:1] * gain[...], width) / count
    m1 = grouped(sums[1:2] * gain[...], width) / count
    coef = (rstd * gain[...], -(rstd * rstd) * m2, -rstd * m1)
    par_out[...] = jnp.zeros(par_out.shape, F32)
    par_out[0:1] = mean
    for i in range(3):
        par_out[1 + i : 2 + i] = coef[i]
    bias = 0.0
    left, right = [], []
    for p in range(2):
        ge = coef[0] * gp[p, 0] + coef[1] * (hid[p, 0] - mean) + coef[2]
        go = coef[0] * gp[p, 1] + coef[1] * (hid[p, 1] - mean) + coef[2]
        bias = bias + jnp.sum(ge + go, axis=0, keepdims=True)
        ge_b, go_b = ge.astype(BF16), go.astype(BF16)
        g_out[p, 0] = ge_b
        g_out[p, 1] = go_b
        left += [lanes(go_b, ge_b, later(go).astype(BF16)), lanes(sooner(ge).astype(BF16), go_b, ge_b)]
        right += [lanes(x[p, c], x[p + 1, c], x[p + 2, c]) for c in range(2)]
    grad = dot_tn(stack(*left), stack(*right))
    full = stack(bias, sum_refs[0][0:2], jnp.zeros((5, chans), F32))
    if not packed:
        grad_out[...] = grad
        small_out[...] = full
        return
    owners = keep_out.shape[1]
    chunk = chans // owners
    wide = [cbias[0:1, i * chans : (i + 1) * chans] for i in range(cbias.shape[1] // chans)]
    row_id = lax.broadcasted_iota(jnp.int32, full.shape, 0)
    small = []
    for d in range(owners):
        at = d * chunk
        mine = full if at == 0 else pltpu.roll(full, chans - at, 1)
        at = d * 2 * chunk
        row = jnp.broadcast_to(wide[at // chans], full.shape)
        if at % chans:
            row = pltpu.roll(row, chans - at % chans, 1)
        small.append(hi_lo(jnp.where(row_id == 3, row, mine))[None])
    quarters = [
        jnp.concatenate(
            [
                grad[kw * chans : (kw + 1) * chans, kh * chans : (kh + 1) * chans].reshape(owners, chunk, chans)
                for kw in range(3)
            ],
            axis=1,
        )
        for kh in range(3)
    ]
    quarters.append(jnp.concatenate([dlast[...].reshape(owners, 2 * chunk, chans), stack(*small)], axis=1))
    halve(me & 1, quarters, keep_out, send_outs)


def block_kernel(ahead, mix_top, mix, dw, dbias, block_out, done_out):
    chans, outs = dw.shape[2:]
    flat = [dw[:, k].reshape(3 * chans, outs) for k in range(3)]
    odd_before = lanes(mix_top[:, :chans], mix[0, :, :chans], mix[1, :, :chans])
    even = lanes(mix_top[:, chans : 2 * chans], mix[0, :, chans : 2 * chans], mix[1, :, chans : 2 * chans])
    odd = lanes(mix_top[:, 2 * chans :], mix[0, :, 2 * chans :], mix[1, :, 2 * chans :])
    block = dot(lanes(odd_before, even, odd), stack(*flat)) + dbias[...]
    block_out[...] = block.astype(BF16)
    done_out[...] = jnp.zeros(done_out.shape, F32)


def image_kernel(last, par, hid, gm, gain, shift, par2, g, w, gi_out, done_out, scr):
    half = g.shape[2]
    chans = g.shape[3]
    mean, rstd = par[0:1], par[1:2]
    me = lax.axis_index("rows")
    edge = []
    for i, p, there in ((0, 0, me > 0), (1, 3, me < last)):
        keep = jnp.where(there, 1.0, 0.0)
        pair = []
        for c in range(2):
            centred = hid[i, c] - mean
            pre = centred * rstd * gain[...] + shift[...]
            sig = jax.nn.sigmoid(pre)
            gp = gm[p, c] * (sig * (1.0 + pre * (1.0 - sig)))
            pair.append(((par2[1:2] * gp + par2[2:3] * centred + par2[3:4]) * keep).astype(BF16))
        edge.append(pair)
    rows = [edge[0], [g[0, 0], g[0, 1]], [g[1, 0], g[1, 1]], edge[1]]
    tap = [lanes(w[0, k], w[1, k], w[2, k]) for k in range(3)]
    both = stack(lanes(tap[1], tap[0]), lanes(tap[2], tap[1]))
    ge = stack(*[lanes(rows[p + 2][0], rows[p + 1][0], rows[p][0]) for p in range(2)])
    go = stack(*[lanes(rows[p + 2][1], rows[p + 1][1], rows[p][1]) for p in range(2)])
    base = dot_nt(lanes(ge, go), both)
    from_odd = dot_nt(go, tap[2])
    from_even = dot_nt(ge, tap[0])
    for p in range(2):
        sl = slice(p * half, (p + 1) * half)
        scr[pl.ds(0, half, stride=2), :] = base[sl, :chans] + later(from_odd[sl]) + gm[p + 1, 0]
        scr[pl.ds(1, half, stride=2), :] = base[sl, chans:] + sooner(from_even[sl]) + gm[p + 1, 1]
        gi_out[p] = scr[...].astype(BF16)
    done_out[...] = jnp.zeros(done_out.shape, F32)


def rounded(total, on):
    n = total.shape[0] - 16
    last = total[n:]
    whole = last[0:8] + last[8:16]
    last = jnp.where(on, hi_lo(whole), last)
    return stack(total[:n], last).astype(BF16)


def early_kernel(keep, got, own, send, done_out):
    done_out[...] = jnp.zeros(done_out.shape, F32)
    chip = lax.axis_index("rows") >> 1
    own[...] = keep[chip] + got[chip].astype(F32)
    send[...] = (keep[1 - chip] + got[1 - chip].astype(F32)).astype(BF16)


def late_kernel( keep, got0, got1, e_own, e_got, own, sx, sy, sxy):
    me, side = lax.axis_index("rows"), lax.axis_index("dp") & 1
    core, chip = me & 1, me >> 1
    mine, other = me == 3, 2 * (1 - chip) + core == 3
    n = e_own.shape[2]

    def total(x, z, y):
        got = (got0, got1)[z // 2]
        return keep[x, 2 * z + y] + got[x, 2 * (z % 2) + y].astype(F32)

    for z in range(own.shape[0]):
        here, there = 2 * z + side, 2 * z + 1 - side
        for t in range(2):
            own[z, t * n : (t + 1) * n] = e_own[t, here] + e_got[t, here].astype(F32)
            sy[z, t * n : (t + 1) * n] = (e_own[t, there] + e_got[t, there].astype(F32)).astype(BF16)
        own[z, 2 * n :] = total(chip, z, side)
        sy[z, 2 * n :] = rounded(total(chip, z, 1 - side), mine)
        sx[z] = rounded(total(1 - chip, z, side), other)
        sxy[z] = rounded(total(1 - chip, z, 1 - side), other)


def pack_kernel( own, gx, gy, gxy, after, out, s1, s2, s3, scr):
    z = lax.axis_index("dp") >> 1
    n = own.shape[1] - gx.shape[1]
    scr[:, :n, :] = own[:, :n, :] + gy[:, :n, :].astype(F32)
    late = gx[...].astype(F32) + gy[:, n:, :].astype(F32) + gxy[...].astype(F32)
    scr[:, n:, :] = own[:, n:, :] + late
    out[...] = scr[z]
    for k, ref in ((1, s1), (2, s2), (3, s3)):
        ref[...] = rounded(scr[(z + k) & 3], lax.axis_index("rows") == 3)


def sum_kernel(own, g1, g2, g3, out, send):
    total = own[...] + g1[...].astype(F32) + g2[...].astype(F32) + g3[...].astype(F32)
    out[...] = total
    send[...] = rounded(total, lax.axis_index("rows") == 3)


def last_kernel(chunk, q0, q1, q2, q3, down, conv, cb, ga, sh, db, scr):
    me = lax.axis_index("rows")
    for k, ref in enumerate((q0, q1, q2, q3)):
        scr[me ^ k] = ref[...].astype(F32)
    wide = 2 * chunk
    for q in range(4):
        for t in range(2):
            down[2 * q + t] = scr[q, t * wide : (t + 1) * wide, :]
    for kh in range(3):
        for kw in range(3):
            at = 2 * wide + kw * chunk
            conv[3 * kh + kw] = scr[kh, at : at + chunk, :]
    down[8] = scr[3, 2 * wide : 3 * wide, :]
    rows = scr[3, 3 * wide : 3 * wide + 8, :] + scr[3, 3 * wide + 8 :, :]
    cb[...] = rows[0:1, :chunk]
    ga[...] = rows[1:2, :chunk]
    sh[...] = rows[2:3, :chunk]
    db[...] = rows[3:4, :wide]


def across(x):
    n = lax.axis_size("rows")
    return lax.ppermute(x, "rows", [p for i in range(1, n - 1, 2) for p in ((i, i + 1), (i + 1, i))])


def swap(x, axis, k):
    return lax.ppermute(x, axis, [(i, i ^ k) for i in range(lax.axis_size(axis))])


def around(x, k):
    n = lax.axis_size("dp")
    return lax.ppermute(x, "dp", [(i, (i + 2 * k) % n) for i in range(n)])


def swap_both(x, k_rows, k_dp):
    both = ("rows", "dp")
    k = k_rows * lax.axis_size("dp") + k_dp
    return lax.ppermute(x, both, [(i, i ^ k) for i in range(lax.axis_size(both))])


def shards(images, conv_weight, conv_bias, norm_gain, norm_shift, down_weight, down_bias, cotangent):
    img, cot = images[0], cotangent[0, 0]
    rows, cols, chans = img.shape
    half, outs = cot.shape
    ranks, owners = lax.axis_size("rows"), lax.axis_size("dp")
    width = chans // GROUPS
    count = float(rows * cols * width * ranks)
    chunk, wide = chans // owners, outs // owners
    packed = ranks == 4 and owners == 8 and chunk == 16 and wide == 32
    vmem = pl.BlockSpec(memory_space=pltpu.VMEM)
    hbm = pl.BlockSpec(memory_space=pltpu.HBM)

    def run(kernel, args, outs, scratch=(), specs=None, cost=1 << 27):
        return pl.pallas_call(
            kernel,
            in_specs=specs or [vmem] * len(args),
            out_shape=[jax.ShapeDtypeStruct(s, d) for s, d in outs],
            out_specs=[vmem] * len(outs),
            scratch_shapes=list(scratch),
            compiler_params=pltpu.CompilerParams(vmem_limit_bytes=24 * MIB),
            cost_estimate=pl.CostEstimate(flops=cost, bytes_accessed=1 << 10, transcendentals=0),
        )(*args)

    def with_swaps(mine, other):
        return [mine] + [swap(other, "rows", k) for k in range(1, ranks)]

    chip_img, core_img = across(img), swap(img, "rows", 1)
    row_scr = pltpu.VMEM((cols, chans), F32)
    block_of = (2, 2, half, chans)
    tile = ((8, chans), F32)
    (ahead,) = run(first_kernel, (), [tile], cost=1 << 34)
    raw = (
        img,
        conv_weight,
        down_weight,
        cot,
        conv_bias.reshape(1, chans),
        norm_gain.reshape(1, chans),
        norm_shift.reshape(1, chans),
        down_bias.reshape(1, outs),
    )
    w, dw, cot, bias, gain, shift, dbias, own_x, own_gm, cbias = run(
        prep_kernel,
        (ahead, *raw),
        [(v.shape, v.dtype) for v in raw[1:]] + [(block_of, BF16), ((3, 2, half, chans), F32), ((8, outs), F32)],
        [pltpu.VMEM(img.shape, BF16), row_scr, pltpu.SemaphoreType.DMA((len(raw),))],
        [vmem] + [hbm] * len(raw),
    )
    chip_cot, core_cot = across(cot), swap(cot, "rows", 1)
    x, hid, stat = run(
        functools.partial(hidden_kernel, width),
        (core_img, chip_img, own_x, w, bias),
        [((4, 2, half, chans), BF16), (block_of, F32), tile],
        [row_scr],
    )
    stats = with_swaps(stat, stat)
    hid_edge, gm = run(
        edge_kernel,
        (core_img, chip_img, x, w, bias, core_cot, chip_cot, dw, own_gm),
        [(block_of, F32), ((4, 2, half, chans), F32)],
        [row_scr],
    )
    par, mix, gp, sums = run(
        functools.partial(norm_kernel, width, count, ranks),
        (*stats, x, hid, gm, gain, shift),
        [tile, ((2, half, 3 * chans), BF16), (block_of, F32), tile],
    )
    all_sums = with_swaps(sums, sums)
    early_shape = (2, owners, wide, chans)
    late_shape = (owners, 3 * chunk, chans)
    deep = 2 * wide + 3 * chunk

    mix_top, *down_grad = run(
        functools.partial(down_kernel, packed),
        (par, x, hid_edge, gain, shift, mix, cot),
        [((half, 3 * chans), BF16)]
        + (
            [((outs, chans), F32), ((2,) + early_shape, F32), ((2,) + early_shape, BF16)]
            if packed
            else [((outs, 9 * chans), F32)]
        ),
    )
    if packed:
        dlast, keep, send = down_grad
        early_own, early_send, ahead = run(
            early_kernel, (keep, swap(send, "rows", 1)), [(early_shape, F32), (early_shape, BF16), tile]
        )
        early_got = swap(early_send, "rows", 2)
    block, block_done = run(block_kernel, (ahead, mix_top, mix, dw, dbias), [((half, outs), BF16), tile])
    par2, g, *conv_grad = run(
        functools.partial(back_kernel, width, count, ranks, packed),
        (*all_sums, par, x, hid, gp, gain, block_done) + ((dlast, cbias) if packed else ()),
        [tile, (block_of, BF16)]
        + (
            [((2,) + late_shape, F32)] + [((2, owners // 2, 3 * chunk, chans), BF16)] * 2
            if packed
            else [((3 * chans, 3 * chans), F32), tile]
        ),
        cost=BACK,
    )
    gi, done = run(
        functools.partial(image_kernel, ranks - 1),
        (par, hid_edge, gm, gain, shift, par2, g, w),
        [((rows, cols, chans), BF16), tile],
        [row_scr],
    )
    if packed:
        keep, *sends = conv_grad
        zs = owners // 2
        late_cut, both_cut = (zs, 3 * chunk, chans), (zs, deep, chans)
        own, sx, sy, sxy = run(
            late_kernel,
            (keep, *[swap(send, "rows", 1) for send in sends], early_own, early_got),
            [(both_cut, F32), (late_cut, BF16), (both_cut, BF16), (late_cut, BF16)],
        )
        gxy = swap_both(sxy, 2, 1)
        gx, gy = swap(sx, "rows", 2), swap(sy, "dp", 1)
        part, *sends = run(
            pack_kernel,
            (own, gx, gy, gxy, done),
            [((deep, chans), F32)] + [((deep, chans), BF16)] * 3,
            [pltpu.VMEM(both_cut, F32)],
        )
        part, send = run(
            sum_kernel,
            (part, *[around(sends[k - 1], k) for k in (1, 2, 3)]),
            [((deep, chans), F32), ((deep, chans), BF16)],
        )
        down, conv, cb, ga, sh, db = run(
            functools.partial(last_kernel, chunk),
            with_swaps(part, send),
            [((9, wide, chans), F32), ((9, chunk, chans), F32)] + [((1, chunk), F32)] * 3 + [((1, wide), F32)],
            [pltpu.VMEM((4, deep, chans), F32)],
        )
    else:
        totals = lax.psum((down_grad[0], conv_grad[0], conv_grad[1], cbias[:1]), ("rows", "dp"))
        owner = lax.axis_index("dp")
        down = totals[0].reshape(outs, 9, chans).transpose(1, 0, 2)
        down = lax.dynamic_slice_in_dim(down, owner * wide, wide, 1)
        conv = totals[1].reshape(3, chans, 3, chans).transpose(2, 0, 1, 3).reshape(9, chans, chans)
        conv = lax.dynamic_slice_in_dim(conv, owner * chunk, chunk, 1)
        cb, ga, sh = lax.dynamic_slice_in_dim(totals[2], owner * chunk, chunk, 1)[:3]
        db = lax.dynamic_slice_in_dim(totals[3], owner * wide, wide, 1)
    return (
        block[None, None],
        gi[None],
        conv.reshape(3, 3, chunk, chans).transpose(0, 1, 3, 2),
        cb.reshape(-1),
        ga.reshape(-1),
        sh.reshape(-1),
        down.reshape(3, 3, wide, chans).transpose(0, 1, 3, 2),
        db.reshape(-1),
    )


def solution(mesh):
    spec = P("dp", "rows", None, None)
    in_specs = (spec, P(), P(), P(), P(), P(), P(), spec)
    last = P(None, None, None, "dp")
    out_specs = (spec, spec, last, P("dp"), P("dp"), P("dp"), last, P("dp"))
    return jax.shard_map(shards, mesh=mesh, in_specs=in_specs, out_specs=out_specs, check_vma=False)
```

```python
import functools

import jax
import jax.numpy as jnp
from jax import lax
from jax.experimental import pallas as pl
from jax.experimental.pallas import tpu as pltpu
from jax.sharding import PartitionSpec as P

GROUPS = 32
EPS = 1e-05
F32 = jnp.float32
BF16 = jnp.bfloat16
MIB = 1 << 20
BACK = 1 << 32


def dot(a, b):
    return jnp.dot(a, b, preferred_element_type=F32)


def dot_nt(a, b):
    return lax.dot_general(a, b, (((1,), (1,)), ((), ())), preferred_element_type=F32)


def dot_tn(a, b):
    return lax.dot_general(a, b, (((0,), (0,)), ((), ())), preferred_element_type=F32)


def lanes(*parts):
    return jnp.concatenate(parts, axis=1)


def stack(*parts):
    return jnp.concatenate(parts, axis=0)


def later(x):
    row = lax.broadcasted_iota(jnp.int32, x.shape, 0)
    return jnp.where(row == 0, 0.0, pltpu.roll(x, 1, 0))


def sooner(x):
    row = lax.broadcasted_iota(jnp.int32, x.shape, 0)
    return jnp.where(row == x.shape[0] - 1, 0.0, pltpu.roll(x, x.shape[0] - 1, 0))


def grouped(row, width):
    n = row.shape[1]
    a = lax.broadcasted_iota(jnp.int32, (n, n), 0) // width
    b = lax.broadcasted_iota(jnp.int32, (n, n), 1) // width
    same = jnp.where(a == b, 1.0, 0.0).astype(F32)
    wide = jnp.broadcast_to(row, (8, n))
    return jnp.dot(wide, same, precision=lax.Precision.HIGHEST, preferred_element_type=F32)[0:1]


def split(scr, row):
    half = row.shape[0] // 2
    scr[...] = row.astype(F32)
    return scr[pl.ds(0, half, stride=2), :], scr[pl.ds(1, half, stride=2), :]


def conv_weights(w):
    tap = [stack(w[0, k], w[1, k], w[2, k]) for k in range(3)]
    return stack(lanes(tap[1], tap[0]), lanes(tap[2], tap[1])), tap[0], tap[2]


def conv_rows(even, odd, weights, bias):
    both, first, last = weights
    base = dot(lanes(even, odd), both)
    chans = first.shape[1]
    from_odd = dot(odd, first)
    from_even = dot(even, last)
    return base[:, :chans] + bias, base[:, chans:] + bias, from_odd, from_even


def first_kernel(out):
    out[...] = jnp.zeros(out.shape, F32)


def prep_kernel(ahead, img, w, dw, cot, bias, gain, shift, dbias, *refs):
    outs, (x_out, gm_out, cb_out, img_v, scr, sems) = refs[:7], refs[7:]
    pairs = list(zip((img, w, dw, cot, bias, gain, shift, dbias), (img_v,) + outs))
    copies = [pltpu.make_async_copy(src, dst, sems.at[i]) for i, (src, dst) in enumerate(pairs)]
    for copy in copies:
        copy.start()
    copies[0].wait()
    for p in range(2):
        even, odd = split(scr, img_v[p])
        x_out[p, 0] = even.astype(BF16)
        x_out[p, 1] = odd.astype(BF16)
    for copy in copies[1:]:
        copy.wait()
    dw_v, cot_v = outs[1], outs[2]
    for p, kh in enumerate(range(3)):
        even, odd, late = back_taps(cot_v[...], dw_v, kh)
        gm_out[p, 0] = even
        gm_out[p, 1] = odd + sooner(late)
    cb_out[...] = jnp.broadcast_to(jnp.sum(cot_v[...].astype(F32), axis=0, keepdims=True), cb_out.shape)


def back_taps(c, dw, kh):
    chans, outs = dw.shape[2:]
    got = dot_nt(c, dw[kh].reshape(3 * chans, outs))
    return got[:, chans : 2 * chans], got[:, 2 * chans :], got[:, :chans]


def either(flag, a, b):
    return jnp.where(flag, a.astype(F32), b.astype(F32))


def hidden_kernel(width, core, chip, own, w, bias, x_out, hid_out, stat_out, scr):
    half = x_out.shape[2]
    odd_rank = (lax.axis_index("rows") & 1) == 1
    for p, row in ((0, either(odd_rank, core[1], chip[1])), (3, either(odd_rank, chip[0], core[0]))):
        even, odd = split(scr, row)
        x_out[p, 0] = even.astype(BF16)
        x_out[p, 1] = odd.astype(BF16)
    for p in range(2):
        x_out[p + 1] = own[p]
    weights = conv_weights(w)
    even = stack(*[lanes(x_out[p, 0], x_out[p + 1, 0], x_out[p + 2, 0]) for p in range(2)])
    odd = stack(*[lanes(x_out[p, 1], x_out[p + 1, 1], x_out[p + 2, 1]) for p in range(2)])
    base_e, base_o, from_odd, from_even = conv_rows(even, odd, weights, bias[...])
    total = 0.0
    for p in range(2):
        sl = slice(p * half, (p + 1) * half)
        he = base_e[sl] + later(from_odd[sl])
        ho = base_o[sl] + sooner(from_even[sl])
        hid_out[p, 0] = he
        hid_out[p, 1] = ho
        total = total + jnp.sum(he + ho, axis=0, keepdims=True)
    mean = grouped(total, width) / float(4 * half * width)
    spread = 0.0
    for p in range(2):
        for c in range(2):
            d = hid_out[p, c] - mean
            spread = spread + jnp.sum(d * d, axis=0, keepdims=True)
    stat_out[...] = jnp.zeros(stat_out.shape, F32)
    stat_out[0:1] = mean
    stat_out[1:2] = grouped(spread, width)


def edge_kernel(core, chip, x, w, bias, cot_core, cot_chip, dw, own_gm, cbias, hid_out, gm_out, low_out, cb_out, scr):
    half = x.shape[2]
    odd_rank = (lax.axis_index("rows") & 1) == 1
    top = [v.astype(BF16) for v in split(scr, either(odd_rank, core[0], chip[0]))]
    low = [v.astype(BF16) for v in split(scr, either(odd_rank, chip[1], core[1]))]
    low_out[0] = low[0]
    low_out[1] = low[1]
    both = jnp.sum(cot_core[...].astype(F32), axis=0, keepdims=True) + cbias[0:1]
    cb_out[...] = jnp.broadcast_to(both, cb_out.shape)
    weights = conv_weights(w)
    even = stack(lanes(top[0], x[0, 0], x[1, 0]), lanes(x[2, 0], x[3, 0], low[0]))
    odd = stack(lanes(top[1], x[0, 1], x[1, 1]), lanes(x[2, 1], x[3, 1], low[1]))
    base_e, base_o, from_odd, from_even = conv_rows(even, odd, weights, bias[...])
    for p in range(2):
        sl = slice(p * half, (p + 1) * half)
        hid_out[p, 0] = base_e[sl] + later(from_odd[sl])
        hid_out[p, 1] = base_o[sl] + sooner(from_even[sl])
    above = either(odd_rank, cot_core[...], cot_chip[...]).astype(BF16)
    below = either(odd_rank, cot_chip[...], cot_core[...]).astype(BF16)
    zero = jnp.zeros((half, x.shape[3]), F32)
    for p, c, kh in ((0, above, 2), (1, None, 0), (2, below, 0), (3, below, 1)):
        even, odd, late = back_taps(c, dw, kh) if c is not None else (zero, zero, zero)
        own = own_gm[p] if p < 3 else (zero, zero)
        gm_out[p, 0] = own[0] + even
        gm_out[p, 1] = own[1] + (odd + sooner(late) if c is not None else odd)


def norm_kernel(width, count, ranks, *refs):
    stats = refs[:ranks]
    x, hid, gm, gain, shift, par_out, mix_out, gp_out, sum_out, far_out = refs[ranks:]
    half = x.shape[2]
    local = float(4 * half * width)
    mean = sum(s[0:1] for s in stats) / float(len(stats))
    spread = 0.0
    for s in stats:
        d = s[0:1] - mean
        spread = spread + (s[1:2] + local * (d * d))
    rstd = lax.rsqrt(spread / count + EPS)
    par_out[...] = jnp.zeros(par_out.shape, F32)
    par_out[0:1] = mean
    par_out[1:2] = rstd
    first = 0.0
    second = 0.0
    for p in range(2):
        mixed = []
        for c in range(2):
            normed = (hid[p, c] - mean) * rstd
            pre = normed * gain[...] + shift[...]
            sig = jax.nn.sigmoid(pre)
            mixed.append(x[p + 1, c].astype(F32) + pre * sig)
            gp = gm[p + 1, c] * (sig * (1.0 + pre * (1.0 - sig)))
            gp_out[p, c] = gp
            first = first + jnp.sum(gp * normed, axis=0, keepdims=True)
            second = second + jnp.sum(gp, axis=0, keepdims=True)
        mix_out[p] = lanes(later(mixed[1]).astype(BF16), mixed[0].astype(BF16), mixed[1].astype(BF16))
    sum_out[...] = jnp.zeros(sum_out.shape, F32)
    sum_out[0:1] = first
    sum_out[1:2] = second
    core = lax.axis_index("rows") & 1
    far_out[0] = gp_out[core]
    for c in range(2):
        far_out[1, c] = hid[core, c] - mean


def down_kernel(packed, par, x, hid, gain, shift, mix, cot, cot_core, top_out, *rest):
    mean, rstd = par[0:1], par[1:2]
    chans = x.shape[3]
    inside = jnp.where(lax.axis_index("rows") > 0, 1.0, 0.0)
    mixed = []
    for c in range(2):
        pre = (hid[0, c] - mean) * rstd * gain[...] + shift[...]
        mixed.append((x[0, c].astype(F32) + pre * jax.nn.sigmoid(pre)) * inside)
    top = lanes(later(mixed[1]).astype(BF16), mixed[0].astype(BF16), mixed[1].astype(BF16))
    top_out[...] = top
    grad = dot_tn(cot[...], lanes(top, mix[0], mix[1]))
    if not packed:
        rest[0][...] = grad
        return
    last_out, keep_out, send_out = rest
    outs_chunk = keep_out.shape[3]
    taps = [grad[:, t * chans : (t + 1) * chans] for t in range(9)]
    last_out[...] = taps[8] + dot_tn(cot_core[...], top[:, 2 * chans :])
    for t in range(2):
        quarters = [taps[2 * q + t].reshape(-1, outs_chunk, chans) for q in range(4)]
        halve(lax.axis_index("rows") & 1, quarters, keep_out, [send_out], (t,))


def halve(core, quarters, keep_out, send_outs, at=()):
    first = core == 0
    for i in range(2):
        one, two = quarters[2 * i], quarters[2 * i + 1]
        keep_out[(i, *at)] = jnp.where(first, one, two)
        other = jnp.where(first, two, one).astype(BF16)
        size = other.shape[0] // len(send_outs)
        for j, ref in enumerate(send_outs):
            ref[(i, *at)] = other[j * size : (j + 1) * size]


def hi_lo(full):
    hi = full.astype(BF16).astype(F32)
    return jnp.concatenate([hi, full - hi], axis=-2)


def gradient(coef, gp, centred):
    return coef[0] * gp + coef[1] * centred + coef[2]


def coefficients(width, count, sums, par, gain, par_out):
    rstd = par[1:2]
    m2 = grouped(sums[0:1] * gain, width) / count
    m1 = grouped(sums[1:2] * gain, width) / count
    coef = (rstd * gain, -(rstd * rstd) * m2, -rstd * m1)
    par_out[...] = jnp.zeros(par_out.shape, F32)
    par_out[0:1] = par[0:1]
    for i in range(3):
        par_out[1 + i : 2 + i] = coef[i]
    return coef


def shifted(even, odd):
    even_b, odd_b = even.astype(BF16), odd.astype(BF16)
    return lanes(odd_b, even_b, later(odd).astype(BF16)), lanes(sooner(even).astype(BF16), odd_b, even_b)


def back_kernel(width, count, ranks, *refs):
    sum_refs = refs[:ranks]
    par, x, hid, gp, gain, par_out, g_out, grad_out, small_out = refs[ranks:]
    chans = x.shape[3]
    coef = coefficients(width, count, sum(s[...] for s in sum_refs), par, gain[...], par_out)
    bias = 0.0
    left, right = [], []
    for p in range(2):
        even, odd = [gradient(coef, gp[p, c], hid[p, c] - par[0:1]) for c in range(2)]
        bias = bias + jnp.sum(even + odd, axis=0, keepdims=True)
        g_out[p, 0] = even.astype(BF16)
        g_out[p, 1] = odd.astype(BF16)
        left += shifted(even, odd)
        right += [lanes(x[p, c], x[p + 1, c], x[p + 2, c]) for c in range(2)]
    grad_out[...] = dot_tn(stack(*left), stack(*right))
    small_out[...] = stack(bias, sum_refs[0][0:2], jnp.zeros((5, chans), F32))


def chip_kernel(width, count, s0, s1, s2, s3, par, x, low, hid, gp, far, edge, gain, dlast, cbias, early, *refs):
    par_out, g_out, own, sx, sy, sxy, scr = refs
    rank = lax.axis_index("rows")
    core, chip, side = rank & 1, rank >> 1, lax.axis_index("dp") & 1
    first = core == 0
    chans = x.shape[3]
    owners = scr.shape[1]
    chunk = chans // owners
    coef = coefficients(width, count, s0[...] + s1[...] + s2[...] + s3[...], par, gain[...], par_out)
    halo = 1 - core
    rows = [[gradient(coef, gp[p, c], hid[p, c] - par[0:1]) for c in range(2)] for p in range(2)]
    rows.append([gradient(coef, edge[halo, 0, c], edge[halo, 1, c]) for c in range(2)])
    rows.append([gradient(coef, far[0, c], far[1, c]) for c in range(2)])
    for p in range(2):
        for c in range(2):
            g_out[p, c] = rows[p][c].astype(BF16)
    beside = (2 * core, 1 + 2 * core, 2 - core, 3 - 3 * core)
    level = (x.at[1], x.at[2], x.at[3], low)
    bias = 0.0
    left, right = [], []
    for (even, odd), at, same in zip(rows, beside, level):
        bias = bias + jnp.sum(even + odd, axis=0, keepdims=True)
        left += shifted(even, odd)
        right += [lanes(x[at, c], same[c]) for c in range(2)]
    grad = dot_tn(stack(*left), stack(*right))
    full = stack(bias, s0[0:2] + s1[0:2], jnp.zeros((5, chans), F32))
    wide = [cbias[0:1, i * chans : (i + 1) * chans] for i in range(cbias.shape[1] // chans)]
    row_id = lax.broadcasted_iota(jnp.int32, full.shape, 0)
    for kw in range(3):
        at = slice(kw * chunk, (kw + 1) * chunk)
        piece = grad[kw * chans : (kw + 1) * chans]
        scr[0, :, at, :] = piece[:, :chans].reshape(owners, chunk, chans)
        one = piece[:, chans:].reshape(owners, chunk, chans)
        if kw < 2:
            two = dlast[...].reshape(owners, 2 * chunk, chans)[:, at]
            scr[1, :, at, :] = jnp.where(first, one, two)
            continue
        for d in range(owners):
            start = d * chunk
            mine = full if start == 0 else pltpu.roll(full, chans - start, 1)
            start = d * 2 * chunk
            row = jnp.broadcast_to(wide[start // chans], full.shape)
            if start % chans:
                row = pltpu.roll(row, chans - start % chans, 1)
            scr[1, d, at, :] = jnp.where(first, one[d], hi_lo(jnp.where(row_id == 3, row, mine)))
    mine, other = rank == 3, 2 * (1 - chip) + core == 3
    n = early.shape[2]
    for z in range(own.shape[0]):
        here, there = 2 * z + side, 2 * z + 1 - side
        own[z] = scr[chip, here]
        sx[z] = rounded(scr[1 - chip, here], other)
        sy[z] = rounded(scr[chip, there], mine)
        sxy[z, 2 * n :] = rounded(scr[1 - chip, there], other)
        for t in range(2):
            sxy[z, t * n : (t + 1) * n] = early[t, z]


def block_kernel(mix_top, mix, dw, dbias, block_out, done_out):
    chans, outs = dw.shape[2:]
    flat = [dw[:, k].reshape(3 * chans, outs) for k in range(3)]
    odd_before = lanes(mix_top[:, :chans], mix[0, :, :chans], mix[1, :, :chans])
    even = lanes(mix_top[:, chans : 2 * chans], mix[0, :, chans : 2 * chans], mix[1, :, chans : 2 * chans])
    odd = lanes(mix_top[:, 2 * chans :], mix[0, :, 2 * chans :], mix[1, :, 2 * chans :])
    block = dot(lanes(odd_before, even, odd), stack(*flat)) + dbias[...]
    block_out[...] = block.astype(BF16)
    done_out[...] = jnp.zeros(done_out.shape, F32)


def halo_kernel(ahead, par, hid, gm, gain, shift, out):
    for i, p in ((0, 0), (1, 3)):
        for c in range(2):
            centred = hid[i, c] - par[0:1]
            pre = centred * par[1:2] * gain[...] + shift[...]
            sig = jax.nn.sigmoid(pre)
            out[i, 0, c] = gm[p, c] * (sig * (1.0 + pre * (1.0 - sig)))
            out[i, 1, c] = centred


def image_kernel(last, parts, gm, par2, g, w, gi_out, done_out, scr):
    half = g.shape[2]
    chans = g.shape[3]
    me = lax.axis_index("rows")
    coef = [par2[1 + i : 2 + i] for i in range(3)]
    edge = []
    for i, there in ((0, me > 0), (1, me < last)):
        keep = jnp.where(there, 1.0, 0.0)
        edge.append([(gradient(coef, parts[i, 0, c], parts[i, 1, c]) * keep).astype(BF16) for c in range(2)])
    rows = [edge[0], [g[0, 0], g[0, 1]], [g[1, 0], g[1, 1]], edge[1]]
    tap = [lanes(w[0, k], w[1, k], w[2, k]) for k in range(3)]
    both = stack(lanes(tap[1], tap[0]), lanes(tap[2], tap[1]))
    ge = stack(*[lanes(rows[p + 2][0], rows[p + 1][0], rows[p][0]) for p in range(2)])
    go = stack(*[lanes(rows[p + 2][1], rows[p + 1][1], rows[p][1]) for p in range(2)])
    base = dot_nt(lanes(ge, go), both)
    from_odd = dot_nt(go, tap[2])
    from_even = dot_nt(ge, tap[0])
    for p in range(2):
        sl = slice(p * half, (p + 1) * half)
        scr[pl.ds(0, half, stride=2), :] = base[sl, :chans] + later(from_odd[sl]) + gm[p + 1, 0]
        scr[pl.ds(1, half, stride=2), :] = base[sl, chans:] + sooner(from_even[sl]) + gm[p + 1, 1]
        gi_out[p] = scr[...].astype(BF16)
    done_out[...] = jnp.zeros(done_out.shape, F32)


def rounded(total, on):
    n = total.shape[0] - 16
    last = total[n:]
    whole = last[0:8] + last[8:16]
    last = jnp.where(on, hi_lo(whole), last)
    return stack(total[:n], last).astype(BF16)


def early_kernel(keep, got, own, sx, sy, sxy, done_out):
    done_out[...] = jnp.zeros(done_out.shape, F32)
    chip, side = lax.axis_index("rows") >> 1, lax.axis_index("dp") & 1
    _, zs, n, _ = own.shape
    for ref in (sx, sy):
        ref[2 * zs * n :] = jnp.zeros((ref.shape[0] - 2 * zs * n, ref.shape[1]), BF16)
    for t in range(2):
        for z in range(zs):

            def total(x, y):
                return keep[x, t, 2 * z + y] + got[x, t, 2 * z + y].astype(F32)

            own[t, z] = total(chip, side)
            sxy[t, z] = total(1 - chip, 1 - side).astype(BF16)
            at = slice((t * zs + z) * n, (t * zs + z + 1) * n)
            sx[at] = total(1 - chip, side).astype(BF16)
            sy[at] = total(chip, 1 - side).astype(BF16)


def pack_kernel(own, gx, gy, gxy, early, ex, ey, after, after_too, out, s1, s2, s3, scr):
    z = lax.axis_index("dp") >> 1
    n = early.shape[2]
    for t in range(2):
        at = slice(t * own.shape[0] * n, (t + 1) * own.shape[0] * n)
        got = (ex[at].astype(F32) + ey[at].astype(F32)).reshape(early.shape[1:])
        scr[:, t * n : (t + 1) * n, :] = early[t] + got + gxy[:, t * n : (t + 1) * n, :].astype(F32)
    late = gx[...].astype(F32) + gy[...].astype(F32) + gxy[:, 2 * n :, :].astype(F32)
    scr[:, 2 * n :, :] = own[...] + late
    out[...] = scr[z]
    for k, ref in ((1, s1), (2, s2), (3, s3)):
        ref[...] = rounded(scr[(z + k) & 3], lax.axis_index("rows") == 3)


def sum_kernel(own, g1, g2, g3, out, send):
    total = own[...] + g1[...].astype(F32) + g2[...].astype(F32) + g3[...].astype(F32)
    out[...] = total
    send[...] = rounded(total, lax.axis_index("rows") == 3)


def last_kernel(chunk, q0, q1, q2, q3, down, conv, cb, ga, sh, db, scr):
    me = lax.axis_index("rows")
    for k, ref in enumerate((q0, q1, q2, q3)):
        scr[me ^ k] = ref[...].astype(F32)
    wide = 2 * chunk
    for q in range(4):
        for t in range(2):
            down[2 * q + t] = scr[q, t * wide : (t + 1) * wide, :]
    for kh in range(3):
        for kw in range(3):
            at = 2 * wide + kw * chunk
            conv[3 * kh + kw] = scr[(0, 2, 1)[kh], at : at + chunk, :]
    down[8] = scr[3, 2 * wide : 3 * wide, :]
    rows = scr[3, 3 * wide : 3 * wide + 8, :] + scr[3, 3 * wide + 8 :, :]
    cb[...] = rows[0:1, :chunk]
    ga[...] = rows[1:2, :chunk]
    sh[...] = rows[2:3, :chunk]
    db[...] = rows[3:4, :wide]


def across(x):
    n = lax.axis_size("rows")
    return lax.ppermute(x, "rows", [p for i in range(1, n - 1, 2) for p in ((i, i + 1), (i + 1, i))])


def swap(x, axis, k):
    return lax.ppermute(x, axis, [(i, i ^ k) for i in range(lax.axis_size(axis))])


def around(x, k):
    n = lax.axis_size("dp")
    return lax.ppermute(x, "dp", [(i, (i + 2 * k) % n) for i in range(n)])


def swap_both(x, k_rows, k_dp):
    both = ("rows", "dp")
    k = k_rows * lax.axis_size("dp") + k_dp
    return lax.ppermute(x, both, [(i, i ^ k) for i in range(lax.axis_size(both))])


def swap_beside(x, y, xy):
    both = swap_both(xy, 2, 1)
    return swap(x, "rows", 2), swap(y, "dp", 1), both


def shards(images, conv_weight, conv_bias, norm_gain, norm_shift, down_weight, down_bias, cotangent):
    img, cot = images[0], cotangent[0, 0]
    rows, cols, chans = img.shape
    half, outs = cot.shape
    ranks, owners = lax.axis_size("rows"), lax.axis_size("dp")
    width = chans // GROUPS
    count = float(rows * cols * width * ranks)
    chunk, wide = chans // owners, outs // owners
    packed = ranks == 4 and owners == 8 and chunk == 16 and wide == 32
    vmem = pl.BlockSpec(memory_space=pltpu.VMEM)
    hbm = pl.BlockSpec(memory_space=pltpu.HBM)

    def run(kernel, args, outs, scratch=(), specs=None, cost=1 << 27):
        return pl.pallas_call(
            kernel,
            in_specs=specs or [vmem] * len(args),
            out_shape=[jax.ShapeDtypeStruct(s, d) for s, d in outs],
            out_specs=[vmem] * len(outs),
            scratch_shapes=list(scratch),
            compiler_params=pltpu.CompilerParams(vmem_limit_bytes=24 * MIB),
            cost_estimate=pl.CostEstimate(flops=cost, bytes_accessed=1 << 10, transcendentals=0),
        )(*args)

    def with_swaps(mine, other):
        return [mine] + [swap(other, "rows", k) for k in range(1, ranks)]

    chip_img, core_img = across(img), swap(img, "rows", 1)
    row_scr = pltpu.VMEM((cols, chans), F32)
    block_of = (2, 2, half, chans)
    tile = ((8, chans), F32)
    (ahead,) = run(first_kernel, (), [tile], cost=1 << 34)
    raw = (
        img,
        conv_weight,
        down_weight,
        cot,
        conv_bias.reshape(1, chans),
        norm_gain.reshape(1, chans),
        norm_shift.reshape(1, chans),
        down_bias.reshape(1, outs),
    )
    w, dw, cot, bias, gain, shift, dbias, own_x, own_gm, cbias = run(
        prep_kernel,
        (ahead, *raw),
        [(v.shape, v.dtype) for v in raw[1:]] + [(block_of, BF16), ((3, 2, half, chans), F32), ((8, outs), F32)],
        [pltpu.VMEM(img.shape, BF16), row_scr, pltpu.SemaphoreType.DMA((len(raw),))],
        [vmem] + [hbm] * len(raw),
    )
    chip_cot, core_cot = across(cot), swap(cot, "rows", 1)
    x, hid, stat = run(
        functools.partial(hidden_kernel, width),
        (core_img, chip_img, own_x, w, bias),
        [((4, 2, half, chans), BF16), (block_of, F32), tile],
        [row_scr],
    )
    stats = with_swaps(stat, stat)
    hid_edge, gm, low, chip_cbias = run(
        edge_kernel,
        (core_img, chip_img, x, w, bias, core_cot, chip_cot, dw, own_gm, cbias),
        [(block_of, F32), ((4, 2, half, chans), F32), (block_of[1:], BF16), ((8, outs), F32)],
        [row_scr],
    )
    par, mix, gp, sums, far = run(
        functools.partial(norm_kernel, width, count, ranks),
        (*stats, x, hid, gm, gain, shift),
        [tile, ((2, half, 3 * chans), BF16), (block_of, F32), tile, (block_of, F32)],
    )
    all_sums = with_swaps(sums, sums)
    early_shape = (2, owners, wide, chans)
    late_shape = (owners, 3 * chunk, chans)
    deep = 2 * wide + 3 * chunk

    mix_top, *down_grad = run(
        functools.partial(down_kernel, packed),
        (par, x, hid_edge, gain, shift, mix, cot, core_cot),
        [((half, 3 * chans), BF16)]
        + (
            [((outs, chans), F32), ((2,) + early_shape, F32), ((2,) + early_shape, BF16)]
            if packed
            else [((outs, 9 * chans), F32)]
        ),
    )
    if packed:
        dlast, keep, send = down_grad
        zs = owners // 2
        late_cut, early_cut = (zs, 3 * chunk, chans), (2, zs, wide, chans)
        sent = ((2 * zs * wide + zs * deep) // 2 + zs * wide, chans)
        early_own, sx, sy, early_sxy, ahead = run(
            early_kernel,
            (keep, swap(send, "rows", 1)),
            [(early_cut, F32), (sent, BF16), (sent, BF16), (early_cut, BF16), tile],
        )
        early_got = swap(sx, "rows", 2), swap(sy, "dp", 1)
    block, block_done = run(block_kernel, (mix_top, mix, dw, dbias), [((half, outs), BF16), tile])
    (edge,) = run(halo_kernel, (ahead, par, hid_edge, gm, gain, shift), [((2,) + block_of, F32)])
    if packed:
        far = swap(far, "rows", 1)
        par2, g, own, sx, sy, sxy = run(
            functools.partial(chip_kernel, width, count),
            (*all_sums, par, x, low, hid, gp, far, edge, gain, dlast, chip_cbias, early_sxy),
            [tile, (block_of, BF16), (late_cut, F32)] + [(late_cut, BF16)] * 2 + [((zs, deep, chans), BF16)],
            [pltpu.VMEM((2,) + late_shape, F32)],
            cost=BACK,
        )
    else:
        par2, g, *conv_grad = run(
            functools.partial(back_kernel, width, count, ranks),
            (*all_sums, par, x, hid, gp, gain),
            [tile, (block_of, BF16), ((3 * chans, 3 * chans), F32), tile],
        )
    gi, done = run(
        functools.partial(image_kernel, ranks - 1),
        (edge, gm, par2, g, w),
        [((rows, cols, chans), BF16), tile],
        [row_scr],
    )
    if packed:
        part, *sends = run(
            pack_kernel,
            (own, *swap_beside(sx, sy, sxy), early_own, *early_got, done, block_done),
            [((deep, chans), F32)] + [((deep, chans), BF16)] * 3,
            [pltpu.VMEM((zs, deep, chans), F32)],
        )
        part, send = run(
            sum_kernel,
            (part, *[around(sends[k - 1], k) for k in (1, 2, 3)]),
            [((deep, chans), F32), ((deep, chans), BF16)],
        )
        down, conv, cb, ga, sh, db = run(
            functools.partial(last_kernel, chunk),
            with_swaps(part, send),
            [((9, wide, chans), F32), ((9, chunk, chans), F32)] + [((1, chunk), F32)] * 3 + [((1, wide), F32)],
            [pltpu.VMEM((4, deep, chans), F32)],
        )
    else:
        totals = lax.psum((down_grad[0], conv_grad[0], conv_grad[1], cbias[:1]), ("rows", "dp"))
        owner = lax.axis_index("dp")
        down = totals[0].reshape(outs, 9, chans).transpose(1, 0, 2)
        down = lax.dynamic_slice_in_dim(down, owner * wide, wide, 1)
        conv = totals[1].reshape(3, chans, 3, chans).transpose(2, 0, 1, 3).reshape(9, chans, chans)
        conv = lax.dynamic_slice_in_dim(conv, owner * chunk, chunk, 1)
        cb, ga, sh = lax.dynamic_slice_in_dim(totals[2], owner * chunk, chunk, 1)[:3]
        db = lax.dynamic_slice_in_dim(totals[3], owner * wide, wide, 1)
    return (
        block[None, None],
        gi[None],
        conv.reshape(3, 3, chunk, chans).transpose(0, 1, 3, 2),
        cb.reshape(-1),
        ga.reshape(-1),
        sh.reshape(-1),
        down.reshape(3, 3, wide, chans).transpose(0, 1, 3, 2),
        db.reshape(-1),
    )


def solution(mesh):
    spec = P("dp", "rows", None, None)
    in_specs = (spec, P(), P(), P(), P(), P(), P(), spec)
    last = P(None, None, None, "dp")
    out_specs = (spec, spec, last, P("dp"), P("dp"), P("dp"), last, P("dp"))
    return jax.shard_map(shards, mesh=mesh, in_specs=in_specs, out_specs=out_specs, check_vma=False)
```

```python
import functools

import jax
import jax.numpy as jnp
from jax import lax
from jax.experimental import pallas as pl
from jax.experimental.pallas import tpu as pltpu
from jax.sharding import PartitionSpec as P

GROUPS = 32
EPS = 1e-05
F32 = jnp.float32
BF16 = jnp.bfloat16
MIB = 1 << 20
BACK = 1 << 32
JOIN = 1 << 29


def dot(a, b):
    return jnp.dot(a, b, preferred_element_type=F32)


def dot_nt(a, b):
    return lax.dot_general(a, b, (((1,), (1,)), ((), ())), preferred_element_type=F32)


def dot_tn(a, b):
    return lax.dot_general(a, b, (((0,), (0,)), ((), ())), preferred_element_type=F32)


def lanes(*parts):
    return jnp.concatenate(parts, axis=1)


def stack(*parts):
    return jnp.concatenate(parts, axis=0)


def later(x):
    row = lax.broadcasted_iota(jnp.int32, x.shape, 0)
    return jnp.where(row == 0, 0.0, pltpu.roll(x, 1, 0))


def sooner(x):
    row = lax.broadcasted_iota(jnp.int32, x.shape, 0)
    return jnp.where(row == x.shape[0] - 1, 0.0, pltpu.roll(x, x.shape[0] - 1, 0))


def grouped(row, width):
    n = row.shape[1]
    a = lax.broadcasted_iota(jnp.int32, (n, n), 0) // width
    b = lax.broadcasted_iota(jnp.int32, (n, n), 1) // width
    same = jnp.where(a == b, 1.0, 0.0).astype(F32)
    wide = jnp.broadcast_to(row, (8, n))
    return jnp.dot(wide, same, precision=lax.Precision.HIGHEST, preferred_element_type=F32)[0:1]


def split(scr, row):
    half = row.shape[0] // 2
    scr[...] = row.astype(F32)
    return scr[pl.ds(0, half, stride=2), :], scr[pl.ds(1, half, stride=2), :]


def conv_weights(w):
    tap = [stack(w[0, k], w[1, k], w[2, k]) for k in range(3)]
    return stack(lanes(tap[1], tap[0]), lanes(tap[2], tap[1])), tap[0], tap[2]


def conv_rows(even, odd, weights, bias):
    both, first, last = weights
    base = dot(lanes(even, odd), both)
    chans = first.shape[1]
    from_odd = dot(odd, first)
    from_even = dot(even, last)
    return base[:, :chans] + bias, base[:, chans:] + bias, from_odd, from_even


def first_kernel(out):
    out[...] = jnp.zeros(out.shape, F32)


def prep_kernel(ahead, img, w, dw, cot, bias, gain, shift, dbias, *refs):
    outs, (x_out, gm_out, cb_out, img_v, scr, sems) = refs[:7], refs[7:]
    pairs = list(zip((img, w, dw, cot, bias, gain, shift, dbias), (img_v,) + outs))
    copies = [pltpu.make_async_copy(src, dst, sems.at[i]) for i, (src, dst) in enumerate(pairs)]
    for copy in copies:
        copy.start()
    copies[0].wait()
    for p in range(2):
        even, odd = split(scr, img_v[p])
        x_out[p, 0] = even.astype(BF16)
        x_out[p, 1] = odd.astype(BF16)
    for copy in copies[1:]:
        copy.wait()
    dw_v, cot_v = outs[1], outs[2]
    for p, kh in enumerate(range(3)):
        even, odd, late = back_taps(cot_v[...], dw_v, kh)
        gm_out[p, 0] = even
        gm_out[p, 1] = odd + sooner(late)
    cb_out[...] = jnp.broadcast_to(jnp.sum(cot_v[...].astype(F32), axis=0, keepdims=True), cb_out.shape)


def back_taps(c, dw, kh):
    chans, outs = dw.shape[2:]
    got = dot_nt(c, dw[kh].reshape(3 * chans, outs))
    return got[:, chans : 2 * chans], got[:, 2 * chans :], got[:, :chans]


def either(flag, a, b):
    return jnp.where(flag, a.astype(F32), b.astype(F32))


def hidden_kernel(width, core, chip, own, w, bias, x_out, hid_out, stat_out, scr):
    half = x_out.shape[2]
    odd_rank = (lax.axis_index("rows") & 1) == 1
    for p, row in ((0, either(odd_rank, core[1], chip[1])), (3, either(odd_rank, chip[0], core[0]))):
        even, odd = split(scr, row)
        x_out[p, 0] = even.astype(BF16)
        x_out[p, 1] = odd.astype(BF16)
    for p in range(2):
        x_out[p + 1] = own[p]
    weights = conv_weights(w)
    even = stack(*[lanes(x_out[p, 0], x_out[p + 1, 0], x_out[p + 2, 0]) for p in range(2)])
    odd = stack(*[lanes(x_out[p, 1], x_out[p + 1, 1], x_out[p + 2, 1]) for p in range(2)])
    base_e, base_o, from_odd, from_even = conv_rows(even, odd, weights, bias[...])
    total = 0.0
    for p in range(2):
        sl = slice(p * half, (p + 1) * half)
        he = base_e[sl] + later(from_odd[sl])
        ho = base_o[sl] + sooner(from_even[sl])
        hid_out[p, 0] = he
        hid_out[p, 1] = ho
        total = total + jnp.sum(he + ho, axis=0, keepdims=True)
    mean = grouped(total, width) / float(4 * half * width)
    spread = 0.0
    for p in range(2):
        for c in range(2):
            d = hid_out[p, c] - mean
            spread = spread + jnp.sum(d * d, axis=0, keepdims=True)
    stat_out[...] = jnp.zeros(stat_out.shape, F32)
    stat_out[0:1] = mean
    stat_out[1:2] = grouped(spread, width)


def edge_kernel(core, chip, x, w, bias, cot_core, cot_chip, dw, own_gm, cbias, hid_out, gm_out, low_out, cb_out, scr):
    half = x.shape[2]
    odd_rank = (lax.axis_index("rows") & 1) == 1
    top = [v.astype(BF16) for v in split(scr, either(odd_rank, core[0], chip[0]))]
    low = [v.astype(BF16) for v in split(scr, either(odd_rank, chip[1], core[1]))]
    low_out[0] = low[0]
    low_out[1] = low[1]
    both = jnp.sum(cot_core[...].astype(F32), axis=0, keepdims=True) + cbias[0:1]
    cb_out[...] = jnp.broadcast_to(both, cb_out.shape)
    weights = conv_weights(w)
    even = stack(lanes(top[0], x[0, 0], x[1, 0]), lanes(x[2, 0], x[3, 0], low[0]))
    odd = stack(lanes(top[1], x[0, 1], x[1, 1]), lanes(x[2, 1], x[3, 1], low[1]))
    base_e, base_o, from_odd, from_even = conv_rows(even, odd, weights, bias[...])
    for p in range(2):
        sl = slice(p * half, (p + 1) * half)
        hid_out[p, 0] = base_e[sl] + later(from_odd[sl])
        hid_out[p, 1] = base_o[sl] + sooner(from_even[sl])
    above = either(odd_rank, cot_core[...], cot_chip[...]).astype(BF16)
    below = either(odd_rank, cot_chip[...], cot_core[...]).astype(BF16)
    zero = jnp.zeros((half, x.shape[3]), F32)
    for p, c, kh in ((0, above, 2), (1, None, 0), (2, below, 0), (3, below, 1)):
        even, odd, late = back_taps(c, dw, kh) if c is not None else (zero, zero, zero)
        own = own_gm[p] if p < 3 else (zero, zero)
        gm_out[p, 0] = own[0] + even
        gm_out[p, 1] = own[1] + (odd + sooner(late) if c is not None else odd)


def norm_kernel(width, count, ranks, *refs):
    stats = refs[:ranks]
    x, hid, gm, gain, shift, par_out, mix_out, gp_out, sum_out, far_out = refs[ranks:]
    half = x.shape[2]
    local = float(4 * half * width)
    mean = sum(s[0:1] for s in stats) / float(len(stats))
    spread = 0.0
    for s in stats:
        d = s[0:1] - mean
        spread = spread + (s[1:2] + local * (d * d))
    rstd = lax.rsqrt(spread / count + EPS)
    par_out[...] = jnp.zeros(par_out.shape, F32)
    par_out[0:1] = mean
    par_out[1:2] = rstd
    first = 0.0
    second = 0.0
    for p in range(2):
        mixed = []
        for c in range(2):
            normed = (hid[p, c] - mean) * rstd
            pre = normed * gain[...] + shift[...]
            sig = jax.nn.sigmoid(pre)
            mixed.append(x[p + 1, c].astype(F32) + pre * sig)
            gp = gm[p + 1, c] * (sig * (1.0 + pre * (1.0 - sig)))
            gp_out[p, c] = gp
            first = first + jnp.sum(gp * normed, axis=0, keepdims=True)
            second = second + jnp.sum(gp, axis=0, keepdims=True)
        mix_out[p] = lanes(later(mixed[1]).astype(BF16), mixed[0].astype(BF16), mixed[1].astype(BF16))
    sum_out[...] = jnp.zeros(sum_out.shape, F32)
    sum_out[0:1] = first
    sum_out[1:2] = second
    core = lax.axis_index("rows") & 1
    far_out[0] = gp_out[core]
    for c in range(2):
        far_out[1, c] = hid[core, c] - mean


def down_kernel(packed, par, x, hid, gain, shift, mix, cot, cot_core, top_out, *rest):
    mean, rstd = par[0:1], par[1:2]
    chans = x.shape[3]
    inside = jnp.where(lax.axis_index("rows") > 0, 1.0, 0.0)
    mixed = []
    for c in range(2):
        pre = (hid[0, c] - mean) * rstd * gain[...] + shift[...]
        mixed.append((x[0, c].astype(F32) + pre * jax.nn.sigmoid(pre)) * inside)
    top = lanes(later(mixed[1]).astype(BF16), mixed[0].astype(BF16), mixed[1].astype(BF16))
    top_out[...] = top
    grad = dot_tn(cot[...], lanes(top, mix[0], mix[1]))
    if not packed:
        rest[0][...] = grad
        return
    last_out, keep_out, send_out = rest
    outs_chunk = keep_out.shape[3]
    taps = [grad[:, t * chans : (t + 1) * chans] for t in range(9)]
    last_out[...] = taps[8] + dot_tn(cot_core[...], top[:, 2 * chans :])
    for t in range(2):
        quarters = [taps[2 * q + t].reshape(-1, outs_chunk, chans) for q in range(4)]
        halve(lax.axis_index("rows") & 1, quarters, keep_out, [send_out], (t,))


def halve(core, quarters, keep_out, send_outs, at=()):
    first = core == 0
    for i in range(2):
        one, two = quarters[2 * i], quarters[2 * i + 1]
        keep_out[(i, *at)] = jnp.where(first, one, two)
        other = jnp.where(first, two, one).astype(BF16)
        size = other.shape[0] // len(send_outs)
        for j, ref in enumerate(send_outs):
            ref[(i, *at)] = other[j * size : (j + 1) * size]


def hi_lo(full):
    hi = full.astype(BF16).astype(F32)
    return jnp.concatenate([hi, full - hi], axis=-2)


def gradient(coef, gp, centred):
    return coef[0] * gp + coef[1] * centred + coef[2]


def coefficients(width, count, sums, par, gain, par_out):
    rstd = par[1:2]
    m2 = grouped(sums[0:1] * gain, width) / count
    m1 = grouped(sums[1:2] * gain, width) / count
    coef = (rstd * gain, -(rstd * rstd) * m2, -rstd * m1)
    par_out[...] = jnp.zeros(par_out.shape, F32)
    par_out[0:1] = par[0:1]
    for i in range(3):
        par_out[1 + i : 2 + i] = coef[i]
    return coef


def shifted(even, odd):
    even_b, odd_b = even.astype(BF16), odd.astype(BF16)
    return lanes(odd_b, even_b, later(odd).astype(BF16)), lanes(sooner(even).astype(BF16), odd_b, even_b)


def back_kernel(width, count, ranks, *refs):
    sum_refs = refs[:ranks]
    par, x, hid, gp, gain, par_out, g_out, grad_out, small_out = refs[ranks:]
    chans = x.shape[3]
    coef = coefficients(width, count, sum(s[...] for s in sum_refs), par, gain[...], par_out)
    bias = 0.0
    left, right = [], []
    for p in range(2):
        even, odd = [gradient(coef, gp[p, c], hid[p, c] - par[0:1]) for c in range(2)]
        bias = bias + jnp.sum(even + odd, axis=0, keepdims=True)
        g_out[p, 0] = even.astype(BF16)
        g_out[p, 1] = odd.astype(BF16)
        left += shifted(even, odd)
        right += [lanes(x[p, c], x[p + 1, c], x[p + 2, c]) for c in range(2)]
    grad_out[...] = dot_tn(stack(*left), stack(*right))
    small_out[...] = stack(bias, sum_refs[0][0:2], jnp.zeros((5, chans), F32))


def chip_kernel(width, count, s0, s1, s2, s3, par, x, low, hid, gp, far, edge, gain, dlast, cbias, early, *refs):
    par_out, g_out, own, sx, sy, sxy, scr = refs
    rank = lax.axis_index("rows")
    core, chip, side = rank & 1, rank >> 1, lax.axis_index("dp") & 1
    first = core == 0
    chans = x.shape[3]
    owners = scr.shape[1]
    chunk = chans // owners
    coef = coefficients(width, count, s0[...] + s1[...] + s2[...] + s3[...], par, gain[...], par_out)
    halo = 1 - core
    rows = [[gradient(coef, gp[p, c], hid[p, c] - par[0:1]) for c in range(2)] for p in range(2)]
    rows.append([gradient(coef, edge[halo, 0, c], edge[halo, 1, c]) for c in range(2)])
    rows.append([gradient(coef, far[0, c], far[1, c]) for c in range(2)])
    for p in range(2):
        for c in range(2):
            g_out[p, c] = rows[p][c].astype(BF16)
    beside = (2 * core, 1 + 2 * core, 2 - core, 3 - 3 * core)
    level = (x.at[1], x.at[2], x.at[3], low)
    bias = 0.0
    left, right = [], []
    for (even, odd), at, same in zip(rows, beside, level):
        bias = bias + jnp.sum(even + odd, axis=0, keepdims=True)
        left += shifted(even, odd)
        right += [lanes(x[at, c], same[c]) for c in range(2)]
    grad = dot_tn(stack(*left), stack(*right))
    full = stack(bias, s0[0:2] + s1[0:2], jnp.zeros((5, chans), F32))
    wide = [cbias[0:1, i * chans : (i + 1) * chans] for i in range(cbias.shape[1] // chans)]
    row_id = lax.broadcasted_iota(jnp.int32, full.shape, 0)
    for kw in range(3):
        at = slice(kw * chunk, (kw + 1) * chunk)
        piece = grad[kw * chans : (kw + 1) * chans]
        scr[0, :, at, :] = piece[:, :chans].reshape(owners, chunk, chans)
        one = piece[:, chans:].reshape(owners, chunk, chans)
        if kw < 2:
            two = dlast[...].reshape(owners, 2 * chunk, chans)[:, at]
            scr[1, :, at, :] = jnp.where(first, one, two)
            continue
        for d in range(owners):
            start = d * chunk
            mine = full if start == 0 else pltpu.roll(full, chans - start, 1)
            start = d * 2 * chunk
            row = jnp.broadcast_to(wide[start // chans], full.shape)
            if start % chans:
                row = pltpu.roll(row, chans - start % chans, 1)
            scr[1, d, at, :] = jnp.where(first, one[d], hi_lo(jnp.where(row_id == 3, row, mine)))
    mine, other = rank == 3, 2 * (1 - chip) + core == 3
    n = early.shape[2]
    for z in range(own.shape[0]):
        here, there = 2 * z + side, 2 * z + 1 - side
        own[z] = scr[chip, here]
        sx[z] = rounded(scr[1 - chip, here], other)
        sy[z] = rounded(scr[chip, there], mine)
        sxy[z, 2 * n :] = rounded(scr[1 - chip, there], other)
        for t in range(2):
            sxy[z, t * n : (t + 1) * n] = early[t, z]


def block_kernel(ahead, mix_top, mix, dw, dbias, block_out, done_out):
    chans, outs = dw.shape[2:]
    flat = [dw[:, k].reshape(3 * chans, outs) for k in range(3)]
    odd_before = lanes(mix_top[:, :chans], mix[0, :, :chans], mix[1, :, :chans])
    even = lanes(mix_top[:, chans : 2 * chans], mix[0, :, chans : 2 * chans], mix[1, :, chans : 2 * chans])
    odd = lanes(mix_top[:, 2 * chans :], mix[0, :, 2 * chans :], mix[1, :, 2 * chans :])
    block = dot(lanes(odd_before, even, odd), stack(*flat)) + dbias[...]
    block_out[...] = block.astype(BF16)
    done_out[...] = jnp.zeros(done_out.shape, F32)


def halo_kernel(ahead, par, hid, gm, gain, shift, out):
    for i, p in ((0, 0), (1, 3)):
        for c in range(2):
            centred = hid[i, c] - par[0:1]
            pre = centred * par[1:2] * gain[...] + shift[...]
            sig = jax.nn.sigmoid(pre)
            out[i, 0, c] = gm[p, c] * (sig * (1.0 + pre * (1.0 - sig)))
            out[i, 1, c] = centred


def image_kernel(last, parts, gm, par2, g, w, gi_out, done_out, scr):
    half = g.shape[2]
    chans = g.shape[3]
    me = lax.axis_index("rows")
    coef = [par2[1 + i : 2 + i] for i in range(3)]
    edge = []
    for i, there in ((0, me > 0), (1, me < last)):
        keep = jnp.where(there, 1.0, 0.0)
        edge.append([(gradient(coef, parts[i, 0, c], parts[i, 1, c]) * keep).astype(BF16) for c in range(2)])
    rows = [edge[0], [g[0, 0], g[0, 1]], [g[1, 0], g[1, 1]], edge[1]]
    tap = [lanes(w[0, k], w[1, k], w[2, k]) for k in range(3)]
    both = stack(lanes(tap[1], tap[0]), lanes(tap[2], tap[1]))
    ge = stack(*[lanes(rows[p + 2][0], rows[p + 1][0], rows[p][0]) for p in range(2)])
    go = stack(*[lanes(rows[p + 2][1], rows[p + 1][1], rows[p][1]) for p in range(2)])
    base = dot_nt(lanes(ge, go), both)
    from_odd = dot_nt(go, tap[2])
    from_even = dot_nt(ge, tap[0])
    for p in range(2):
        sl = slice(p * half, (p + 1) * half)
        scr[pl.ds(0, half, stride=2), :] = base[sl, :chans] + later(from_odd[sl]) + gm[p + 1, 0]
        scr[pl.ds(1, half, stride=2), :] = base[sl, chans:] + sooner(from_even[sl]) + gm[p + 1, 1]
        gi_out[p] = scr[...].astype(BF16)
    done_out[...] = jnp.zeros(done_out.shape, F32)


def rounded(total, on):
    n = total.shape[0] - 16
    last = total[n:]
    whole = last[0:8] + last[8:16]
    last = jnp.where(on, hi_lo(whole), last)
    return stack(total[:n], last).astype(BF16)


def early_kernel(keep, got, own, sx, sy, sxy, done_out):
    done_out[...] = jnp.zeros(done_out.shape, F32)
    chip, side = lax.axis_index("rows") >> 1, lax.axis_index("dp") & 1
    _, zs, n, _ = own.shape
    for t in range(2):
        for z in range(zs):

            def total(x, y):
                return keep[x, t, 2 * z + y] + got[x, t, 2 * z + y].astype(F32)

            own[t, z] = total(chip, side)
            sxy[t, z] = total(1 - chip, 1 - side).astype(BF16)
            sx[t, z] = total(1 - chip, side).astype(BF16)
            sy[t, z] = total(chip, 1 - side).astype(BF16)


def join_kernel(early, ex, ey, out):
    out[...] = early[...] + ex[...].astype(F32) + ey[...].astype(F32)


def pack_kernel(own, gx, gy, gxy, early, after, after_too, out, s1, s2, s3, scr):
    z = lax.axis_index("dp") >> 1
    n = early.shape[2]
    for t in range(2):
        scr[:, t * n : (t + 1) * n, :] = early[t] + gxy[:, t * n : (t + 1) * n, :].astype(F32)
    late = gx[...].astype(F32) + gy[...].astype(F32) + gxy[:, 2 * n :, :].astype(F32)
    scr[:, 2 * n :, :] = own[...] + late
    out[...] = scr[z]
    for k, ref in ((1, s1), (2, s2), (3, s3)):
        ref[...] = rounded(scr[(z + k) & 3], lax.axis_index("rows") == 3)


def sum_kernel(own, g1, g2, g3, out, send):
    total = own[...] + g1[...].astype(F32) + g2[...].astype(F32) + g3[...].astype(F32)
    out[...] = total
    send[...] = rounded(total, lax.axis_index("rows") == 3)


def last_kernel(chunk, q0, q1, q2, q3, down, conv, cb, ga, sh, db, scr):
    me = lax.axis_index("rows")
    for k, ref in enumerate((q0, q1, q2, q3)):
        scr[me ^ k] = ref[...].astype(F32)
    wide = 2 * chunk
    for q in range(4):
        for t in range(2):
            down[2 * q + t] = scr[q, t * wide : (t + 1) * wide, :]
    for kh in range(3):
        for kw in range(3):
            at = 2 * wide + kw * chunk
            conv[3 * kh + kw] = scr[(0, 2, 1)[kh], at : at + chunk, :]
    down[8] = scr[3, 2 * wide : 3 * wide, :]
    rows = scr[3, 3 * wide : 3 * wide + 8, :] + scr[3, 3 * wide + 8 :, :]
    cb[...] = rows[0:1, :chunk]
    ga[...] = rows[1:2, :chunk]
    sh[...] = rows[2:3, :chunk]
    db[...] = rows[3:4, :wide]


def across(x):
    n = lax.axis_size("rows")
    return lax.ppermute(x, "rows", [p for i in range(1, n - 1, 2) for p in ((i, i + 1), (i + 1, i))])


def swap(x, axis, k):
    return lax.ppermute(x, axis, [(i, i ^ k) for i in range(lax.axis_size(axis))])


def around(x, k):
    n = lax.axis_size("dp")
    return lax.ppermute(x, "dp", [(i, (i + 2 * k) % n) for i in range(n)])


def swap_both(x, k_rows, k_dp):
    both = ("rows", "dp")
    k = k_rows * lax.axis_size("dp") + k_dp
    return lax.ppermute(x, both, [(i, i ^ k) for i in range(lax.axis_size(both))])


def swap_beside(x, y, xy):
    both = swap_both(xy, 2, 1)
    return swap(x, "rows", 2), swap(y, "dp", 1), both


def shards(images, conv_weight, conv_bias, norm_gain, norm_shift, down_weight, down_bias, cotangent):
    img, cot = images[0], cotangent[0, 0]
    rows, cols, chans = img.shape
    half, outs = cot.shape
    ranks, owners = lax.axis_size("rows"), lax.axis_size("dp")
    width = chans // GROUPS
    count = float(rows * cols * width * ranks)
    chunk, wide = chans // owners, outs // owners
    packed = ranks == 4 and owners == 8 and chunk == 16 and wide == 32
    vmem = pl.BlockSpec(memory_space=pltpu.VMEM)
    hbm = pl.BlockSpec(memory_space=pltpu.HBM)

    def run(kernel, args, outs, scratch=(), specs=None, cost=1 << 27):
        return pl.pallas_call(
            kernel,
            in_specs=specs or [vmem] * len(args),
            out_shape=[jax.ShapeDtypeStruct(s, d) for s, d in outs],
            out_specs=[vmem] * len(outs),
            scratch_shapes=list(scratch),
            compiler_params=pltpu.CompilerParams(vmem_limit_bytes=24 * MIB),
            cost_estimate=pl.CostEstimate(flops=cost, bytes_accessed=1 << 10, transcendentals=0),
        )(*args)

    def with_swaps(mine, other):
        return [mine] + [swap(other, "rows", k) for k in range(1, ranks)]

    chip_img, core_img = across(img), swap(img, "rows", 1)
    row_scr = pltpu.VMEM((cols, chans), F32)
    block_of = (2, 2, half, chans)
    tile = ((8, chans), F32)
    (ahead,) = run(first_kernel, (), [tile], cost=1 << 34)
    raw = (
        img,
        conv_weight,
        down_weight,
        cot,
        conv_bias.reshape(1, chans),
        norm_gain.reshape(1, chans),
        norm_shift.reshape(1, chans),
        down_bias.reshape(1, outs),
    )
    w, dw, cot, bias, gain, shift, dbias, own_x, own_gm, cbias = run(
        prep_kernel,
        (ahead, *raw),
        [(v.shape, v.dtype) for v in raw[1:]] + [(block_of, BF16), ((3, 2, half, chans), F32), ((8, outs), F32)],
        [pltpu.VMEM(img.shape, BF16), row_scr, pltpu.SemaphoreType.DMA((len(raw),))],
        [vmem] + [hbm] * len(raw),
    )
    chip_cot, core_cot = across(cot), swap(cot, "rows", 1)
    x, hid, stat = run(
        functools.partial(hidden_kernel, width),
        (core_img, chip_img, own_x, w, bias),
        [((4, 2, half, chans), BF16), (block_of, F32), tile],
        [row_scr],
    )
    stats = with_swaps(stat, stat)
    hid_edge, gm, low, chip_cbias = run(
        edge_kernel,
        (core_img, chip_img, x, w, bias, core_cot, chip_cot, dw, own_gm, cbias),
        [(block_of, F32), ((4, 2, half, chans), F32), (block_of[1:], BF16), ((8, outs), F32)],
        [row_scr],
    )
    par, mix, gp, sums, far = run(
        functools.partial(norm_kernel, width, count, ranks),
        (*stats, x, hid, gm, gain, shift),
        [tile, ((2, half, 3 * chans), BF16), (block_of, F32), tile, (block_of, F32)],
    )
    all_sums = with_swaps(sums, sums)
    early_shape = (2, owners, wide, chans)
    late_shape = (owners, 3 * chunk, chans)
    deep = 2 * wide + 3 * chunk

    mix_top, *down_grad = run(
        functools.partial(down_kernel, packed),
        (par, x, hid_edge, gain, shift, mix, cot, core_cot),
        [((half, 3 * chans), BF16)]
        + (
            [((outs, chans), F32), ((2,) + early_shape, F32), ((2,) + early_shape, BF16)]
            if packed
            else [((outs, 9 * chans), F32)]
        ),
    )
    if packed:
        dlast, keep, send = down_grad
        zs = owners // 2
        late_cut, early_cut = (zs, 3 * chunk, chans), (2, zs, wide, chans)
        early_own, sx, sy, early_sxy, ahead = run(
            early_kernel,
            (keep, swap(send, "rows", 1)),
            [(early_cut, F32)] + [(early_cut, BF16)] * 3 + [tile],
        )
        (early,) = run(
            join_kernel, (early_own, swap(sx, "rows", 2), swap(sy, "dp", 1)), [(early_cut, F32)], cost=JOIN
        )
    (edge,) = run(halo_kernel, (ahead, par, hid_edge, gm, gain, shift), [((2,) + block_of, F32)])
    if packed:
        far = swap(far, "rows", 1)
        par2, g, own, sx, sy, sxy = run(
            functools.partial(chip_kernel, width, count),
            (*all_sums, par, x, low, hid, gp, far, edge, gain, dlast, chip_cbias, early_sxy),
            [tile, (block_of, BF16), (late_cut, F32)] + [(late_cut, BF16)] * 2 + [((zs, deep, chans), BF16)],
            [pltpu.VMEM((2,) + late_shape, F32)],
            cost=BACK,
        )
    else:
        par2, g, *conv_grad = run(
            functools.partial(back_kernel, width, count, ranks),
            (*all_sums, par, x, hid, gp, gain),
            [tile, (block_of, BF16), ((3 * chans, 3 * chans), F32), tile],
        )
    block, block_done = run(block_kernel, (par2, mix_top, mix, dw, dbias), [((half, outs), BF16), tile])
    gi, done = run(
        functools.partial(image_kernel, ranks - 1),
        (edge, gm, par2, g, w),
        [((rows, cols, chans), BF16), tile],
        [row_scr],
    )
    if packed:
        part, *sends = run(
            pack_kernel,
            (own, *swap_beside(sx, sy, sxy), early, done, block_done),
            [((deep, chans), F32)] + [((deep, chans), BF16)] * 3,
            [pltpu.VMEM((zs, deep, chans), F32)],
        )
        part, send = run(
            sum_kernel,
            (part, *[around(sends[k - 1], k) for k in (1, 2, 3)]),
            [((deep, chans), F32), ((deep, chans), BF16)],
        )
        down, conv, cb, ga, sh, db = run(
            functools.partial(last_kernel, chunk),
            with_swaps(part, send),
            [((9, wide, chans), F32), ((9, chunk, chans), F32)] + [((1, chunk), F32)] * 3 + [((1, wide), F32)],
            [pltpu.VMEM((4, deep, chans), F32)],
        )
    else:
        totals = lax.psum((down_grad[0], conv_grad[0], conv_grad[1], cbias[:1]), ("rows", "dp"))
        owner = lax.axis_index("dp")
        down = totals[0].reshape(outs, 9, chans).transpose(1, 0, 2)
        down = lax.dynamic_slice_in_dim(down, owner * wide, wide, 1)
        conv = totals[1].reshape(3, chans, 3, chans).transpose(2, 0, 1, 3).reshape(9, chans, chans)
        conv = lax.dynamic_slice_in_dim(conv, owner * chunk, chunk, 1)
        cb, ga, sh = lax.dynamic_slice_in_dim(totals[2], owner * chunk, chunk, 1)[:3]
        db = lax.dynamic_slice_in_dim(totals[3], owner * wide, wide, 1)
    return (
        block[None, None],
        gi[None],
        conv.reshape(3, 3, chunk, chans).transpose(0, 1, 3, 2),
        cb.reshape(-1),
        ga.reshape(-1),
        sh.reshape(-1),
        down.reshape(3, 3, wide, chans).transpose(0, 1, 3, 2),
        db.reshape(-1),
    )


def solution(mesh):
    spec = P("dp", "rows", None, None)
    in_specs = (spec, P(), P(), P(), P(), P(), P(), spec)
    last = P(None, None, None, "dp")
    out_specs = (spec, spec, last, P("dp"), P("dp"), P("dp"), last, P("dp"))
    return jax.shard_map(shards, mesh=mesh, in_specs=in_specs, out_specs=out_specs, check_vma=False)
```

```python
import functools

import jax
import jax.numpy as jnp
from jax import lax
from jax.experimental import pallas as pl
from jax.experimental.pallas import tpu as pltpu
from jax.sharding import PartitionSpec as P

GROUPS = 32
EPS = 1e-05
F32 = jnp.float32
BF16 = jnp.bfloat16
MIB = 1 << 20
BACK = 1 << 32
JOIN = 1 << 29


def dot(a, b):
    return jnp.dot(a, b, preferred_element_type=F32)


def dot_nt(a, b):
    return lax.dot_general(a, b, (((1,), (1,)), ((), ())), preferred_element_type=F32)


def dot_tn(a, b):
    return lax.dot_general(a, b, (((0,), (0,)), ((), ())), preferred_element_type=F32)


def lanes(*parts):
    return jnp.concatenate(parts, axis=1)


def stack(*parts):
    return jnp.concatenate(parts, axis=0)


def later(x):
    row = lax.broadcasted_iota(jnp.int32, x.shape, 0)
    return jnp.where(row == 0, 0.0, pltpu.roll(x, 1, 0))


def sooner(x):
    row = lax.broadcasted_iota(jnp.int32, x.shape, 0)
    return jnp.where(row == x.shape[0] - 1, 0.0, pltpu.roll(x, x.shape[0] - 1, 0))


def grouped(row, width):
    n = row.shape[1]
    a = lax.broadcasted_iota(jnp.int32, (n, n), 0) // width
    b = lax.broadcasted_iota(jnp.int32, (n, n), 1) // width
    same = jnp.where(a == b, 1.0, 0.0).astype(F32)
    wide = jnp.broadcast_to(row, (8, n))
    return jnp.dot(wide, same, precision=lax.Precision.HIGHEST, preferred_element_type=F32)[0:1]


def split(scr, row):
    half = row.shape[0] // 2
    scr[...] = row.astype(F32)
    return scr[pl.ds(0, half, stride=2), :], scr[pl.ds(1, half, stride=2), :]


def conv_weights(w):
    tap = [stack(w[0, k], w[1, k], w[2, k]) for k in range(3)]
    return stack(lanes(tap[1], tap[0]), lanes(tap[2], tap[1])), tap[0], tap[2]


def conv_rows(even, odd, weights, bias):
    both, first, last = weights
    base = dot(lanes(even, odd), both)
    chans = first.shape[1]
    from_odd = dot(odd, first)
    from_even = dot(even, last)
    return base[:, :chans] + bias, base[:, chans:] + bias, from_odd, from_even


def conv_sum(rows, w):
    even, odd = lanes(*[r[0] for r in rows]), lanes(*[r[1] for r in rows])
    taps = [stack(*[w[r[2], k] for r in rows]) for k in range(3)]
    base = dot(lanes(even, odd), stack(lanes(taps[1], taps[0]), lanes(taps[2], taps[1])))
    chans = base.shape[1] // 2
    return base[:, :chans] + later(dot(odd, taps[0])), base[:, chans:] + sooner(dot(even, taps[2]))


def first_kernel(out):
    out[...] = jnp.zeros(out.shape, F32)


def prep_kernel(ahead, img, w, dw, cot, bias, gain, shift, dbias, *refs):
    outs, (x_out, part_out, gm_out, cb_out, img_v, scr, sems) = refs[:7], refs[7:]
    pairs = list(zip((img, w, dw, cot, bias, gain, shift, dbias), (img_v,) + outs))
    copies = [pltpu.make_async_copy(src, dst, sems.at[i]) for i, (src, dst) in enumerate(pairs)]
    for copy in copies:
        copy.start()
    copies[0].wait()
    for p in range(2):
        even, odd = split(scr, img_v[p])
        x_out[p, 0] = even.astype(BF16)
        x_out[p, 1] = odd.astype(BF16)
    for copy in copies[1:]:
        copy.wait()
    w_v, dw_v, cot_v, bias_v = outs[:4]
    own = [(x_out[p, 0], x_out[p, 1]) for p in range(2)]
    for p in range(2):
        he, ho = conv_sum([(*own[0], 1 - p), (*own[1], 2 - p)], w_v)
        part_out[p, 0] = he + bias_v[...]
        part_out[p, 1] = ho + bias_v[...]
    for p, kh in enumerate(range(3)):
        even, odd, late = back_taps(cot_v[...], dw_v, kh)
        gm_out[p, 0] = even
        gm_out[p, 1] = odd + sooner(late)
    cb_out[...] = jnp.broadcast_to(jnp.sum(cot_v[...].astype(F32), axis=0, keepdims=True), cb_out.shape)


def back_taps(c, dw, kh):
    chans, outs = dw.shape[2:]
    got = dot_nt(c, dw[kh].reshape(3 * chans, outs))
    return got[:, chans : 2 * chans], got[:, 2 * chans :], got[:, :chans]


def either(flag, a, b):
    return jnp.where(flag, a.astype(F32), b.astype(F32))


def hidden_kernel(width, core, chip, own, part, w, x_out, hid_out, stat_out, scr):
    half = x_out.shape[2]
    odd_rank = (lax.axis_index("rows") & 1) == 1
    for p, row in ((0, either(odd_rank, core[1], chip[1])), (3, either(odd_rank, chip[0], core[0]))):
        even, odd = split(scr, row)
        x_out[p, 0] = even.astype(BF16)
        x_out[p, 1] = odd.astype(BF16)
    for p in range(2):
        x_out[p + 1] = own[p]
    total = 0.0
    for p in range(2):
        he, ho = conv_sum([(x_out[3 * p, 0], x_out[3 * p, 1], 2 * p)], w)
        he, ho = part[p, 0] + he, part[p, 1] + ho
        hid_out[p, 0] = he
        hid_out[p, 1] = ho
        total = total + jnp.sum(he + ho, axis=0, keepdims=True)
    mean = grouped(total, width) / float(4 * half * width)
    spread = 0.0
    for p in range(2):
        for c in range(2):
            d = hid_out[p, c] - mean
            spread = spread + jnp.sum(d * d, axis=0, keepdims=True)
    stat_out[...] = jnp.zeros(stat_out.shape, F32)
    stat_out[0:1] = mean
    stat_out[1:2] = grouped(spread, width)


def edge_kernel(core, chip, x, w, bias, cot_core, cot_chip, dw, own_gm, cbias, hid_out, gm_out, low_out, cb_out, scr):
    half = x.shape[2]
    odd_rank = (lax.axis_index("rows") & 1) == 1
    top = [v.astype(BF16) for v in split(scr, either(odd_rank, core[0], chip[0]))]
    low = [v.astype(BF16) for v in split(scr, either(odd_rank, chip[1], core[1]))]
    low_out[0] = low[0]
    low_out[1] = low[1]
    both = jnp.sum(cot_core[...].astype(F32), axis=0, keepdims=True) + cbias[0:1]
    cb_out[...] = jnp.broadcast_to(both, cb_out.shape)
    weights = conv_weights(w)
    even = stack(lanes(top[0], x[0, 0], x[1, 0]), lanes(x[2, 0], x[3, 0], low[0]))
    odd = stack(lanes(top[1], x[0, 1], x[1, 1]), lanes(x[2, 1], x[3, 1], low[1]))
    base_e, base_o, from_odd, from_even = conv_rows(even, odd, weights, bias[...])
    for p in range(2):
        sl = slice(p * half, (p + 1) * half)
        hid_out[p, 0] = base_e[sl] + later(from_odd[sl])
        hid_out[p, 1] = base_o[sl] + sooner(from_even[sl])
    above = either(odd_rank, cot_core[...], cot_chip[...]).astype(BF16)
    below = either(odd_rank, cot_chip[...], cot_core[...]).astype(BF16)
    zero = jnp.zeros((half, x.shape[3]), F32)
    for p, c, kh in ((0, above, 2), (1, None, 0), (2, below, 0), (3, below, 1)):
        even, odd, late = back_taps(c, dw, kh) if c is not None else (zero, zero, zero)
        own = own_gm[p] if p < 3 else (zero, zero)
        gm_out[p, 0] = own[0] + even
        gm_out[p, 1] = own[1] + (odd + sooner(late) if c is not None else odd)


def norm_kernel(width, count, ranks, *refs):
    stats = refs[:ranks]
    x, hid, gm, gain, shift, par_out, mix_out, gp_out, sum_out, far_out = refs[ranks:]
    half = x.shape[2]
    local = float(4 * half * width)
    mean = sum(s[0:1] for s in stats) / float(len(stats))
    spread = 0.0
    for s in stats:
        d = s[0:1] - mean
        spread = spread + (s[1:2] + local * (d * d))
    rstd = lax.rsqrt(spread / count + EPS)
    par_out[...] = jnp.zeros(par_out.shape, F32)
    par_out[0:1] = mean
    par_out[1:2] = rstd
    first = 0.0
    second = 0.0
    for p in range(2):
        mixed = []
        for c in range(2):
            normed = (hid[p, c] - mean) * rstd
            pre = normed * gain[...] + shift[...]
            sig = jax.nn.sigmoid(pre)
            mixed.append(x[p + 1, c].astype(F32) + pre * sig)
            gp = gm[p + 1, c] * (sig * (1.0 + pre * (1.0 - sig)))
            gp_out[p, c] = gp
            first = first + jnp.sum(gp * normed, axis=0, keepdims=True)
            second = second + jnp.sum(gp, axis=0, keepdims=True)
        mix_out[p] = lanes(later(mixed[1]).astype(BF16), mixed[0].astype(BF16), mixed[1].astype(BF16))
    sum_out[...] = jnp.zeros(sum_out.shape, F32)
    sum_out[0:1] = first
    sum_out[1:2] = second
    core = lax.axis_index("rows") & 1
    far_out[0] = gp_out[core]
    for c in range(2):
        far_out[1, c] = hid[core, c] - mean


def down_kernel(packed, par, x, hid, gain, shift, mix, cot, cot_core, top_out, *rest):
    mean, rstd = par[0:1], par[1:2]
    chans = x.shape[3]
    inside = jnp.where(lax.axis_index("rows") > 0, 1.0, 0.0)
    mixed = []
    for c in range(2):
        pre = (hid[0, c] - mean) * rstd * gain[...] + shift[...]
        mixed.append((x[0, c].astype(F32) + pre * jax.nn.sigmoid(pre)) * inside)
    top = lanes(later(mixed[1]).astype(BF16), mixed[0].astype(BF16), mixed[1].astype(BF16))
    top_out[...] = top
    grad = dot_tn(cot[...], lanes(top, mix[0], mix[1]))
    if not packed:
        rest[0][...] = grad
        return
    last_out, keep_out, send_out = rest
    outs_chunk = keep_out.shape[3]
    taps = [grad[:, t * chans : (t + 1) * chans] for t in range(9)]
    last_out[...] = taps[8] + dot_tn(cot_core[...], top[:, 2 * chans :])
    for t in range(2):
        quarters = [taps[2 * q + t].reshape(-1, outs_chunk, chans) for q in range(4)]
        halve(lax.axis_index("rows") & 1, quarters, keep_out, [send_out], (t,))


def halve(core, quarters, keep_out, send_outs, at=()):
    first = core == 0
    for i in range(2):
        one, two = quarters[2 * i], quarters[2 * i + 1]
        keep_out[(i, *at)] = jnp.where(first, one, two)
        other = jnp.where(first, two, one).astype(BF16)
        size = other.shape[0] // len(send_outs)
        for j, ref in enumerate(send_outs):
            ref[(i, *at)] = other[j * size : (j + 1) * size]


def hi_lo(full):
    hi = full.astype(BF16).astype(F32)
    return jnp.concatenate([hi, full - hi], axis=-2)


def gradient(coef, gp, centred):
    return coef[0] * gp + coef[1] * centred + coef[2]


def coefficients(width, count, sums, par, gain, par_out):
    rstd = par[1:2]
    m2 = grouped(sums[0:1] * gain, width) / count
    m1 = grouped(sums[1:2] * gain, width) / count
    coef = (rstd * gain, -(rstd * rstd) * m2, -rstd * m1)
    par_out[...] = jnp.zeros(par_out.shape, F32)
    par_out[0:1] = par[0:1]
    for i in range(3):
        par_out[1 + i : 2 + i] = coef[i]
    return coef


def shifted(even, odd):
    even_b, odd_b = even.astype(BF16), odd.astype(BF16)
    return lanes(odd_b, even_b, later(odd).astype(BF16)), lanes(sooner(even).astype(BF16), odd_b, even_b)


def back_kernel(width, count, ranks, *refs):
    sum_refs = refs[:ranks]
    par, x, hid, gp, gain, par_out, g_out, grad_out, small_out = refs[ranks:]
    chans = x.shape[3]
    coef = coefficients(width, count, sum(s[...] for s in sum_refs), par, gain[...], par_out)
    bias = 0.0
    left, right = [], []
    for p in range(2):
        even, odd = [gradient(coef, gp[p, c], hid[p, c] - par[0:1]) for c in range(2)]
        bias = bias + jnp.sum(even + odd, axis=0, keepdims=True)
        g_out[p, 0] = even.astype(BF16)
        g_out[p, 1] = odd.astype(BF16)
        left += shifted(even, odd)
        right += [lanes(x[p, c], x[p + 1, c], x[p + 2, c]) for c in range(2)]
    grad_out[...] = dot_tn(stack(*left), stack(*right))
    small_out[...] = stack(bias, sum_refs[0][0:2], jnp.zeros((5, chans), F32))


def chip_kernel(width, count, s0, s1, s2, s3, par, x, low, hid, gp, far, edge, gain, dlast, cbias, early, *refs):
    par_out, g_out, own, sx, sy, sxy, scr = refs
    rank = lax.axis_index("rows")
    core, chip, side = rank & 1, rank >> 1, lax.axis_index("dp") & 1
    first = core == 0
    chans = x.shape[3]
    owners = scr.shape[1]
    chunk = chans // owners
    coef = coefficients(width, count, s0[...] + s1[...] + s2[...] + s3[...], par, gain[...], par_out)
    halo = 1 - core
    rows = [[gradient(coef, gp[p, c], hid[p, c] - par[0:1]) for c in range(2)] for p in range(2)]
    rows.append([gradient(coef, edge[halo, 0, c], edge[halo, 1, c]) for c in range(2)])
    rows.append([gradient(coef, far[0, c], far[1, c]) for c in range(2)])
    for p in range(2):
        for c in range(2):
            g_out[p, c] = rows[p][c].astype(BF16)
    beside = (2 * core, 1 + 2 * core, 2 - core, 3 - 3 * core)
    level = (x.at[1], x.at[2], x.at[3], low)
    bias = 0.0
    left, right = [], []
    for (even, odd), at, same in zip(rows, beside, level):
        bias = bias + jnp.sum(even + odd, axis=0, keepdims=True)
        left += shifted(even, odd)
        right += [lanes(x[at, c], same[c]) for c in range(2)]
    grad = dot_tn(stack(*left), stack(*right))
    full = stack(bias, s0[0:2] + s1[0:2], jnp.zeros((5, chans), F32))
    wide = [cbias[0:1, i * chans : (i + 1) * chans] for i in range(cbias.shape[1] // chans)]
    row_id = lax.broadcasted_iota(jnp.int32, full.shape, 0)
    for kw in range(3):
        at = slice(kw * chunk, (kw + 1) * chunk)
        piece = grad[kw * chans : (kw + 1) * chans]
        scr[0, :, at, :] = piece[:, :chans].reshape(owners, chunk, chans)
        one = piece[:, chans:].reshape(owners, chunk, chans)
        if kw < 2:
            two = dlast[...].reshape(owners, 2 * chunk, chans)[:, at]
            scr[1, :, at, :] = jnp.where(first, one, two)
            continue
        for d in range(owners):
            start = d * chunk
            mine = full if start == 0 else pltpu.roll(full, chans - start, 1)
            start = d * 2 * chunk
            row = jnp.broadcast_to(wide[start // chans], full.shape)
            if start % chans:
                row = pltpu.roll(row, chans - start % chans, 1)
            scr[1, d, at, :] = jnp.where(first, one[d], hi_lo(jnp.where(row_id == 3, row, mine)))
    mine, other = rank == 3, 2 * (1 - chip) + core == 3
    n = early.shape[2]
    for z in range(own.shape[0]):
        here, there = 2 * z + side, 2 * z + 1 - side
        own[z] = scr[chip, here]
        sx[z] = rounded(scr[1 - chip, here], other)
        sy[z] = rounded(scr[chip, there], mine)
        sxy[z, 2 * n :] = rounded(scr[1 - chip, there], other)
        for t in range(2):
            sxy[z, t * n : (t + 1) * n] = early[t, z]


def block_kernel(ahead, mix_top, mix, dw, dbias, block_out, done_out):
    chans, outs = dw.shape[2:]
    flat = [dw[:, k].reshape(3 * chans, outs) for k in range(3)]
    odd_before = lanes(mix_top[:, :chans], mix[0, :, :chans], mix[1, :, :chans])
    even = lanes(mix_top[:, chans : 2 * chans], mix[0, :, chans : 2 * chans], mix[1, :, chans : 2 * chans])
    odd = lanes(mix_top[:, 2 * chans :], mix[0, :, 2 * chans :], mix[1, :, 2 * chans :])
    block = dot(lanes(odd_before, even, odd), stack(*flat)) + dbias[...]
    block_out[...] = block.astype(BF16)
    done_out[...] = jnp.zeros(done_out.shape, F32)


def halo_kernel(ahead, par, hid, gm, gain, shift, out):
    for i, p in ((0, 0), (1, 3)):
        for c in range(2):
            centred = hid[i, c] - par[0:1]
            pre = centred * par[1:2] * gain[...] + shift[...]
            sig = jax.nn.sigmoid(pre)
            out[i, 0, c] = gm[p, c] * (sig * (1.0 + pre * (1.0 - sig)))
            out[i, 1, c] = centred


def image_kernel(last, parts, gm, par2, g, w, gi_out, done_out, scr):
    half = g.shape[2]
    chans = g.shape[3]
    me = lax.axis_index("rows")
    coef = [par2[1 + i : 2 + i] for i in range(3)]
    edge = []
    for i, there in ((0, me > 0), (1, me < last)):
        keep = jnp.where(there, 1.0, 0.0)
        edge.append([(gradient(coef, parts[i, 0, c], parts[i, 1, c]) * keep).astype(BF16) for c in range(2)])
    rows = [edge[0], [g[0, 0], g[0, 1]], [g[1, 0], g[1, 1]], edge[1]]
    tap = [lanes(w[0, k], w[1, k], w[2, k]) for k in range(3)]
    both = stack(lanes(tap[1], tap[0]), lanes(tap[2], tap[1]))
    ge = stack(*[lanes(rows[p + 2][0], rows[p + 1][0], rows[p][0]) for p in range(2)])
    go = stack(*[lanes(rows[p + 2][1], rows[p + 1][1], rows[p][1]) for p in range(2)])
    base = dot_nt(lanes(ge, go), both)
    from_odd = dot_nt(go, tap[2])
    from_even = dot_nt(ge, tap[0])
    for p in range(2):
        sl = slice(p * half, (p + 1) * half)
        scr[pl.ds(0, half, stride=2), :] = base[sl, :chans] + later(from_odd[sl]) + gm[p + 1, 0]
        scr[pl.ds(1, half, stride=2), :] = base[sl, chans:] + sooner(from_even[sl]) + gm[p + 1, 1]
        gi_out[p] = scr[...].astype(BF16)
    done_out[...] = jnp.zeros(done_out.shape, F32)


def rounded(total, on):
    n = total.shape[0] - 16
    last = total[n:]
    whole = last[0:8] + last[8:16]
    last = jnp.where(on, hi_lo(whole), last)
    return stack(total[:n], last).astype(BF16)


def early_kernel(keep, got, own, sx, sy, sxy, done_out):
    done_out[...] = jnp.zeros(done_out.shape, F32)
    chip, side = lax.axis_index("rows") >> 1, lax.axis_index("dp") & 1
    _, zs, n, _ = own.shape
    for t in range(2):
        for z in range(zs):

            def total(x, y):
                return keep[x, t, 2 * z + y] + got[x, t, 2 * z + y].astype(F32)

            own[t, z] = total(chip, side)
            sxy[t, z] = total(1 - chip, 1 - side).astype(BF16)
            sx[t, z] = total(1 - chip, side).astype(BF16)
            sy[t, z] = total(chip, 1 - side).astype(BF16)


def join_kernel(early, ex, ey, out):
    out[...] = early[...] + ex[...].astype(F32) + ey[...].astype(F32)


def pack_kernel(own, gx, gy, gxy, early, after, after_too, out, s1, s2, s3, scr):
    z = lax.axis_index("dp") >> 1
    n = early.shape[2]
    for t in range(2):
        scr[:, t * n : (t + 1) * n, :] = early[t] + gxy[:, t * n : (t + 1) * n, :].astype(F32)
    late = gx[...].astype(F32) + gy[...].astype(F32) + gxy[:, 2 * n :, :].astype(F32)
    scr[:, 2 * n :, :] = own[...] + late
    out[...] = scr[z]
    for k, ref in ((1, s1), (2, s2), (3, s3)):
        ref[...] = rounded(scr[(z + k) & 3], lax.axis_index("rows") == 3)


def sum_kernel(own, g1, g2, g3, out, send):
    total = own[...] + g1[...].astype(F32) + g2[...].astype(F32) + g3[...].astype(F32)
    out[...] = total
    send[...] = rounded(total, lax.axis_index("rows") == 3)


def last_kernel(chunk, q0, q1, q2, q3, down, conv, cb, ga, sh, db, scr):
    me = lax.axis_index("rows")
    for k, ref in enumerate((q0, q1, q2, q3)):
        scr[me ^ k] = ref[...].astype(F32)
    wide = 2 * chunk
    for q in range(4):
        for t in range(2):
            down[2 * q + t] = scr[q, t * wide : (t + 1) * wide, :]
    for kh in range(3):
        for kw in range(3):
            at = 2 * wide + kw * chunk
            conv[3 * kh + kw] = scr[(0, 2, 1)[kh], at : at + chunk, :]
    down[8] = scr[3, 2 * wide : 3 * wide, :]
    rows = scr[3, 3 * wide : 3 * wide + 8, :] + scr[3, 3 * wide + 8 :, :]
    cb[...] = rows[0:1, :chunk]
    ga[...] = rows[1:2, :chunk]
    sh[...] = rows[2:3, :chunk]
    db[...] = rows[3:4, :wide]


def across(x):
    n = lax.axis_size("rows")
    return lax.ppermute(x, "rows", [p for i in range(1, n - 1, 2) for p in ((i, i + 1), (i + 1, i))])


def swap(x, axis, k):
    return lax.ppermute(x, axis, [(i, i ^ k) for i in range(lax.axis_size(axis))])


def around(x, k):
    n = lax.axis_size("dp")
    return lax.ppermute(x, "dp", [(i, (i + 2 * k) % n) for i in range(n)])


def swap_both(x, k_rows, k_dp):
    both = ("rows", "dp")
    k = k_rows * lax.axis_size("dp") + k_dp
    return lax.ppermute(x, both, [(i, i ^ k) for i in range(lax.axis_size(both))])


def swap_beside(x, y, xy):
    both = swap_both(xy, 2, 1)
    return swap(x, "rows", 2), swap(y, "dp", 1), both


def shards(images, conv_weight, conv_bias, norm_gain, norm_shift, down_weight, down_bias, cotangent):
    img, cot = images[0], cotangent[0, 0]
    rows, cols, chans = img.shape
    half, outs = cot.shape
    ranks, owners = lax.axis_size("rows"), lax.axis_size("dp")
    width = chans // GROUPS
    count = float(rows * cols * width * ranks)
    chunk, wide = chans // owners, outs // owners
    packed = ranks == 4 and owners == 8 and chunk == 16 and wide == 32
    vmem = pl.BlockSpec(memory_space=pltpu.VMEM)
    hbm = pl.BlockSpec(memory_space=pltpu.HBM)

    def run(kernel, args, outs, scratch=(), specs=None, cost=1 << 27):
        return pl.pallas_call(
            kernel,
            in_specs=specs or [vmem] * len(args),
            out_shape=[jax.ShapeDtypeStruct(s, d) for s, d in outs],
            out_specs=[vmem] * len(outs),
            scratch_shapes=list(scratch),
            compiler_params=pltpu.CompilerParams(vmem_limit_bytes=24 * MIB),
            cost_estimate=pl.CostEstimate(flops=cost, bytes_accessed=1 << 10, transcendentals=0),
        )(*args)

    def with_swaps(mine, other):
        return [mine] + [swap(other, "rows", k) for k in range(1, ranks)]

    chip_img, core_img = across(img), swap(img, "rows", 1)
    row_scr = pltpu.VMEM((cols, chans), F32)
    block_of = (2, 2, half, chans)
    tile = ((8, chans), F32)
    (ahead,) = run(first_kernel, (), [tile], cost=1 << 34)
    raw = (
        img,
        conv_weight,
        down_weight,
        cot,
        conv_bias.reshape(1, chans),
        norm_gain.reshape(1, chans),
        norm_shift.reshape(1, chans),
        down_bias.reshape(1, outs),
    )
    w, dw, cot, bias, gain, shift, dbias, own_x, part, own_gm, cbias = run(
        prep_kernel,
        (ahead, *raw),
        [(v.shape, v.dtype) for v in raw[1:]] + [(block_of, BF16), (block_of, F32), ((3, 2, half, chans), F32), ((8, outs), F32)],
        [pltpu.VMEM(img.shape, BF16), row_scr, pltpu.SemaphoreType.DMA((len(raw),))],
        [vmem] + [hbm] * len(raw),
    )
    chip_cot, core_cot = across(cot), swap(cot, "rows", 1)
    x, hid, stat = run(
        functools.partial(hidden_kernel, width),
        (core_img, chip_img, own_x, part, w),
        [((4, 2, half, chans), BF16), (block_of, F32), tile],
        [row_scr],
    )
    stats = with_swaps(stat, stat)
    hid_edge, gm, low, chip_cbias = run(
        edge_kernel,
        (core_img, chip_img, x, w, bias, core_cot, chip_cot, dw, own_gm, cbias),
        [(block_of, F32), ((4, 2, half, chans), F32), (block_of[1:], BF16), ((8, outs), F32)],
        [row_scr],
    )
    par, mix, gp, sums, far = run(
        functools.partial(norm_kernel, width, count, ranks),
        (*stats, x, hid, gm, gain, shift),
        [tile, ((2, half, 3 * chans), BF16), (block_of, F32), tile, (block_of, F32)],
    )
    all_sums = with_swaps(sums, sums)
    early_shape = (2, owners, wide, chans)
    late_shape = (owners, 3 * chunk, chans)
    deep = 2 * wide + 3 * chunk

    mix_top, *down_grad = run(
        functools.partial(down_kernel, packed),
        (par, x, hid_edge, gain, shift, mix, cot, core_cot),
        [((half, 3 * chans), BF16)]
        + (
            [((outs, chans), F32), ((2,) + early_shape, F32), ((2,) + early_shape, BF16)]
            if packed
            else [((outs, 9 * chans), F32)]
        ),
    )
    if packed:
        dlast, keep, send = down_grad
        zs = owners // 2
        late_cut, early_cut = (zs, 3 * chunk, chans), (2, zs, wide, chans)
        early_own, sx, sy, early_sxy, ahead = run(
            early_kernel,
            (keep, swap(send, "rows", 1)),
            [(early_cut, F32)] + [(early_cut, BF16)] * 3 + [tile],
        )
        (early,) = run(
            join_kernel, (early_own, swap(sx, "rows", 2), swap(sy, "dp", 1)), [(early_cut, F32)], cost=JOIN
        )
    (edge,) = run(halo_kernel, (ahead, par, hid_edge, gm, gain, shift), [((2,) + block_of, F32)])
    if packed:
        far = swap(far, "rows", 1)
        par2, g, own, sx, sy, sxy = run(
            functools.partial(chip_kernel, width, count),
            (*all_sums, par, x, low, hid, gp, far, edge, gain, dlast, chip_cbias, early_sxy),
            [tile, (block_of, BF16), (late_cut, F32)] + [(late_cut, BF16)] * 2 + [((zs, deep, chans), BF16)],
            [pltpu.VMEM((2,) + late_shape, F32)],
            cost=BACK,
        )
    else:
        par2, g, *conv_grad = run(
            functools.partial(back_kernel, width, count, ranks),
            (*all_sums, par, x, hid, gp, gain),
            [tile, (block_of, BF16), ((3 * chans, 3 * chans), F32), tile],
        )
    block, block_done = run(block_kernel, (par2, mix_top, mix, dw, dbias), [((half, outs), BF16), tile])
    gi, done = run(
        functools.partial(image_kernel, ranks - 1),
        (edge, gm, par2, g, w),
        [((rows, cols, chans), BF16), tile],
        [row_scr],
    )
    if packed:
        part, *sends = run(
            pack_kernel,
            (own, *swap_beside(sx, sy, sxy), early, done, block_done),
            [((deep, chans), F32)] + [((deep, chans), BF16)] * 3,
            [pltpu.VMEM((zs, deep, chans), F32)],
        )
        part, send = run(
            sum_kernel,
            (part, *[around(sends[k - 1], k) for k in (1, 2, 3)]),
            [((deep, chans), F32), ((deep, chans), BF16)],
        )
        down, conv, cb, ga, sh, db = run(
            functools.partial(last_kernel, chunk),
            with_swaps(part, send),
            [((9, wide, chans), F32), ((9, chunk, chans), F32)] + [((1, chunk), F32)] * 3 + [((1, wide), F32)],
            [pltpu.VMEM((4, deep, chans), F32)],
        )
    else:
        totals = lax.psum((down_grad[0], conv_grad[0], conv_grad[1], cbias[:1]), ("rows", "dp"))
        owner = lax.axis_index("dp")
        down = totals[0].reshape(outs, 9, chans).transpose(1, 0, 2)
        down = lax.dynamic_slice_in_dim(down, owner * wide, wide, 1)
        conv = totals[1].reshape(3, chans, 3, chans).transpose(2, 0, 1, 3).reshape(9, chans, chans)
        conv = lax.dynamic_slice_in_dim(conv, owner * chunk, chunk, 1)
        cb, ga, sh = lax.dynamic_slice_in_dim(totals[2], owner * chunk, chunk, 1)[:3]
        db = lax.dynamic_slice_in_dim(totals[3], owner * wide, wide, 1)
    return (
        block[None, None],
        gi[None],
        conv.reshape(3, 3, chunk, chans).transpose(0, 1, 3, 2),
        cb.reshape(-1),
        ga.reshape(-1),
        sh.reshape(-1),
        down.reshape(3, 3, wide, chans).transpose(0, 1, 3, 2),
        db.reshape(-1),
    )


def solution(mesh):
    spec = P("dp", "rows", None, None)
    in_specs = (spec, P(), P(), P(), P(), P(), P(), spec)
    last = P(None, None, None, "dp")
    out_specs = (spec, spec, last, P("dp"), P("dp"), P("dp"), last, P("dp"))
    return jax.shard_map(shards, mesh=mesh, in_specs=in_specs, out_specs=out_specs, check_vma=False)
```
